32 devices in a mesh: dp: 2 (over y), ctx: 4 (over x, core), tp: 4 (over z).
Axes of the slice: x: 2, y: 2, z: 4, core: 2. Of those that a mesh axis runs over, the one named last changes fastest.
Arguments:
- hidden_in: bfloat16 [4, 1024, 1024], P('dp', 'ctx'), may hold values from -6 to 6
- encoder_states: bfloat16 [4, 4096, 1024], P('dp', 'ctx'), may hold values from -6 to 6
- out_cotangent: bfloat16 [4, 1024, 1024], P('dp', 'ctx'), may hold values from -6 to 6
- self_proj: bfloat16 [3, 1024, 1024], P(None, ('dp', 'ctx'), 'tp'), may hold values from -0.1875 to 0.1875
- self_qv_bias: bfloat16 [16, 128], P('tp', ('dp', 'ctx')), may hold values from -0.3125 to 0.3125
- self_out_proj: bfloat16 [1024, 1024], P('tp', ('dp', 'ctx')), may hold values from -3 to 3
- cross_q_proj: bfloat16 [1024, 1024], P(('dp', 'ctx'), 'tp'), may hold values from -0.1875 to 0.1875
- cross_kv_proj: bfloat16 [2, 1024, 1024], P(None, ('dp', 'ctx'), 'tp'), may hold values from -0.1875 to 0.1875
- cross_qv_bias: bfloat16 [16, 128], P('tp', ('dp', 'ctx')), may hold values from -0.3125 to 0.3125
- cross_out_proj: bfloat16 [1024, 1024], P('tp', ('dp', 'ctx')), may hold values from -6 to 6
- up_proj: bfloat16 [1024, 4096], P(('dp', 'ctx'), 'tp'), may hold values from -0.1875 to 0.1875
- up_bias: bfloat16 [128, 32], P('tp', ('dp', 'ctx')), may hold values from -1.75 to 1.75
- down_proj: bfloat16 [4096, 1024], P('tp', ('dp', 'ctx')), may hold values from -0.09375 to 0.09375
- norm_gain: bfloat16 [3, 1024], P(None, ('dp', 'ctx')), may hold values from 0.5 to 1.5
- norm_bias: bfloat16 [3, 1024], P(None, ('dp', 'ctx')), may hold values from -0.625 to 0.625
- out_bias: bfloat16 [3, 1024], P(None, ('dp', 'ctx')), may hold values from -0.625 to 0.625
Outputs:
- hidden_out: bfloat16 [4, 1024, 1024], P('dp', 'ctx')
- input_grad: float32 [4, 1024, 1024], P('dp', 'ctx')
- encoder_grad: float32 [4, 4096, 1024], P('dp', 'ctx', 'tp')
- self_proj_grad: float32 [3, 1024, 1024], P(None, ('dp', 'ctx'), 'tp')
- self_qv_bias_grad: float32 [16, 128], P('tp', ('dp', 'ctx'))
- self_out_proj_grad: float32 [1024, 1024], P('tp', ('dp', 'ctx'))
- cross_q_proj_grad: float32 [1024, 1024], P(('dp', 'ctx'), 'tp')
- cross_kv_proj_grad: float32 [2, 1024, 1024], P(None, ('dp', 'ctx'), 'tp')
- cross_qv_bias_grad: float32 [16, 128], P('tp', ('dp', 'ctx'))
- cross_out_proj_grad: float32 [1024, 1024], P('tp', ('dp', 'ctx'))
- up_proj_grad: float32 [1024, 4096], P(('dp', 'ctx'), 'tp')
- up_bias_grad: float32 [128, 32], P('tp', ('dp', 'ctx'))
- down_proj_grad: float32 [4096, 1024], P('tp', ('dp', 'ctx'))
- norm_gain_grad: float32 [3, 1024], P(None, ('dp', 'ctx'))
- norm_bias_grad: float32 [3, 1024], P(None, ('dp', 'ctx'))
- out_bias_grad: float32 [3, 1024], P(None, ('dp', 'ctx'))
- stream_rms: float32 [4, 4, 1024], P(None, 'dp', 'ctx')
The draws below stay inside these ranges and needn't reach their ends.
All inputs are finite; a program needn't handle non-finite values.
Results may differ from the reference program's by a relative error of at most 0.04.
Values may be sent and summed in bfloat16 or wider, within the bound.
No kernel may reach another device: no remote copies, remote signals or barrier semaphores. Data moves between devices by JAX's collectives and lax.ppermute only.
A program may use at most 256 MiB of HBM per device.

```python
import math
import jax
import jax.numpy as jnp
from jax import lax

D = 1024
H = 16
HD = 64
FF = 4096
BLOCK = 256
ENC = 4096
SEQS = 4
LEN = 1024


def block_levels(stream_key, extent, cuts, least, top_value):
    loudness = 1.0
    for dim, blocks in cuts:
        heights = jax.random.uniform(jax.random.fold_in(jax.random.fold_in(stream_key, 6), dim), (blocks,), jnp.float32, least / len(cuts), top_value / len(cuts))
        loudness = loudness * jnp.repeat(jnp.exp(heights), extent[dim] // blocks).reshape((-1,) + (1,) * (len(extent) - 1 - dim))
    return loudness


def gaussian(stream_key, extent, spread, bound, shards=(), held_as=jnp.bfloat16):
    level = block_levels(stream_key, extent, shards, -0.22, 0.18) if shards else 1.0
    values = jax.random.normal(stream_key, extent, jnp.float32) * spread * level
    return jnp.minimum(jnp.maximum(values, -bound), bound).astype(held_as)


def setup_inputs(seed: int = 0) -> dict:
    key_of = jax.random.split(jax.random.key(seed), 17)
    return {
        "hidden_in": gaussian(key_of[0], (SEQS, LEN, D), 1.0, 6.0, ((0, 2), (1, 4))),
        "encoder_states": gaussian(key_of[1], (SEQS, ENC, D), 1.0, 6.0, ((0, 2), (1, 4))),
        "out_cotangent": gaussian(key_of[2], (SEQS, LEN, D), 1.0, 6.0, ((0, 2), (1, 4))),
        "self_proj": gaussian(key_of[3], (3, D, D), D ** -0.5, 0.1875, ((1, 8), (2, 4))),
        "self_qv_bias": gaussian(key_of[4], (H, 2 * HD), 0.05, 0.3125, ((0, 4), (1, 8))),
        "self_out_proj": gaussian(key_of[5], (D, D), (max(1, D // 256)) ** -0.5, 3.0, ((0, 4), (1, 8))),
        "cross_q_proj": gaussian(key_of[6], (D, D), D ** -0.5, 0.1875, ((0, 8), (1, 4))),
        "cross_kv_proj": gaussian(key_of[7], (2, D, D), D ** -0.5, 0.1875, ((1, 8), (2, 4))),
        "cross_qv_bias": gaussian(key_of[8], (H, 2 * HD), 0.05, 0.3125, ((0, 4), (1, 8))),
        "cross_out_proj": gaussian(key_of[9], (D, D), (max(1, D // 1024)) ** -0.5, 6.0, ((0, 4), (1, 8))),
        "up_proj": gaussian(key_of[10], (D, FF), D ** -0.5, 0.1875, ((0, 8), (1, 4))),
        "up_bias": gaussian(key_of[11], (FF // 32, 32), 0.3, 1.75, ((0, 4), (1, 8))),
        "down_proj": gaussian(key_of[12], (FF, D), FF ** -0.5, 0.09375, ((0, 4), (1, 8))),
        "norm_gain": jnp.clip(1.0 + 0.1 * jax.random.normal(key_of[13], (3, D), jnp.float32), 0.5, 1.5).astype(jnp.bfloat16),
        "norm_bias": gaussian(key_of[14], (3, D), 0.1, 0.625, ((1, 8),)),
        "out_bias": gaussian(key_of[15], (3, D), 0.1, 0.625, ((1, 8),)),
    }


EPSILON = 1e-05
NEGATIVE = -1e+30
FULL_PRECISION = lax.Precision.HIGHEST

@jax.custom_vjp
def reduced_copy(v):
    return lax.optimization_barrier(v.astype(jnp.bfloat16)).astype(jnp.float32)

@jax.custom_vjp
def low_back(v):
    return v

def low_keep(v):
    return (reduced_copy(v), None)

def low_pass(kept, grad):
    return (grad,)

def back_keep(v):
    return (v, None)

def back_low(kept, grad):
    return (reduced_copy(grad),)
reduced_copy.defvjp(low_keep, low_pass)
low_back.defvjp(back_keep, back_low)

def matmul(left, right):
    return jnp.dot(left, right, precision=FULL_PRECISION)

def rounded(values):
    return reduced_copy(low_back(values))

def layer_norm(values, norm_gain, norm_shift):
    row_mean = lax.optimization_barrier(jnp.mean(values, -1, keepdims=True))
    centered = values - row_mean
    variance = lax.optimization_barrier(jnp.mean(centered * centered, -1, keepdims=True))
    return centered * lax.rsqrt(variance + EPSILON) * norm_gain + norm_shift

def root_mean(values):
    return jnp.sqrt(lax.optimization_barrier(jnp.mean(values * values, -1)))

def split_heads(values):
    return values.reshape(values.shape[0], H, HD)

def attend(query_rows, key_matrix, value_matrix, allowed):
    score_scale = 1.0 / math.sqrt(HD)
    logit_scores = jnp.einsum('eqf,jqf->qej', query_rows, key_matrix, precision=FULL_PRECISION) * score_scale
    logit_scores = jnp.where(allowed[None], low_back(logit_scores), NEGATIVE)
    row_max = lax.optimization_barrier(jnp.max(logit_scores, -1, keepdims=True))
    exp_scores = jnp.exp(logit_scores - row_max)
    attention_weights = exp_scores / lax.optimization_barrier(jnp.sum(exp_scores, -1, keepdims=True))
    return jnp.einsum('jgr,rjq->gjq', reduced_copy(attention_weights), value_matrix, precision=FULL_PRECISION)
attend_saved = jax.checkpoint(attend)

def layer(tokens, encoder, self_proj, self_qv_bias, self_out_proj, cross_q_proj, cross_kv_proj, cross_qv_bias, cross_out_proj, up_proj, up_bias, down_proj, norm_gain, norm_bias, out_bias):
    length = tokens.shape[0]
    positions = jnp.arange(length) // BLOCK
    causal = positions[None, :] <= positions[:, None]
    query_rows = rounded(matmul(tokens, self_proj[0]) + self_qv_bias[:, :HD].reshape(D))
    key_matrix = rounded(matmul(tokens, self_proj[1]))
    value_matrix = rounded(matmul(tokens, self_proj[2]) + self_qv_bias[:, HD:].reshape(D))
    mixed = attend_saved(split_heads(query_rows), split_heads(key_matrix), split_heads(value_matrix), causal)
    mixed = rounded(mixed.reshape(length, D))
    attn_branch = low_back(matmul(mixed, self_out_proj)) + out_bias[0]
    first = reduced_copy(layer_norm(tokens + attn_branch, norm_gain[0], norm_bias[0]))
    cross_queries = rounded(matmul(first, cross_q_proj) + cross_qv_bias[:, :HD].reshape(D))
    enc_keys = rounded(matmul(encoder, cross_kv_proj[0]))
    enc_values = rounded(matmul(encoder, cross_kv_proj[1]) + cross_qv_bias[:, HD:].reshape(D))
    everywhere = jnp.arange(encoder.shape[0])[None, :] >= 0
    cross_mixed = attend_saved(split_heads(cross_queries), split_heads(enc_keys), split_heads(enc_values), everywhere)
    cross_mixed = rounded(cross_mixed.reshape(length, D))
    cross_branch = low_back(matmul(cross_mixed, cross_out_proj)) + out_bias[1]
    second = reduced_copy(layer_norm(first + cross_branch, norm_gain[1], norm_bias[1]))
    pre_act = low_back(matmul(second, up_proj) + up_bias.reshape(FF))
    active = reduced_copy(jax.nn.gelu(pre_act, approximate=False))
    mlp_branch = low_back(matmul(active, down_proj)) + out_bias[2]
    result = layer_norm(second + mlp_branch, norm_gain[2], norm_bias[2])
    stream_stats = jnp.stack([root_mean(tokens), root_mean(attn_branch), root_mean(cross_branch), root_mean(mlp_branch)])
    return (result, stream_stats)

def reference(hidden_in, encoder_states, out_cotangent, self_proj, self_qv_bias, self_out_proj, cross_q_proj, cross_kv_proj, cross_qv_bias, cross_out_proj, up_proj, up_bias, down_proj, norm_gain, norm_bias, out_bias):
    weights = (self_proj.astype(jnp.float32), self_qv_bias.astype(jnp.float32), self_out_proj.astype(jnp.float32), cross_q_proj.astype(jnp.float32), cross_kv_proj.astype(jnp.float32), cross_qv_bias.astype(jnp.float32), cross_out_proj.astype(jnp.float32), up_proj.astype(jnp.float32), up_bias.astype(jnp.float32), down_proj.astype(jnp.float32), norm_gain.astype(jnp.float32), norm_bias.astype(jnp.float32), out_bias.astype(jnp.float32))

    def one_sequence(running, inputs):
        tokens, encoder, cotangent = inputs
        result, pullback, stream_stats = jax.vjp(layer, tokens.astype(jnp.float32), encoder.astype(jnp.float32), *weights, has_aux=True)
        gradients = pullback(cotangent.astype(jnp.float32))
        running = tuple((previous + gradient for previous, gradient in zip(running, gradients[2:])))
        return (running, (result.astype(jnp.bfloat16), gradients[0], gradients[1], stream_stats))
    zero_grads = tuple((jnp.zeros(weight.shape, jnp.float32) for weight in weights))
    running, outputs = lax.scan(one_sequence, zero_grads, (hidden_in, encoder_states, out_cotangent))
    hidden_out, input_grad, encoder_grad, stream_stats = outputs
    self_proj_grad, self_qv_bias_grad, self_out_proj_grad, cross_q_proj_grad, cross_kv_proj_grad, cross_qv_bias_grad, cross_out_proj_grad, up_proj_grad, up_bias_grad, down_proj_grad, norm_gain_grad, norm_bias_grad, out_bias_grad = running
    stream_rms = jnp.transpose(stream_stats, (1, 0, 2))
    return (hidden_out, input_grad, encoder_grad, self_proj_grad, self_qv_bias_grad, self_out_proj_grad, cross_q_proj_grad, cross_kv_proj_grad, cross_qv_bias_grad, cross_out_proj_grad, up_proj_grad, up_bias_grad, down_proj_grad, norm_gain_grad, norm_bias_grad, out_bias_grad, stream_rms)
```

```python
import functools

import jax
import jax.numpy as jnp
from jax import lax
from jax.experimental import pallas as pl
from jax.experimental.pallas import tpu as pltpu
from jax.sharding import PartitionSpec as P

EPSILON = 1e-05
HEAD = 64
KEY_TILE = 512
VMEM_BYTES = 50 * 1024 * 1024
PLANE = ("dp", "ctx")
HEADS = ("tp", "ctx")
F32 = jnp.float32
BF16 = jnp.bfloat16


def contract(left, right, left_dim, right_dim):
    return lax.dot_general(
        left, right, (((left_dim,), (right_dim,)), ((), ())), preferred_element_type=F32
    )


def norm_forward(values, norm_gain, norm_shift):
    row_mean = jnp.mean(values, -1, keepdims=True)
    centered = values - row_mean
    inv_std = lax.rsqrt(jnp.mean(centered * centered, -1, keepdims=True) + EPSILON)
    normed = centered * inv_std
    return (normed * norm_gain + norm_shift, normed, inv_std)


def norm_backward(gradient, normed, inv_std, norm_gain):
    gain_grad = jnp.sum(gradient * normed, 0)
    shift_grad = jnp.sum(gradient, 0)
    scaled = gradient * norm_gain
    input_part = inv_std * (
        scaled
        - jnp.mean(scaled, -1, keepdims=True)
        - normed * jnp.mean(scaled * normed, -1, keepdims=True)
    )
    return (input_part, gain_grad, shift_grad)


def root_mean(values):
    return jnp.sqrt(jnp.mean(values * values, -1))


def exact_gelu(values):
    return jax.nn.gelu(values, approximate=False)


def with_zeros_below(values):
    return jnp.concatenate([values, jnp.zeros_like(values)], 0)


def with_zeros_above(values):
    return jnp.concatenate([jnp.zeros_like(values), values], 0)


def gather_chunks(ref):
    halves, blocks = ref.shape[:2]
    return jnp.concatenate([ref[h, b] for h in range(halves) for b in range(blocks)], 1)


def self_forward_kernel(x_ref, w_ref, bq_ref, bv_ref, q_ref, kv_ref, o_ref, lse_ref):
    tokens = x_ref[0]
    weights = w_ref[...]
    halves, blocks, _, part = o_ref.shape
    block = halves * part
    scale = HEAD**-0.5
    query = (contract(weights[:HEAD], tokens, 1, 1) + bq_ref[...]).astype(BF16) * scale
    pair = (contract(tokens, weights[HEAD:], 1, 1) + bv_ref[...]).astype(BF16)
    q_ref[0] = query
    kv_ref[0] = pair
    for i in range(blocks):
        keys = pair[: (i + 1) * block]
        scores = contract(keys, with_zeros_below(query[:, i * block : (i + 1) * block]), 1, 0)
        top = jnp.max(scores, 0, keepdims=True)
        weight = jnp.exp(scores - top)
        total = jnp.sum(weight, 0, keepdims=True)
        mixed = contract(keys, weight.astype(BF16), 0, 0)[HEAD:]
        out = (mixed / total).astype(BF16)
        for h in range(halves):
            o_ref[h, i] = out[:, h * part : (h + 1) * part]
        lse_ref[0, :, i * block : (i + 1) * block] = top + jnp.log(total)


def cross_forward_kernel(q_ref, *refs):
    kv_refs, (o_ref, lse_ref) = refs[:-2], refs[-2:]
    halves, blocks, _, part = q_ref.shape
    query = with_zeros_below(gather_chunks(q_ref))
    top = total = mixed = None
    for kv_ref in kv_refs:
        for start in range(0, kv_ref.shape[1], KEY_TILE):
            pair = kv_ref[0, start : start + KEY_TILE]
            scores = contract(pair, query, 1, 0)
            tile_top = jnp.max(scores, 0, keepdims=True)
            new_top = tile_top if top is None else jnp.maximum(top, tile_top)
            weight = jnp.exp(scores - new_top)
            tile_total = jnp.sum(weight, 0, keepdims=True)
            tile_mixed = contract(pair, weight.astype(BF16), 0, 0)
            if top is None:
                total, mixed = tile_total, tile_mixed
            else:
                fade = jnp.exp(top - new_top)
                total = total * fade + tile_total
                mixed = mixed * fade + tile_mixed
            top = new_top
    out = (mixed[HEAD:] / total).astype(BF16)
    for h in range(halves):
        for b in range(blocks):
            at = (h * blocks + b) * part
            o_ref[h, b] = out[:, at : at + part]
    lse_ref[0] = top + jnp.log(total)


def cross_backward_kernel(q_ref, o_ref, do_ref, lse_ref, *refs):
    count = (len(refs) - 1) // 2
    kv_refs, dkv_refs, dq_ref = refs[:count], refs[count:-1], refs[-1]
    halves, blocks, _, part = q_ref.shape
    width = halves * blocks * part
    query = with_zeros_below(gather_chunks(q_ref))
    grad = gather_chunks(do_ref)
    inner = jnp.sum(
        grad.astype(F32) * gather_chunks(o_ref).astype(F32), 0, keepdims=True
    )
    grad = with_zeros_above(grad)
    both = jnp.concatenate([query, grad], 1)
    lse = lse_ref[0]
    query_grad = None
    for kv_ref, dkv_ref in zip(kv_refs, dkv_refs):
        for start in range(0, kv_ref.shape[1], KEY_TILE):
            pair = kv_ref[0, start : start + KEY_TILE]
            products = contract(pair, both, 1, 0)
            weight = jnp.exp(products[:, :width] - lse)
            slope = (weight * (products[:, width:] - inner)).astype(BF16)
            dkv_ref[0, start : start + KEY_TILE] = (
                contract(slope, query, 1, 1) + contract(weight.astype(BF16), grad, 1, 1)
            ).astype(BF16)
            part_grad = contract(pair, slope, 0, 0)
            query_grad = part_grad if query_grad is None else query_grad + part_grad
    out = (query_grad[:HEAD] * HEAD**-0.5).astype(BF16)
    for h in range(halves):
        for b in range(blocks):
            at = (h * blocks + b) * part
            dq_ref[h, b] = out[:, at : at + part]


def self_backward_kernel(
    x_ref, q_ref, kv_ref, o_ref, do_ref, lse_ref, grad_ref, dw_ref, db_ref, dkv_ref
):
    halves, blocks, _, part = o_ref.shape
    block = halves * part
    dkv_ref[...] = jnp.zeros_like(dkv_ref)
    parts = []
    for i in range(blocks):
        lanes = slice(i * block, (i + 1) * block)
        reach = (i + 1) * block
        keys = kv_ref[0, :reach]
        query = with_zeros_below(q_ref[0, :, lanes])
        grad = jnp.concatenate([do_ref[h, i] for h in range(halves)], 1)
        mixed = jnp.concatenate([o_ref[h, i] for h in range(halves)], 1)
        inner = jnp.sum(grad.astype(F32) * mixed.astype(F32), 0, keepdims=True)
        grad = with_zeros_above(grad)
        weight = jnp.exp(contract(keys, query, 1, 0) - lse_ref[0, :, lanes])
        slope = (weight * (contract(keys, grad, 1, 0) - inner)).astype(BF16)
        parts.append(contract(keys, slope, 0, 0)[:HEAD] * HEAD**-0.5)
        dkv_ref[:, :reach] += contract(query, slope, 1, 1) + contract(
            grad, weight.astype(BF16), 1, 1
        )
    grads = jnp.concatenate(
        [jnp.concatenate(parts, 1).astype(BF16), dkv_ref[...].astype(BF16)], 0
    )
    for i in range(blocks):
        for h in range(halves):
            at = i * block + h * part
            grad_ref[h, i] = grads[:, at : at + part]

    @pl.when(pl.program_id(0) == 0)
    def _():
        dw_ref[...] = jnp.zeros_like(dw_ref)
        db_ref[...] = jnp.zeros_like(db_ref)

    dw_ref[...] += contract(grads, x_ref[0], 1, 0)
    db_ref[...] += jnp.sum(grads.astype(F32), 1, keepdims=True)


def by_first(shape, lead=1):
    return pl.BlockSpec((lead,) + shape[1:], lambda s: (s,) + (0,) * (len(shape) - 1))


def whole(shape):
    return pl.BlockSpec(shape, lambda s: (0,) * len(shape))


def shaped(shape, dtype):
    return jax.ShapeDtypeStruct(shape, dtype)


def call(kernel, seqs, in_specs, out_specs, out_shape, operands, cost, scratch=()):
    flops, transcendentals = cost
    moved = sum(o.size * o.dtype.itemsize for o in operands)
    moved += sum(o.size * o.dtype.itemsize for o in out_shape)
    return pl.pallas_call(
        kernel,
        grid=(seqs,),
        in_specs=in_specs,
        out_specs=out_specs,
        out_shape=out_shape,
        scratch_shapes=scratch,
        compiler_params=pltpu.CompilerParams(
            dimension_semantics=("arbitrary",), vmem_limit_bytes=VMEM_BYTES
        ),
        cost_estimate=pl.CostEstimate(
            flops=flops, bytes_accessed=moved, transcendentals=transcendentals
        ),
    )(*operands)


def self_forward(x_all, weights, query_bias, pair_bias, chunk_shape):
    seqs, length, width = x_all.shape
    halves = chunk_shape[0] // seqs
    query, pair, lse = (seqs, HEAD, length), (seqs, length, 2 * HEAD), (seqs, 1, length)
    return call(
        self_forward_kernel,
        seqs,
        [by_first(x_all.shape), whole(weights.shape), whole(query_bias.shape), whole(pair_bias.shape)],
        [by_first(query), by_first(pair), by_first(chunk_shape, halves), by_first(lse)],
        [shaped(query, BF16), shaped(pair, BF16), shaped(chunk_shape, BF16), shaped(lse, F32)],
        [x_all, weights, query_bias, pair_bias],
        (seqs * length * (2 * width * 3 * HEAD + 8 * length * HEAD), seqs * length * length),
    )


def cross_forward(query, pairs):
    seqs = pairs[0].shape[0]
    halves, blocks, _, part = query.shape
    halves //= seqs
    length = halves * blocks * part
    keys = sum(p.shape[1] for p in pairs)
    lse = (seqs, 1, length)
    return call(
        cross_forward_kernel,
        seqs,
        [by_first(query.shape, halves)] + [by_first(p.shape) for p in pairs],
        [by_first(query.shape, halves), by_first(lse)],
        [shaped(query.shape, BF16), shaped(lse, F32)],
        [query, *pairs],
        (seqs * length * keys * 8 * HEAD, seqs * length * keys),
    )


def cross_backward(query, mixed, grad, lse, pairs):
    seqs = pairs[0].shape[0]
    halves, blocks, _, part = query.shape
    halves //= seqs
    length = halves * blocks * part
    keys = sum(p.shape[1] for p in pairs)
    chunk = by_first(query.shape, halves)
    return call(
        cross_backward_kernel,
        seqs,
        [chunk, chunk, chunk, by_first(lse.shape)] + [by_first(p.shape) for p in pairs],
        [by_first(p.shape) for p in pairs] + [chunk],
        [shaped(p.shape, BF16) for p in pairs] + [shaped(query.shape, BF16)],
        [query, mixed, grad, lse, *pairs],
        (seqs * length * keys * 20 * HEAD, seqs * length * keys),
    )


def self_backward(x_all, query, pair, mixed, grad, lse):
    seqs, length, width = x_all.shape
    halves = mixed.shape[0] // seqs
    chunk = by_first(mixed.shape, halves)
    out = mixed.shape[:2] + (3 * HEAD, mixed.shape[3])
    return call(
        self_backward_kernel,
        seqs,
        [by_first(x_all.shape), by_first(query.shape), by_first(pair.shape), chunk, chunk, by_first(lse.shape)],
        [by_first(out, halves), whole((3 * HEAD, width)), whole((3 * HEAD, 1))],
        [shaped(out, BF16), shaped((3 * HEAD, width), F32), shaped((3 * HEAD, 1), F32)],
        [x_all, query, pair, mixed, grad, lse],
        (seqs * length * (2 * width * 3 * HEAD + 20 * length * HEAD), seqs * length * length),
        [pltpu.VMEM((2 * HEAD, length), F32)],
    )


def body(
    hidden_in,
    encoder_states,
    out_cotangent,
    self_proj,
    self_qv_bias,
    self_out_proj,
    cross_q_proj,
    cross_kv_proj,
    cross_qv_bias,
    cross_out_proj,
    up_proj,
    up_bias,
    down_proj,
    norm_gain,
    norm_bias,
    out_bias,
):
    blocks, ranks = lax.axis_size("ctx"), lax.axis_size("tp")
    plane = lax.axis_size("dp") * blocks
    own_ctx, own_tp = lax.axis_index("ctx"), lax.axis_index("tp")
    seqs, block, width = hidden_in.shape
    rows = seqs * block
    part = rows // ranks
    shard = width // plane
    heads_here = self_qv_bias.shape[0]
    local_width = heads_here * HEAD
    all_heads = heads_here * ranks
    enc_len = encoder_states.shape[1]
    hidden = up_proj.shape[1]
    slots = range(blocks)

    def ctx_swap(values, k):
        return lax.ppermute(values, "ctx", [(i, i ^ k) for i in slots])

    def tp_swap(values, k):
        return lax.ppermute(values, "tp", [(i, i ^ k) for i in range(ranks)])

    def exchange(values):
        return lax.all_to_all(values, HEADS, split_axis=0, concat_axis=0, tiled=True)

    def own_rows(values):
        return lax.dynamic_slice_in_dim(values.reshape(rows, width), own_tp * part, part, 0)

    def in_swap_order(values, axis):
        return [lax.dynamic_index_in_dim(values, own_ctx ^ k, axis, keepdims=False) for k in slots]

    x_all = lax.all_gather(hidden_in, "ctx", axis=1, tiled=True)
    small = jnp.concatenate(
        [v.reshape(-1) for v in (norm_gain, norm_bias, out_bias, self_qv_bias, cross_qv_bias, up_bias)]
    )
    small = lax.all_gather(small, ("dp", "ctx", "tp")).reshape(plane, ranks, -1)
    vectors = small[:, 0, : 9 * shard].reshape(plane, 9, shard).swapaxes(0, 1).reshape(9, width)
    vectors = vectors.astype(F32)
    gains, shifts, branch_bias = vectors[:3], vectors[3:6], vectors[6:]
    at = 9 * shard
    bias_part = 2 * HEAD // plane
    count = heads_here * bias_part

    def head_bias(values):
        values = values.reshape(plane, ranks, heads_here, bias_part)
        return values.transpose(1, 2, 0, 3).reshape(all_heads, 2 * HEAD).astype(F32)

    self_bias = head_bias(small[:, :, at : at + count])
    cross_bias = head_bias(small[:, :, at + count : at + 2 * count])
    up_vector = (
        small[:, :, at + 2 * count :]
        .reshape(plane, ranks, hidden // (up_bias.shape[1] * plane), up_bias.shape[1])
        .transpose(1, 2, 0, 3)
        .reshape(ranks, hidden)
        .astype(F32)
    )
    up_vector = jnp.concatenate(
        [
            lax.dynamic_index_in_dim(up_vector, own_tp, 0, keepdims=False),
            lax.dynamic_index_in_dim(up_vector, own_tp ^ 2, 0, keepdims=False),
        ]
    )

    own_head = (
        self_proj.reshape(3, shard, heads_here, HEAD).transpose(2, 0, 3, 1).reshape(blocks, 3 * HEAD, shard)
    )
    own_head = lax.all_to_all(own_head, "ctx", split_axis=0, concat_axis=0, tiled=True)
    own_head = lax.all_gather(own_head, "dp")
    own_head = own_head.transpose(2, 0, 1, 3).reshape(3 * HEAD, width)

    kv_weights = cross_kv_proj.reshape(2, shard, heads_here, HEAD).transpose(1, 2, 0, 3)
    kv_weights = lax.all_gather(
        kv_weights.reshape(shard, heads_here * 2 * HEAD), PLANE, axis=0, tiled=True
    )
    square = jnp.stack(
        [self_proj[0], self_proj[1], self_proj[2], cross_q_proj, self_out_proj.T, cross_out_proj.T]
    )
    square = lax.all_gather(square, "tp", axis=2, tiled=True)
    square = square.transpose(1, 0, 2).reshape(shard, 6 * width)
    square = lax.all_gather(square, PLANE, axis=0, tiled=True)
    proj_q, proj_k, proj_v, cross_q_all, self_out_all, cross_out_all = (
        square[:, i * width : (i + 1) * width] for i in range(6)
    )
    mlp = jnp.concatenate([up_proj, down_proj.T], 1)
    mlp_other = tp_swap(mlp, 2)
    mlp = jnp.concatenate(
        [mlp[:, :hidden], mlp_other[:, :hidden], mlp[:, hidden:], mlp_other[:, hidden:]], 1
    )
    mlp = lax.all_gather(mlp, PLANE, axis=0, tiled=True)
    up_all, down_all = mlp[:, : 2 * hidden], mlp[:, 2 * hidden :]

    head_row = lax.dynamic_index_in_dim(self_bias, own_tp * blocks + own_ctx, 0, keepdims=False)
    query_column = head_row[:HEAD].reshape(HEAD, 1)
    pair_row = jnp.concatenate([jnp.zeros((HEAD,), F32), head_row[HEAD:]]).reshape(1, 2 * HEAD)
    chunk_shape = (ranks, blocks, HEAD, part)
    self_query, self_pair, self_mixed, self_lse = self_forward(
        x_all, own_head, query_column, pair_row, chunk_shape
    )
    tokens_f = own_rows(hidden_in).astype(F32)
    mixed_t = exchange(self_mixed.reshape(all_heads, HEAD, part)).reshape(width, part)
    attn_branch = contract(mixed_t, self_out_all, 0, 1) + branch_bias[0]
    first_out, first_normed, first_inv = norm_forward(tokens_f + attn_branch, gains[0], shifts[0])
    first_low = first_out.astype(BF16)
    cross_query = (
        contract(cross_q_all, first_low, 0, 1) + cross_bias[:, :HEAD].reshape(width, 1)
    ).astype(BF16) * HEAD**-0.5
    cross_query = exchange(cross_query.reshape(all_heads, HEAD, part)).reshape(chunk_shape)

    enc_rows = encoder_states.reshape(-1, width)
    kv_slots = in_swap_order(kv_weights.reshape(width, heads_here, 2 * HEAD), 1)
    kv_weights = jnp.concatenate(kv_slots, 1)
    value_bias = lax.dynamic_slice_in_dim(cross_bias, own_tp * heads_here, heads_here, 0)
    value_bias = jnp.concatenate([jnp.zeros((heads_here, HEAD), F32), value_bias[:, HEAD:]], 1)
    value_bias = jnp.concatenate(in_swap_order(value_bias, 0))
    enc_pairs = (contract(enc_rows, kv_weights, 1, 0) + value_bias).astype(BF16)
    pairs = []
    for k in slots:
        pair = enc_pairs[:, k * 2 * HEAD : (k + 1) * 2 * HEAD].reshape(seqs, enc_len, 2 * HEAD)
        pairs.append(ctx_swap(pair, k) if k else pair)
    cross_mixed, cross_lse = cross_forward(cross_query, pairs)
    cross_t = exchange(cross_mixed.reshape(all_heads, HEAD, part)).reshape(width, part)
    cross_branch = contract(cross_t, cross_out_all, 0, 1) + branch_bias[1]
    second_out, second_normed, second_inv = norm_forward(
        first_low.astype(F32) + cross_branch, gains[1], shifts[1]
    )
    second_low = second_out.astype(BF16)

    two = jnp.concatenate([second_low, tp_swap(second_low, 1)])
    pre_act = contract(two, up_all, 1, 0) + up_vector
    active = exact_gelu(pre_act).astype(BF16)
    mlp_part = contract(active, down_all, 1, 1)
    mlp_branch = (
        mlp_part[:part] + tp_swap(mlp_part[part:].astype(BF16), 1).astype(F32) + branch_bias[2]
    )
    third_out, third_normed, third_inv = norm_forward(
        second_low.astype(F32) + mlp_branch, gains[2], shifts[2]
    )
    hidden_out = lax.all_gather(third_out.astype(BF16), "tp", axis=0, tiled=True)
    rms = jnp.stack([root_mean(attn_branch), root_mean(cross_branch), root_mean(mlp_branch)])
    rms = lax.all_gather(rms, "tp", axis=1, tiled=True)
    rms = jnp.concatenate([root_mean(hidden_in.reshape(rows, width).astype(F32))[None], rms])

    out_grad = own_rows(out_cotangent).astype(F32)
    third_grad, gain_two, shift_two = norm_backward(out_grad, third_normed, third_inv, gains[2])
    mlp_bias_grad = jnp.sum(third_grad, 0)
    mlp_low = third_grad.astype(BF16)
    mlp_low = jnp.concatenate([mlp_low, tp_swap(mlp_low, 1)])
    active_grad = contract(mlp_low, down_all, 1, 0)
    pre_low = jax.vjp(exact_gelu, pre_act)[1](active_grad)[0].astype(BF16)
    back_part = contract(pre_low, up_all, 1, 1)
    back = back_part[:part] + tp_swap(back_part[part:].astype(BF16), 1).astype(F32)
    up_bias_grad = jnp.sum(pre_low.astype(F32), 0).reshape(2, hidden)
    mlp_grad = jnp.concatenate(
        [contract(two, pre_low, 0, 0).astype(BF16), contract(mlp_low, active, 0, 0).astype(BF16)], 1
    )
    mlp_grad = lax.psum_scatter(mlp_grad, PLANE, scatter_dimension=0, tiled=True)
    mlp_grad = mlp_grad.reshape(shard, 2, 2, hidden)
    mlp_grad = mlp_grad[:, :, 0].astype(F32) + tp_swap(mlp_grad[:, :, 1], 2).astype(F32)
    up_out, down_out = mlp_grad[:, 0], mlp_grad[:, 1].T

    second_grad, gain_one, shift_one = norm_backward(
        third_grad + back, second_normed, second_inv, gains[1]
    )
    cross_bias_sum = jnp.sum(second_grad, 0)
    second_grad_low = second_grad.astype(BF16)
    cross_out_grad = contract(second_grad_low, cross_t, 0, 1).astype(BF16)
    mix_grad = contract(cross_out_all, second_grad_low, 0, 1).astype(BF16)
    mix_grad = exchange(mix_grad.reshape(all_heads, HEAD, part)).reshape(chunk_shape)
    *pair_grads, query_grad = cross_backward(cross_query, cross_mixed, mix_grad, cross_lse, pairs)
    query_grad = exchange(query_grad.reshape(all_heads, HEAD, part)).reshape(width, part)
    pair_grads = [ctx_swap(g, k) if k else g for k, g in enumerate(pair_grads)]
    pair_grads = jnp.concatenate([g.reshape(-1, 2 * HEAD) for g in pair_grads], 1)
    enc_part = contract(pair_grads, kv_weights, 1, 1).astype(BF16)
    encoder_grad = lax.psum_scatter(
        enc_part.reshape(seqs, enc_len, width), "tp", scatter_dimension=2, tiled=True
    ).astype(F32)
    kv_grad = contract(enc_rows, pair_grads, 0, 0).astype(BF16)
    kv_grad = jnp.concatenate(in_swap_order(kv_grad.reshape(width, heads_here, 2 * HEAD), 1), 1)
    kv_grad = lax.psum_scatter(kv_grad, PLANE, scatter_dimension=0, tiled=True).astype(F32)
    kv_grad = kv_grad.reshape(shard, heads_here, 2, HEAD).transpose(2, 0, 1, 3).reshape(2, shard, local_width)
    value_sum = jnp.sum(pair_grads.astype(F32), 0).reshape(heads_here, 2 * HEAD)
    value_sum = jnp.stack(in_swap_order(value_sum, 0))[:, HEAD:]
    query_sum = jnp.sum(query_grad.astype(F32), 1).reshape(all_heads, HEAD)

    cross_q_grad = contract(first_low, query_grad, 0, 1).astype(BF16)
    first_grad, gain_zero, shift_zero = norm_backward(
        second_grad + contract(query_grad, cross_q_all, 0, 1), first_normed, first_inv, gains[0]
    )
    attn_bias_sum = jnp.sum(first_grad, 0)
    first_grad_low = first_grad.astype(BF16)
    self_out_grad = contract(first_grad_low, mixed_t, 0, 1).astype(BF16)
    square_grad = jnp.concatenate([self_out_grad, cross_q_grad, cross_out_grad], 1)
    square_grad = lax.psum_scatter(square_grad, PLANE, scatter_dimension=0, tiled=True)
    square_grad = lax.psum_scatter(
        square_grad.reshape(shard, 3, width), "tp", scatter_dimension=2, tiled=True
    ).astype(F32)
    self_out_out, cross_q_out, cross_out_out = (
        square_grad[:, 0].T,
        square_grad[:, 1],
        square_grad[:, 2].T,
    )
    self_mix_grad = contract(self_out_all, first_grad_low, 0, 1).astype(BF16)
    self_mix_grad = exchange(self_mix_grad.reshape(all_heads, HEAD, part)).reshape(chunk_shape)
    stacked, head_grad, head_sum = self_backward(
        x_all, self_query, self_pair, self_mixed, self_mix_grad, self_lse
    )
    stacked = exchange(stacked.reshape(all_heads, 3 * HEAD, part)).reshape(all_heads, 3, HEAD, part)
    stacked = stacked.swapaxes(0, 1).reshape(3, width, part)
    input_grad = first_grad + (
        contract(stacked[0], proj_q, 0, 1)
        + contract(stacked[1], proj_k, 0, 1)
        + contract(stacked[2], proj_v, 0, 1)
    )
    input_grad = lax.all_gather(input_grad.astype(BF16), "tp", axis=0, tiled=True).astype(F32)

    head_grad = head_grad.astype(BF16).reshape(3 * HEAD, plane, shard).swapaxes(0, 1)
    head_grad = lax.all_to_all(head_grad, PLANE, split_axis=0, concat_axis=0, tiled=True)
    head_grad = jnp.sum(head_grad.reshape(-1, blocks, 3, HEAD, shard).astype(F32), 0)
    self_proj_out = head_grad.transpose(1, 3, 0, 2).reshape(3, shard, local_width)

    norm_sums = jnp.stack(
        [gain_zero, gain_one, gain_two, shift_zero, shift_one, shift_two]
        + [attn_bias_sum, cross_bias_sum, mlp_bias_grad]
    )
    norm_sums = norm_sums.reshape(9, plane, 1, shard).transpose(1, 2, 0, 3).reshape(plane, 1, 9 * shard)
    norm_sums = jnp.broadcast_to(norm_sums, (plane, ranks, 9 * shard))
    up_cols = up_bias.shape[1]
    up_sums = up_bias_grad.reshape(2, -1, plane, up_cols).transpose(2, 0, 1, 3).reshape(plane, 2, -1)
    rank_ids = jnp.arange(ranks).reshape(1, ranks, 1)
    up_sums = jnp.where(rank_ids == own_tp, up_sums[:, :1], 0.0) + jnp.where(
        rank_ids == own_tp ^ 2, up_sums[:, 1:], 0.0
    )

    def bias_pieces(values):
        values = values.reshape(ranks, heads_here, plane, bias_part)
        return values.transpose(2, 0, 1, 3).reshape(plane, ranks, count)

    own_heads = (jnp.arange(all_heads) // heads_here == own_tp).reshape(all_heads, 1)
    value_full = jnp.where(own_heads, jnp.tile(value_sum, (ranks, 1)), 0.0)
    cross_sums = bias_pieces(jnp.concatenate([query_sum, value_full], 1))
    head_sum = head_sum.reshape(3, HEAD)
    own_head_id = (jnp.arange(all_heads) == own_tp * blocks + own_ctx).reshape(all_heads, 1)
    self_sums = bias_pieces(
        jnp.where(own_head_id, jnp.concatenate([head_sum[0], head_sum[2]]), 0.0)
    )
    sums = jnp.concatenate([norm_sums, up_sums, cross_sums, self_sums], 2)
    sums = lax.all_to_all(
        sums.reshape(plane * ranks, -1), ("dp", "ctx", "tp"), split_axis=0, concat_axis=0, tiled=True
    )
    sums = jnp.sum(sums, 0)
    norm_out = sums[: 9 * shard].reshape(9, shard)
    up_size = hidden // plane
    at = 9 * shard + up_size
    return (
        hidden_out.reshape(seqs, block, width),
        input_grad.reshape(seqs, block, width),
        encoder_grad,
        self_proj_out,
        sums[at + count :].reshape(heads_here, bias_part),
        self_out_out,
        cross_q_out,
        kv_grad,
        sums[at : at + count].reshape(heads_here, bias_part),
        cross_out_out,
        up_out,
        sums[9 * shard : at].reshape(up_bias.shape),
        down_out,
        norm_out[:3],
        norm_out[3:6],
        norm_out[6:],
        rms.reshape(4, seqs, block),
    )


def solution(mesh):
    rows, heads, columns = P("dp", "ctx", None), P("tp", PLANE), P(PLANE, "tp")
    stacked, vectors = P(None, PLANE, "tp"), P(None, PLANE)
    weights = (
        stacked, heads, heads, columns, stacked, heads, heads, columns, heads, heads,
        vectors, vectors, vectors,
    )
    return jax.shard_map(
        body,
        mesh=mesh,
        in_specs=(rows, rows, rows) + weights,
        out_specs=(rows, rows, P("dp", "ctx", "tp")) + weights + (P(None, "dp", "ctx"),),
        check_vma=False,
    )
```

```python
import functools

import jax
import jax.numpy as jnp
from jax import lax
from jax.experimental import pallas as pl
from jax.experimental.pallas import tpu as pltpu
from jax.sharding import PartitionSpec as P

EPSILON = 1e-05
HEAD = 64
KEY_TILE = 512
ROW_TILE = 512
COST_SHARE = 10
VMEM_BYTES = 50 * 1024 * 1024
PLANE = ("dp", "ctx")
HEADS = ("tp", "ctx")
F32 = jnp.float32
BF16 = jnp.bfloat16
IN_SMEM = pl.BlockSpec(memory_space=pltpu.SMEM)


def contract(left, right, left_dim, right_dim):
    return lax.dot_general(
        left, right, (((left_dim,), (right_dim,)), ((), ())), preferred_element_type=F32
    )


def together(*values):
    return lax.optimization_barrier(values)


def norm_forward(values, norm_gain, norm_shift):
    row_mean = jnp.mean(values, -1, keepdims=True)
    centered = values - row_mean
    inv_std = lax.rsqrt(jnp.mean(centered * centered, -1, keepdims=True) + EPSILON)
    normed = centered * inv_std
    return (normed * norm_gain + norm_shift, normed, inv_std)


def norm_backward(gradient, normed, inv_std, norm_gain):
    gain_grad = jnp.sum(gradient * normed, 0)
    shift_grad = jnp.sum(gradient, 0)
    scaled = gradient * norm_gain
    input_part = inv_std * (
        scaled
        - jnp.mean(scaled, -1, keepdims=True)
        - normed * jnp.mean(scaled * normed, -1, keepdims=True)
    )
    return (input_part, gain_grad, shift_grad)


def root_mean(values):
    return jnp.sqrt(jnp.mean(values * values, -1))


def exact_gelu(values):
    return jax.nn.gelu(values, approximate=False)


def with_zeros_below(values):
    return jnp.concatenate([values, jnp.zeros_like(values)], 0)


def with_zeros_above(values):
    return jnp.concatenate([jnp.zeros_like(values), values], 0)


def gather_chunks(ref):
    halves, blocks = ref.shape[:2]
    return jnp.concatenate([ref[h, b] for h in range(halves) for b in range(blocks)], 1)


def slot_at(own, k, size):
    return pl.ds(pl.multiple_of((own ^ k) * size, size), size)


def first_pack_kernel(proj_ref, small_ref, out_ref):
    blocks = proj_ref.shape[2] // HEAD
    for j in range(3):
        turned = proj_ref[j].T
        for e in range(out_ref.shape[0]):
            head = e % blocks * HEAD
            out_ref[e, j * HEAD : (j + 1) * HEAD] = turned[head : head + HEAD]
    for e in range(out_ref.shape[0]):
        out_ref[e, 3 * HEAD :] = small_ref[...]


def square_pack_kernel(self_out_ref, cross_q_ref, cross_out_ref, out_ref):
    out_ref[0] = self_out_ref[...].T
    out_ref[1] = cross_q_ref[...]
    out_ref[2] = cross_out_ref[...].T


def mlp_pack_kernel(up_ref, down_ref, out_ref):
    width = up_ref.shape[1]
    out_ref[:, :width] = up_ref[...]
    out_ref[:, width:] = down_ref[...].T


def rank_kernel(at_ref, *refs):
    part_refs, out_ref = refs[:-1], refs[-1]
    for k, part_ref in enumerate(part_refs):
        count, _, columns = part_ref.shape
        for i in range(count):
            first = (i * len(part_refs) + (at_ref[0] ^ k)) * columns
            out_ref[:, pl.ds(pl.multiple_of(first, columns), columns)] = part_ref[i]


def self_forward_kernel(at_ref, *refs):
    x_refs, (w_ref, bq_ref, bv_ref, q_ref, kv_ref, o_ref, lse_ref) = refs[:-7], refs[-7:]
    weights = w_ref[...]
    halves, blocks, _, part = o_ref.shape
    block = halves * part
    scale = HEAD**-0.5
    for k, x_ref in enumerate(x_refs):
        here = slot_at(at_ref[0], k, block)
        tokens = x_ref[0]
        q_ref[0, :, here] = (contract(weights[:HEAD], tokens, 1, 1) + bq_ref[...]).astype(BF16) * scale
        kv_ref[0, here] = (contract(tokens, weights[HEAD:], 1, 1) + bv_ref[...]).astype(BF16)
    for i in range(blocks):
        keys = kv_ref[0, : (i + 1) * block]
        query = q_ref[0, :, i * block : (i + 1) * block]
        scores = contract(keys, with_zeros_below(query), 1, 0)
        top = jnp.max(scores, 0, keepdims=True)
        weight = jnp.exp(scores - top)
        total = jnp.sum(weight, 0, keepdims=True)
        mixed = contract(keys, weight.astype(BF16), 0, 0)[HEAD:]
        out = (mixed / total).astype(BF16)
        for h in range(halves):
            o_ref[h, i] = out[:, h * part : (h + 1) * part]
        lse_ref[0, :, i * block : (i + 1) * block] = top + jnp.log(total)


def cross_forward_kernel(q_ref, *refs):
    kv_refs, (o_ref, lse_ref) = refs[:-2], refs[-2:]
    halves, blocks, _, part = q_ref.shape
    query = with_zeros_below(gather_chunks(q_ref))
    top = total = mixed = None
    for kv_ref in kv_refs:
        for start in range(0, kv_ref.shape[1], KEY_TILE):
            pair = kv_ref[0, start : start + KEY_TILE]
            scores = contract(pair, query, 1, 0)
            tile_top = jnp.max(scores, 0, keepdims=True)
            new_top = tile_top if top is None else jnp.maximum(top, tile_top)
            weight = jnp.exp(scores - new_top)
            tile_total = jnp.sum(weight, 0, keepdims=True)
            tile_mixed = contract(pair, weight.astype(BF16), 0, 0)
            if top is None:
                total, mixed = tile_total, tile_mixed
            else:
                fade = jnp.exp(top - new_top)
                total = total * fade + tile_total
                mixed = mixed * fade + tile_mixed
            top = new_top
    out = (mixed[HEAD:] / total).astype(BF16)
    for h in range(halves):
        for b in range(blocks):
            at = (h * blocks + b) * part
            o_ref[h, b] = out[:, at : at + part]
    lse_ref[0] = top + jnp.log(total)


def cross_backward_kernel(q_ref, o_ref, do_ref, lse_ref, *refs):
    count = (len(refs) - 1) // 2
    kv_refs, dkv_refs, dq_ref = refs[:count], refs[count:-1], refs[-1]
    halves, blocks, _, part = q_ref.shape
    width = halves * blocks * part
    query = with_zeros_below(gather_chunks(q_ref))
    grad = gather_chunks(do_ref)
    inner = jnp.sum(
        grad.astype(F32) * gather_chunks(o_ref).astype(F32), 0, keepdims=True
    )
    grad = with_zeros_above(grad)
    both = jnp.concatenate([query, grad], 1)
    lse = lse_ref[0]
    query_grad = None
    for kv_ref, dkv_ref in zip(kv_refs, dkv_refs):
        for start in range(0, kv_ref.shape[1], KEY_TILE):
            pair = kv_ref[0, start : start + KEY_TILE]
            products = contract(pair, both, 1, 0)
            weight = jnp.exp(products[:, :width] - lse)
            slope = (weight * (products[:, width:] - inner)).astype(BF16)
            dkv_ref[0, start : start + KEY_TILE] = (
                contract(slope, query, 1, 1) + contract(weight.astype(BF16), grad, 1, 1)
            ).astype(BF16)
            part_grad = contract(pair, slope, 0, 0)
            query_grad = part_grad if query_grad is None else query_grad + part_grad
    out = (query_grad[:HEAD] * HEAD**-0.5).astype(BF16)
    for h in range(halves):
        for b in range(blocks):
            at = (h * blocks + b) * part
            dq_ref[h, b] = out[:, at : at + part]


def self_backward_kernel(at_ref, *refs):
    x_refs, refs = refs[:-10], refs[-10:]
    q_ref, kv_ref, o_ref, do_ref, lse_ref, grad_ref, dw_ref, db_ref, dkv_ref, all_ref = refs
    halves, blocks, _, part = o_ref.shape
    block = halves * part
    dkv_ref[...] = jnp.zeros_like(dkv_ref)
    parts = []
    for i in range(blocks):
        lanes = slice(i * block, (i + 1) * block)
        reach = (i + 1) * block
        keys = kv_ref[0, :reach]
        query = with_zeros_below(q_ref[0, :, lanes])
        grad = jnp.concatenate([do_ref[h, i] for h in range(halves)], 1)
        mixed = jnp.concatenate([o_ref[h, i] for h in range(halves)], 1)
        inner = jnp.sum(grad.astype(F32) * mixed.astype(F32), 0, keepdims=True)
        grad = with_zeros_above(grad)
        weight = jnp.exp(contract(keys, query, 1, 0) - lse_ref[0, :, lanes])
        slope = (weight * (contract(keys, grad, 1, 0) - inner)).astype(BF16)
        parts.append(contract(keys, slope, 0, 0)[:HEAD] * HEAD**-0.5)
        dkv_ref[:, :reach] += contract(query, slope, 1, 1) + contract(
            grad, weight.astype(BF16), 1, 1
        )
    grads = jnp.concatenate(
        [jnp.concatenate(parts, 1).astype(BF16), dkv_ref[...].astype(BF16)], 0
    )
    all_ref[...] = grads
    for i in range(blocks):
        for h in range(halves):
            at = i * block + h * part
            grad_ref[h, i] = grads[:, at : at + part]

    @pl.when(pl.program_id(0) == 0)
    def _():
        dw_ref[...] = jnp.zeros_like(dw_ref)
        db_ref[...] = jnp.zeros_like(db_ref)

    dw_ref[...] += sum(
        contract(all_ref[:, slot_at(at_ref[0], k, block)], x_ref[0], 1, 0)
        for k, x_ref in enumerate(x_refs)
    )
    db_ref[...] += jnp.sum(grads.astype(F32), 1, keepdims=True)


def encoder_kernel(at_ref, e_ref, w_ref, b_ref, *refs):
    out_refs, all_ref = refs[:-1], refs[-1]
    all_ref[...] = (contract(e_ref[...], w_ref[...], 1, 0) + b_ref[...]).astype(BF16)
    for k, out_ref in enumerate(out_refs):
        out_ref[...] = all_ref[:, slot_at(at_ref[0], k, 2 * HEAD)]


def encoder_back_kernel(at_ref, e_ref, w_ref, *refs):
    grad_refs, (part_ref, sum_ref, dw_ref, total_ref, all_ref) = refs[:-5], refs[-5:]
    for k, grad_ref in enumerate(grad_refs):
        all_ref[:, slot_at(at_ref[0], k, 2 * HEAD)] = grad_ref[...]
    grads = all_ref[...]
    part_ref[...] = contract(grads, w_ref[...], 1, 1).astype(BF16)

    @pl.when(pl.program_id(0) == 0)
    def _():
        total_ref[...] = jnp.zeros_like(total_ref)
        sum_ref[...] = jnp.zeros_like(sum_ref)

    total_ref[...] += contract(e_ref[...], grads, 0, 0)
    sum_ref[...] += jnp.sum(grads.astype(F32), 0, keepdims=True)

    @pl.when(pl.program_id(0) == pl.num_programs(0) - 1)
    def _():
        dw_ref[...] = total_ref[...].astype(BF16)


def plane_grad_kernel(sides, ready, at_ref, *refs):
    count = len(sides)
    lefts, rights, refs = refs[:count], refs[count : 2 * count], refs[2 * count :]
    ready_refs, out_refs = refs[:ready], refs[ready:]
    shard = out_refs[0].shape[1]
    for bit, out_ref in enumerate(out_refs):
        here = slot_at(at_ref[0], 2 * pl.program_id(0) + bit, shard)
        column = 0
        for left, right, side in zip(lefts, rights, sides):
            width = right.shape[1 - side]
            out_ref[0, :, column : column + width] = contract(
                left[:, here], right[...], 0, side
            ).astype(BF16)
            column += width
        for ready_ref in ready_refs:
            width = ready_ref.shape[1]
            out_ref[0, :, column : column + width] = ready_ref[here]
            column += width


def mlp_grad_kernel(two_ref, pre_ref, low_ref, active_ref, out_ref):
    width = pre_ref.shape[1]
    out_ref[:, :width] = contract(two_ref[...], pre_ref[...], 0, 0).astype(BF16)
    out_ref[:, width:] = contract(low_ref[...], active_ref[...], 0, 0).astype(BF16)


def halve_kernel(keep_ref, got_ref, *out_refs):
    size = out_refs[0].shape[0]
    for i, out_ref in enumerate(out_refs):
        for j in range(size):
            total = keep_ref[i * size + j].astype(F32) + got_ref[i * size + j].astype(F32)
            out_ref[j] = total.astype(BF16)


def by_first(shape, lead=1):
    return pl.BlockSpec((lead,) + shape[1:], lambda s: (s,) + (0,) * (len(shape) - 1))


def whole(shape):
    return pl.BlockSpec(shape, lambda s: (0,) * len(shape))


def shaped(shape, dtype):
    return jax.ShapeDtypeStruct(shape, dtype)


def call(kernel, seqs, in_specs, out_specs, out_shape, operands, cost, scratch=()):
    flops, transcendentals = cost
    moved = sum(o.size * o.dtype.itemsize for o in operands)
    moved += sum(o.size * o.dtype.itemsize for o in out_shape)
    return pl.pallas_call(
        kernel,
        grid=(seqs,),
        in_specs=in_specs,
        out_specs=out_specs,
        out_shape=out_shape,
        scratch_shapes=scratch,
        compiler_params=pltpu.CompilerParams(
            dimension_semantics=("arbitrary",), vmem_limit_bytes=VMEM_BYTES
        ),
        cost_estimate=pl.CostEstimate(
            flops=flops // COST_SHARE,
            bytes_accessed=moved // COST_SHARE,
            transcendentals=transcendentals // COST_SHARE,
        ),
    )(*operands)


def one_step(kernel, out, *operands, flops=0):
    specs = [IN_SMEM if v.dtype == jnp.int32 else whole(v.shape) for v in operands]
    return call(kernel, 1, specs, [whole(out)], [shaped(out, BF16)], operands, (flops, 0))[0]


def self_forward(at, slots, weights, query_bias, pair_bias, chunk_shape):
    seqs, block, width = slots[0].shape
    length = block * len(slots)
    halves = chunk_shape[0] // seqs
    query, pair, lse = (seqs, HEAD, length), (seqs, length, 2 * HEAD), (seqs, 1, length)
    return call(
        self_forward_kernel,
        seqs,
        [IN_SMEM]
        + [by_first(x.shape) for x in slots]
        + [whole(weights.shape), whole(query_bias.shape), whole(pair_bias.shape)],
        [by_first(query), by_first(pair), by_first(chunk_shape, halves), by_first(lse)],
        [shaped(query, BF16), shaped(pair, BF16), shaped(chunk_shape, BF16), shaped(lse, F32)],
        [at, *slots, weights, query_bias, pair_bias],
        (seqs * length * (2 * width * 3 * HEAD + 8 * length * HEAD), seqs * length * length),
    )


def cross_forward(query, pairs):
    seqs = pairs[0].shape[0]
    halves, blocks, _, part = query.shape
    halves //= seqs
    length = halves * blocks * part
    keys = sum(p.shape[1] for p in pairs)
    lse = (seqs, 1, length)
    return call(
        cross_forward_kernel,
        seqs,
        [by_first(query.shape, halves)] + [by_first(p.shape) for p in pairs],
        [by_first(query.shape, halves), by_first(lse)],
        [shaped(query.shape, BF16), shaped(lse, F32)],
        [query, *pairs],
        (seqs * length * keys * 8 * HEAD, seqs * length * keys),
    )


def cross_backward(query, mixed, grad, lse, pairs):
    seqs = pairs[0].shape[0]
    halves, blocks, _, part = query.shape
    halves //= seqs
    length = halves * blocks * part
    keys = sum(p.shape[1] for p in pairs)
    chunk = by_first(query.shape, halves)
    return call(
        cross_backward_kernel,
        seqs,
        [chunk, chunk, chunk, by_first(lse.shape)] + [by_first(p.shape) for p in pairs],
        [by_first(p.shape) for p in pairs] + [chunk],
        [shaped(p.shape, BF16) for p in pairs] + [shaped(query.shape, BF16)],
        [query, mixed, grad, lse, *pairs],
        (seqs * length * keys * 20 * HEAD, seqs * length * keys),
    )


def self_backward(at, slots, query, pair, mixed, grad, lse):
    seqs, block, width = slots[0].shape
    length = block * len(slots)
    halves = mixed.shape[0] // seqs
    chunk = by_first(mixed.shape, halves)
    out = mixed.shape[:2] + (3 * HEAD, mixed.shape[3])
    return call(
        self_backward_kernel,
        seqs,
        [IN_SMEM]
        + [by_first(x.shape) for x in slots]
        + [by_first(query.shape), by_first(pair.shape), chunk, chunk, by_first(lse.shape)],
        [by_first(out, halves), whole((3 * HEAD, width)), whole((3 * HEAD, 1))],
        [shaped(out, BF16), shaped((3 * HEAD, width), F32), shaped((3 * HEAD, 1), F32)],
        [at, *slots, query, pair, mixed, grad, lse],
        (seqs * length * (2 * width * 3 * HEAD + 20 * length * HEAD), seqs * length * length),
        [pltpu.VMEM((2 * HEAD, length), F32), pltpu.VMEM((3 * HEAD, length), BF16)],
    )


def encoder_pairs(at, rows, weights, bias, count):
    length, width = rows.shape
    tile = min(ROW_TILE, length)
    pair = (length, 2 * HEAD)
    return call(
        encoder_kernel,
        length // tile,
        [IN_SMEM, by_first(rows.shape, tile), whole(weights.shape), whole(bias.shape)],
        [by_first(pair, tile)] * count,
        [shaped(pair, BF16)] * count,
        [at, rows, weights, bias],
        (2 * length * width * weights.shape[1], 0),
        [pltpu.VMEM((tile, weights.shape[1]), BF16)],
    )


def encoder_back(at, rows, weights, grads):
    length, width = rows.shape
    tile = min(ROW_TILE, length)
    columns = weights.shape[1]
    return call(
        encoder_back_kernel,
        length // tile,
        [IN_SMEM, by_first(rows.shape, tile), whole(weights.shape)]
        + [by_first(g.shape, tile) for g in grads],
        [by_first(rows.shape, tile), whole((1, columns)), whole(weights.shape)],
        [shaped(rows.shape, BF16), shaped((1, columns), F32), shaped(weights.shape, BF16)],
        [at, rows, weights, *grads],
        (4 * length * width * columns, 0),
        [pltpu.VMEM(weights.shape, F32), pltpu.VMEM((tile, columns), BF16)],
    )


def mlp_grads(two, pre_low, low, active):
    count, width = two.shape
    columns = pre_low.shape[1]
    tile = 256
    strip = pl.BlockSpec((count, tile), lambda i: (0, i))
    out = (width, 2 * columns)
    return call(
        mlp_grad_kernel,
        width // tile,
        [strip, whole(pre_low.shape), strip, whole(active.shape)],
        [by_first(out, tile)],
        [shaped(out, BF16)],
        [two, pre_low, low, active],
        (4 * count * width * columns, 0),
    )[0]


def halve(keep, got, groups):
    count, rows, columns = keep.shape
    tile = min(512, columns)
    stack = pl.BlockSpec((count, rows, tile), lambda i: (0, 0, i))
    strip = pl.BlockSpec((count // groups, rows, tile), lambda i: (0, 0, i))
    return call(
        halve_kernel,
        columns // tile,
        [stack, stack],
        [strip] * groups,
        [shaped((count // groups, rows, columns), BF16)] * groups,
        [keep, got],
        (keep.size, 0),
    )


def plane_grads(at, items, ready, shard):
    lefts, rights, sides = zip(*items) if items else ((), (), ())
    width = (lefts[0].T if items else ready[0]).shape[0]
    columns = sum(right.shape[1 - side] for right, side in zip(rights, sides))
    columns += sum(v.shape[1] for v in ready)
    out = (width // shard // 2, shard, columns)
    flops = sum(2 * width * right.size for right in rights)
    return call(
        functools.partial(plane_grad_kernel, sides, len(ready)),
        out[0],
        [IN_SMEM] + [whole(v.shape) for v in (*lefts, *rights, *ready)],
        [by_first(out)] * 2,
        [shaped(out, BF16)] * 2,
        [at, *lefts, *rights, *ready],
        (flops, 0),
    )


def body(
    hidden_in,
    encoder_states,
    out_cotangent,
    self_proj,
    self_qv_bias,
    self_out_proj,
    cross_q_proj,
    cross_kv_proj,
    cross_qv_bias,
    cross_out_proj,
    up_proj,
    up_bias,
    down_proj,
    norm_gain,
    norm_bias,
    out_bias,
):
    blocks, ranks = lax.axis_size("ctx"), lax.axis_size("tp")
    plane = lax.axis_size("dp") * blocks
    own_ctx, own_tp = lax.axis_index("ctx"), lax.axis_index("tp")
    seqs, block, width = hidden_in.shape
    rows = seqs * block
    part = rows // ranks
    shard = width // plane
    heads_here = self_qv_bias.shape[0]
    local_width = heads_here * HEAD
    all_heads = heads_here * ranks
    enc_len = encoder_states.shape[1]
    hidden = up_proj.shape[1]
    slots = range(blocks)

    def ctx_swap(values, k):
        return lax.ppermute(values, "ctx", [(i, i ^ k) for i in slots])

    def tp_swap(values, k):
        return lax.ppermute(values, "tp", [(i, i ^ k) for i in range(ranks)])

    def exchange(values):
        return lax.all_to_all(values, HEADS, split_axis=0, concat_axis=0, tiled=True)

    def own_rows(values):
        return lax.dynamic_slice_in_dim(values.reshape(rows, width), own_tp * part, part, 0)

    def in_swap_order(values, axis):
        return [lax.dynamic_index_in_dim(values, own_ctx ^ k, axis, keepdims=False) for k in slots]

    ctx_at, plane_at = own_ctx.reshape(1), (lax.axis_index("dp") * blocks + own_ctx).reshape(1)

    def plane_swap(values, k):
        return lax.ppermute(values, PLANE, [(i, i ^ k) for i in range(plane)])

    def sum_begin(items, ready=()):
        if plane == 8:
            keep, send = plane_grads(plane_at, items, ready, shard)
            return (keep, plane_swap(send, 1))
        sums = [contract(left, right, 0, side).astype(BF16) for left, right, side in items]
        sums = jnp.concatenate([*sums, *ready], 1)
        return (lax.psum_scatter(sums, PLANE, scatter_dimension=0, tiled=True),)

    def sum_near(state, groups):
        return halve(*state, groups) if plane == 8 else state

    def sum_far(parts):
        return [plane_swap(part, 2 * j) if j else part for j, part in enumerate(parts)]

    def sum_dp(parts):
        return [parts[0], plane_swap(parts[1], 4)] if plane == 8 else parts

    def sum_x(parts):
        if plane != 8:
            return parts
        own, other = (parts[0][j].astype(F32) + parts[1][j].astype(F32) for j in range(2))
        return [own, plane_swap(other.astype(BF16), 2)]

    def sum_end(parts):
        return sum(part.astype(F32).reshape(shard, -1) for part in parts)

    def whole_on_ranks(values):
        values = jnp.broadcast_to(values[None], (ranks,) + values.shape)
        return lax.all_to_all(values, "tp", split_axis=0, concat_axis=0, tiled=True)

    bias_part = 2 * HEAD // plane
    count = heads_here * bias_part
    core_tokens, x_tokens = ctx_swap(hidden_in, 1), ctx_swap(hidden_in, 2)
    rank_at = own_tp.reshape(1)

    def rank_parts(values):
        return [values] + [tp_swap(values, k) for k in range(1, ranks)]

    def from_ranks(parts):
        out = (shard, parts[0].shape[0] * width)
        return one_step(rank_kernel, out, rank_at, *parts)

    square = one_step(
        square_pack_kernel, (3, shard, local_width), self_out_proj, cross_q_proj, cross_out_proj
    )
    square = rank_parts(square)
    vectors = jnp.concatenate([norm_gain, norm_bias, out_bias])
    small = jnp.concatenate([v.reshape(-1) for v in (self_qv_bias, cross_qv_bias, up_bias)])
    small = jnp.concatenate([vectors, small.reshape(-1, shard)])
    small = jnp.pad(small, ((0, 16 - small.shape[0]), (0, 0)))
    first = one_step(
        first_pack_kernel, (plane, 3 * HEAD + small.shape[0], shard), self_proj, small, flops=1 << 38
    )
    first = lax.all_to_all(first, PLANE, split_axis=0, concat_axis=0, tiled=True)
    kv_weights = cross_kv_proj.reshape(2, shard, heads_here, HEAD).transpose(1, 2, 0, 3)
    kv_weights = lax.all_gather(
        kv_weights.reshape(shard, heads_here * 2 * HEAD), PLANE, axis=0, tiled=True
    )

    core_tokens, x_tokens, first, square, up_proj, down_proj = together(
        core_tokens, x_tokens, first, square, up_proj, down_proj
    )

    square = lax.all_gather(from_ranks(square), PLANE, axis=0, tiled=True)
    mlp = one_step(mlp_pack_kernel, (shard, 2 * hidden), up_proj, down_proj)
    mlp_other = tp_swap(mlp, 2)
    x_slots = [hidden_in, core_tokens, x_tokens, ctx_swap(x_tokens, 1)]
    own_head = first[:, : 3 * HEAD].swapaxes(0, 1).reshape(3 * HEAD, width)
    small = first[:, 3 * HEAD :]
    vectors = small[:, :9].swapaxes(0, 1).reshape(9, width).astype(F32)
    gains, shifts, branch_bias = vectors[:3], vectors[3:6], vectors[6:]
    small = small[:, 9:].reshape(plane, -1)

    def head_bias(values):
        values = values.reshape(plane, heads_here, bias_part).swapaxes(0, 1)
        return values.reshape(heads_here, 2 * HEAD).astype(F32)

    self_bias = head_bias(small[:, :count])
    cross_bias = head_bias(small[:, count : 2 * count])
    up_vector = small[:, 2 * count : 2 * count + up_bias.size]
    up_vector = up_vector.reshape((plane,) + up_bias.shape).swapaxes(0, 1).reshape(1, hidden)
    enc_rows = encoder_states.reshape(-1, width)
    value_bias = jnp.concatenate([jnp.zeros((heads_here, HEAD), F32), cross_bias[:, HEAD:]], 1)
    pairs = encoder_pairs(ctx_at, enc_rows, kv_weights, value_bias.reshape(1, -1), blocks)
    x_slots, pairs = together(x_slots, pairs)
    pairs = [
        (ctx_swap(pair, k) if k else pair).reshape(seqs, enc_len, 2 * HEAD)
        for k, pair in enumerate(pairs)
    ]
    head_row = lax.dynamic_index_in_dim(self_bias, own_ctx, 0, keepdims=False)
    query_column = head_row[:HEAD].reshape(HEAD, 1)
    pair_row = jnp.concatenate([jnp.zeros((HEAD,), F32), head_row[HEAD:]]).reshape(1, 2 * HEAD)
    chunk_shape = (ranks, blocks, HEAD, part)
    self_query, self_pair, self_mixed, self_lse = self_forward(
        ctx_at, x_slots, own_head, query_column, pair_row, chunk_shape
    )
    tokens_f = own_rows(hidden_in).astype(F32)
    mixed_t = exchange(self_mixed.reshape(all_heads, HEAD, part)).reshape(width, part)
    mixed_t, square, mlp_other, self_proj, pairs, up_vector = together(
        mixed_t, square, mlp_other, self_proj, pairs, up_vector
    )
    up_vector = jnp.concatenate([up_vector, tp_swap(up_vector, 2)], 1).astype(F32)
    self_out_all, cross_q_all, cross_out_all = (square[:, i * width : (i + 1) * width] for i in range(3))
    mlp = jnp.concatenate(
        [mlp[:, :hidden], mlp_other[:, :hidden], mlp[:, hidden:], mlp_other[:, hidden:]], 1
    )
    mlp = lax.all_gather(mlp, PLANE, axis=0, tiled=True)
    up_all, down_all = mlp[:, : 2 * hidden], mlp[:, 2 * hidden :]
    rank_proj = rank_parts(self_proj)
    attn_branch = contract(mixed_t, self_out_all, 0, 1) + branch_bias[0]
    first_out, first_normed, first_inv = norm_forward(tokens_f + attn_branch, gains[0], shifts[0])
    first_low = first_out.astype(BF16)
    cross_query = contract(cross_q_all, first_low, 0, 1).astype(BF16)
    cross_query = exchange(cross_query.reshape(all_heads, HEAD, part)).reshape(chunk_shape)
    cross_row = lax.dynamic_index_in_dim(cross_bias, own_ctx, 0, keepdims=False)[:HEAD]
    cross_query = (
        (cross_query.astype(F32) + cross_row.reshape(HEAD, 1)).astype(BF16) * HEAD**-0.5
    )

    cross_mixed, cross_lse = cross_forward(cross_query, pairs)
    cross_mixed, rank_proj = together(cross_mixed, rank_proj)
    proj = from_ranks(rank_proj)
    cross_t = exchange(cross_mixed.reshape(all_heads, HEAD, part)).reshape(width, part)
    cross_branch = contract(cross_t, cross_out_all, 0, 1) + branch_bias[1]
    second_out, second_normed, second_inv = norm_forward(
        first_low.astype(F32) + cross_branch, gains[1], shifts[1]
    )
    second_low = second_out.astype(BF16)

    two = jnp.concatenate([second_low, tp_swap(second_low, 1)])
    pre_act = contract(two, up_all, 1, 0) + up_vector
    active = exact_gelu(pre_act).astype(BF16)
    mlp_part = contract(active, down_all, 1, 1)
    mlp_branch = (
        mlp_part[:part] + tp_swap(mlp_part[part:].astype(BF16), 1).astype(F32) + branch_bias[2]
    )
    third_out, third_normed, third_inv = norm_forward(
        second_low.astype(F32) + mlp_branch, gains[2], shifts[2]
    )
    hidden_out = third_out.astype(BF16)
    rms = jnp.stack([root_mean(attn_branch), root_mean(cross_branch), root_mean(mlp_branch)])

    out_grad = own_rows(out_cotangent).astype(F32)
    third_grad, gain_two, shift_two = norm_backward(out_grad, third_normed, third_inv, gains[2])
    mlp_bias_grad = jnp.sum(third_grad, 0)
    mlp_low = third_grad.astype(BF16)
    mlp_low = jnp.concatenate([mlp_low, tp_swap(mlp_low, 1)])
    active_grad = contract(mlp_low, down_all, 1, 0)
    pre_low = jax.vjp(exact_gelu, pre_act)[1](active_grad)[0].astype(BF16)
    mlp_grad = mlp_grads(two, pre_low, mlp_low, active)
    back_part = contract(pre_low, up_all, 1, 1)
    back_part, mlp_grad = together(back_part, mlp_grad)
    mlp_grad = lax.psum_scatter(mlp_grad, PLANE, scatter_dimension=0, tiled=True)
    back = back_part[:part] + tp_swap(back_part[part:].astype(BF16), 1).astype(F32)
    up_bias_grad = jnp.sum(pre_low.astype(F32), 0).reshape(2, hidden)
    second_grad, gain_one, shift_one = norm_backward(
        third_grad + back, second_normed, second_inv, gains[1]
    )
    cross_bias_sum = jnp.sum(second_grad, 0)
    second_grad_low = second_grad.astype(BF16)
    mix_grad = contract(cross_out_all, second_grad_low, 0, 1).astype(BF16)
    mix_grad = exchange(mix_grad.reshape(all_heads, HEAD, part)).reshape(chunk_shape)
    mix_grad, hidden_out = together(mix_grad, hidden_out)
    hidden_out = whole_on_ranks(hidden_out)
    *pair_grads, query_grad = cross_backward(cross_query, cross_mixed, mix_grad, cross_lse, pairs)
    query_grad, hidden_out = together(query_grad, hidden_out)
    query_grad = exchange(query_grad.reshape(all_heads, HEAD, part)).reshape(width, part)
    pair_grads = [
        (ctx_swap(g, k) if k else g).reshape(-1, 2 * HEAD) for k, g in enumerate(pair_grads)
    ]
    query_grad, proj = together(query_grad, proj)
    proj = lax.all_gather(proj, PLANE, axis=0, tiled=True)
    mlp_grad = mlp_grad.reshape(shard, 2, 2, hidden)
    mlp_grad = [mlp_grad[:, :, 0], tp_swap(mlp_grad[:, :, 1], 2)]
    query_sum = jnp.sum(query_grad.astype(F32), 1)

    first_grad, gain_zero, shift_zero = norm_backward(
        second_grad + contract(query_grad, cross_q_all, 0, 1), first_normed, first_inv, gains[0]
    )
    attn_bias_sum = jnp.sum(first_grad, 0)
    first_grad_low = first_grad.astype(BF16)
    squares = [(first_grad_low, mixed_t, 1), (first_low, query_grad, 1), (second_grad_low, cross_t, 1)]
    square_grad = sum_begin(squares)

    self_mix_grad = contract(self_out_all, first_grad_low, 0, 1).astype(BF16)
    self_mix_grad = exchange(self_mix_grad.reshape(all_heads, HEAD, part)).reshape(chunk_shape)
    self_mix_grad, pair_grads = together(self_mix_grad, pair_grads)
    enc_part, value_sum, kv_grad = encoder_back(ctx_at, enc_rows, kv_weights, pair_grads)
    value_sum = value_sum.reshape(heads_here, 2 * HEAD)[:, HEAD:]
    self_mix_grad, enc_part, mlp_grad, kv_grad = together(self_mix_grad, enc_part, mlp_grad, kv_grad)
    mlp_grad = mlp_grad[0].astype(F32) + mlp_grad[1].astype(F32)
    up_out, down_out = mlp_grad[:, 0], mlp_grad[:, 1].T
    encoder_grad = lax.psum_scatter(
        enc_part.reshape(seqs, enc_len, width), "tp", scatter_dimension=2, tiled=True
    )
    kv_grad = sum_begin((), [kv_grad])
    stacked, head_grad, head_sum = self_backward(
        ctx_at, x_slots, self_query, self_pair, self_mixed, self_mix_grad, self_lse
    )
    stacked, head_grad, square_grad, kv_grad = together(stacked, head_grad, square_grad, kv_grad)
    kv_grad = sum_dp(sum_near(kv_grad, 2))
    square_grad = sum_near(square_grad, 4)
    stacked = exchange(stacked.reshape(all_heads, 3 * HEAD, part)).reshape(all_heads, 3, HEAD, part)
    stacked, head_grad, square_grad, kv_grad = together(stacked, head_grad, square_grad, kv_grad)
    square_grad, kv_grad = sum_far(square_grad), sum_x(kv_grad)
    square_grad = sum_end(square_grad)
    square_grad = square_grad.reshape(shard, 3, ranks, width // ranks)

    stacked = stacked.swapaxes(0, 1).reshape(3, width, part)
    input_grad = first_grad + (
        contract(stacked[0], proj[:, :width], 0, 1)
        + contract(stacked[1], proj[:, width : 2 * width], 0, 1)
        + contract(stacked[2], proj[:, 2 * width :], 0, 1)
    )
    input_grad = input_grad.astype(BF16)

    def for_rank(k):
        return lax.dynamic_index_in_dim(square_grad, own_tp ^ k, 2, False)

    square_grad = for_rank(0) + sum(
        tp_swap(for_rank(k).astype(BF16), k).astype(F32) for k in range(1, ranks)
    )
    self_out_out, cross_q_out, cross_out_out = (
        square_grad[:, 0].T,
        square_grad[:, 1],
        square_grad[:, 2].T,
    )
    head_grad = head_grad.reshape(3 * HEAD, plane, shard).swapaxes(0, 1)
    head_sum = head_sum.reshape(3, HEAD)
    head_sum = jnp.concatenate([head_sum[0], head_sum[2]]).reshape(plane, bias_part, 1)
    head_sum = jnp.pad(head_sum, ((0, 0), (0, 16 - bias_part), (0, 0)))
    def pieces(values):
        return values.reshape(-1, plane, values.shape[-1] // plane).swapaxes(0, 1).reshape(plane, -1)

    norm_sums = jnp.stack(
        [gain_zero, gain_one, gain_two, shift_zero, shift_one, shift_two]
        + [attn_bias_sum, cross_bias_sum, mlp_bias_grad]
    )
    up_cols = up_bias.shape[1]
    up_sums = pieces(up_bias_grad.reshape(-1, plane * up_cols))
    query_sums = pieces(jnp.pad(query_sum.reshape(all_heads, HEAD), ((0, 0), (0, HEAD))))
    value_sums = pieces(jnp.pad(value_sum, ((0, 0), (HEAD, 0))))
    sums = jnp.concatenate([pieces(norm_sums), up_sums, query_sums, value_sums], 1)
    sums = jnp.pad(sums, ((0, 0), (0, 16 * shard - sums.shape[1]))).reshape(plane, 16, shard)
    head_grad = jnp.concatenate(
        [head_grad, jnp.broadcast_to(head_sum, (plane, 16, shard)), sums], 1
    ).astype(BF16)
    head_grad = lax.all_to_all(head_grad, PLANE, split_axis=0, concat_axis=0, tiled=True)
    head_grad = head_grad.reshape(-1, blocks, 3 * HEAD + 32, shard).astype(F32)
    kv_grad = sum_end(kv_grad).reshape(shard, heads_here, 2, HEAD)
    kv_grad = kv_grad.transpose(2, 0, 1, 3).reshape(2, shard, local_width)
    sums = jnp.sum(head_grad[:, :, 3 * HEAD + 16 :], (0, 1))
    head_grad = jnp.sum(head_grad[:, :, : 3 * HEAD + 16], 0)
    self_proj_out = head_grad[:, : 3 * HEAD].reshape(blocks, 3, HEAD, shard)
    self_proj_out = self_proj_out.transpose(1, 3, 0, 2).reshape(3, shard, local_width)
    self_bias_out = head_grad[:, 3 * HEAD : 3 * HEAD + bias_part, 0]
    norm_out, sums = sums[:9].reshape(-1), sums[9:].reshape(-1)
    sums = jnp.concatenate([norm_out, sums[: 2 * up_bias.size + ranks * count + count], rms.reshape(-1)])
    ends = [0, norm_out.size]
    for size in (up_bias.size, up_bias.size, ranks * count, count, rms.size):
        ends.append(ends[-1] + size)
    sums = jnp.pad(sums, (0, 16 * width - sums.size)).reshape(16, width).astype(BF16)

    last = whole_on_ranks(jnp.concatenate([input_grad, sums]))
    last, encoder_grad = together(last, encoder_grad)
    input_grad, encoder_grad = last[:, :part].astype(F32), encoder_grad.astype(F32)
    sums = last[:, part:].astype(F32).reshape(ranks, -1)
    norm_out, up_own, up_other, query_sums, value_sums, rms = (
        sums[:, i:j] for i, j in zip(ends, ends[1:])
    )
    norm_out = jnp.sum(norm_out, 0).reshape(9, shard)

    def of_rank(values, at):
        return lax.dynamic_index_in_dim(values, at, 0, False)

    up_bias_out = (of_rank(up_own, own_tp) + of_rank(up_other, own_tp ^ 2)).reshape(up_bias.shape)
    cross_bias_out = of_rank(jnp.sum(query_sums, 0).reshape(ranks, count), own_tp)
    cross_bias_out = (cross_bias_out + of_rank(value_sums, own_tp)).reshape(heads_here, bias_part)
    rms = rms.reshape(ranks, 3, part).swapaxes(0, 1).reshape(3, rows)
    rms = jnp.concatenate([root_mean(hidden_in.reshape(rows, width).astype(F32))[None], rms])
    return (
        hidden_out.reshape(seqs, block, width),
        input_grad.reshape(seqs, block, width),
        encoder_grad,
        self_proj_out,
        self_bias_out,
        self_out_out,
        cross_q_out,
        kv_grad,
        cross_bias_out,
        cross_out_out,
        up_out,
        up_bias_out,
        down_out,
        norm_out[:3],
        norm_out[3:6],
        norm_out[6:],
        rms.reshape(4, seqs, block),
    )


def solution(mesh):
    rows, heads, columns = P("dp", "ctx", None), P("tp", PLANE), P(PLANE, "tp")
    stacked, vectors = P(None, PLANE, "tp"), P(None, PLANE)
    weights = (
        stacked, heads, heads, columns, stacked, heads, heads, columns, heads, heads,
        vectors, vectors, vectors,
    )
    return jax.shard_map(
        body,
        mesh=mesh,
        in_specs=(rows, rows, rows) + weights,
        out_specs=(rows, rows, P("dp", "ctx", "tp")) + weights + (P(None, "dp", "ctx"),),
        check_vma=False,
    )
```

```python
import functools

import jax
import jax.numpy as jnp
from jax import lax
from jax.experimental import pallas as pl
from jax.experimental.pallas import tpu as pltpu
from jax.sharding import PartitionSpec as P

EPSILON = 1e-05
HEAD = 64
KEY_TILE = 512
STAT_ROWS = 16
ROW_TILE = 512
COST_SHARE = 10
VMEM_BYTES = 50 * 1024 * 1024
PLANE = ("dp", "ctx")
HEADS = ("tp", "ctx")
F32 = jnp.float32
BF16 = jnp.bfloat16
IN_SMEM = pl.BlockSpec(memory_space=pltpu.SMEM)


def contract(left, right, left_dim, right_dim):
    return lax.dot_general(
        left, right, (((left_dim,), (right_dim,)), ((), ())), preferred_element_type=F32
    )


def together(*values):
    return lax.optimization_barrier(values)


def norm_forward(values, norm_gain, norm_shift):
    row_mean = jnp.mean(values, -1, keepdims=True)
    centered = values - row_mean
    inv_std = lax.rsqrt(jnp.mean(centered * centered, -1, keepdims=True) + EPSILON)
    normed = centered * inv_std
    return (normed * norm_gain + norm_shift, normed, inv_std)


def norm_backward(gradient, normed, inv_std, norm_gain):
    gain_grad = jnp.sum(gradient * normed, 0)
    shift_grad = jnp.sum(gradient, 0)
    scaled = gradient * norm_gain
    input_part = inv_std * (
        scaled
        - jnp.mean(scaled, -1, keepdims=True)
        - normed * jnp.mean(scaled * normed, -1, keepdims=True)
    )
    return (input_part, gain_grad, shift_grad)


def root_mean(values):
    return jnp.sqrt(jnp.mean(values * values, -1))


def exact_gelu(values):
    return jax.nn.gelu(values, approximate=False)


def with_zeros_below(values):
    return jnp.concatenate([values, jnp.zeros_like(values)], 0)


def with_zeros_above(values):
    return jnp.concatenate([jnp.zeros_like(values), values], 0)


def gather_chunks(ref):
    halves, blocks = ref.shape[:2]
    return jnp.concatenate([ref[h, b] for h in range(halves) for b in range(blocks)], 1)


def slot_at(own, k, size):
    return pl.ds(pl.multiple_of((own ^ k) * size, size), size)


def first_pack_kernel(proj_ref, small_ref, out_ref):
    blocks = proj_ref.shape[2] // HEAD
    for j in range(3):
        turned = proj_ref[j].T
        for e in range(out_ref.shape[0]):
            head = e % blocks * HEAD
            out_ref[e, j * HEAD : (j + 1) * HEAD] = turned[head : head + HEAD]
    for e in range(out_ref.shape[0]):
        out_ref[e, 3 * HEAD :] = small_ref[...]


def square_pack_kernel(self_out_ref, cross_q_ref, cross_out_ref, out_ref):
    out_ref[0] = self_out_ref[...].T
    out_ref[1] = cross_q_ref[...]
    out_ref[2] = cross_out_ref[...].T


def mlp_pack_kernel(up_ref, down_ref, out_ref):
    width = up_ref.shape[1]
    out_ref[:, :width] = up_ref[...]
    out_ref[:, width:] = down_ref[...].T


def rank_kernel(at_ref, *refs):
    part_refs, out_ref = refs[:-1], refs[-1]
    for k, part_ref in enumerate(part_refs):
        count, _, columns = part_ref.shape
        for i in range(count):
            first = (i * len(part_refs) + (at_ref[0] ^ k)) * columns
            out_ref[:, pl.ds(pl.multiple_of(first, columns), columns)] = part_ref[i]


def self_forward_kernel(at_ref, *refs):
    x_refs, (w_ref, bq_ref, bv_ref, q_ref, kv_ref, o_ref, lse_ref) = refs[:-7], refs[-7:]
    weights = w_ref[...]
    halves, blocks, _, part = o_ref.shape
    block = halves * part
    scale = HEAD**-0.5
    for k, x_ref in enumerate(x_refs):
        here = slot_at(at_ref[0], k, block)
        tokens = x_ref[0]
        q_ref[0, :, here] = (contract(weights[:HEAD], tokens, 1, 1) + bq_ref[...]).astype(BF16) * scale
        kv_ref[0, here] = (contract(tokens, weights[HEAD:], 1, 1) + bv_ref[...]).astype(BF16)
    for i in range(blocks):
        keys = kv_ref[0, : (i + 1) * block]
        query = q_ref[0, :, i * block : (i + 1) * block]
        scores = contract(keys, with_zeros_below(query), 1, 0)
        top = jnp.max(scores, 0, keepdims=True)
        weight = jnp.exp(scores - top)
        total = jnp.sum(weight, 0, keepdims=True)
        mixed = contract(keys, weight.astype(BF16), 0, 0)[HEAD:]
        out = (mixed / total).astype(BF16)
        for h in range(halves):
            o_ref[h, i] = out[:, h * part : (h + 1) * part]
        lse_ref[0, :, i * block : (i + 1) * block] = top + jnp.log(total)


def spread(values):
    rows = []
    for _ in range(3):
        rows.append(values.astype(BF16))
        values = values - rows[-1].astype(F32)
    return rows


def gathered(rows, at):
    return sum(rows[at + i : at + i + 1].astype(F32) for i in range(3))


def cross_forward_kernel(q_ref, *refs):
    kv_refs, o_ref = refs[:-1], refs[-1]
    halves, blocks, features, part = q_ref.shape
    queries = gather_chunks(q_ref)
    heads = features // HEAD
    outs, stats = [], []
    for n in range(heads):
        query = with_zeros_below(queries[n * HEAD : (n + 1) * HEAD])
        lanes = slice(n * 2 * HEAD, (n + 1) * 2 * HEAD)
        top = total = mixed = None
        for kv_ref in kv_refs:
            for start in range(0, kv_ref.shape[1], KEY_TILE):
                pair = kv_ref[0, start : start + KEY_TILE, lanes]
                scores = contract(pair, query, 1, 0)
                tile_top = jnp.max(scores, 0, keepdims=True)
                new_top = tile_top if top is None else jnp.maximum(top, tile_top)
                weight = jnp.exp(scores - new_top)
                tile_total = jnp.sum(weight, 0, keepdims=True)
                tile_mixed = contract(pair, weight.astype(BF16), 0, 0)
                if top is None:
                    total, mixed = tile_total, tile_mixed
                else:
                    fade = jnp.exp(top - new_top)
                    total = total * fade + tile_total
                    mixed = mixed * fade + tile_mixed
                top = new_top
        outs.append((mixed[HEAD:] / total).astype(BF16))
        stats += spread(top + jnp.log(total))
    spare = jnp.zeros((STAT_ROWS - len(stats), stats[0].shape[1]), BF16)
    out = jnp.concatenate([*outs, *stats, spare], 0)
    for h in range(halves):
        for b in range(blocks):
            at = (h * blocks + b) * part
            o_ref[h, b] = out[:, at : at + part]


def cross_backward_kernel(q_ref, do_ref, *refs):
    count = (len(refs) - 1) // 2
    kv_refs, dkv_refs, dq_ref = refs[:count], refs[count:-1], refs[-1]
    halves, blocks, features, part = q_ref.shape
    width = halves * blocks * part
    queries, grads = gather_chunks(q_ref), gather_chunks(do_ref)
    heads = features // HEAD
    outs = []
    for n in range(heads):
        query = with_zeros_below(queries[n * HEAD : (n + 1) * HEAD])
        grad = with_zeros_above(grads[n * HEAD : (n + 1) * HEAD])
        lse = gathered(grads, features + 6 * n)
        inner = gathered(grads, features + 6 * n + 3)
        lanes = slice(n * 2 * HEAD, (n + 1) * 2 * HEAD)
        both = jnp.concatenate([query, grad], 1)
        query_grad = None
        for kv_ref, dkv_ref in zip(kv_refs, dkv_refs):
            for start in range(0, kv_ref.shape[1], KEY_TILE):
                pair = kv_ref[0, start : start + KEY_TILE, lanes]
                products = contract(pair, both, 1, 0)
                weight = jnp.exp(products[:, :width] - lse)
                slope = (weight * (products[:, width:] - inner)).astype(BF16)
                dkv_ref[0, start : start + KEY_TILE, lanes] = (
                    contract(slope, query, 1, 1) + contract(weight.astype(BF16), grad, 1, 1)
                ).astype(BF16)
                part_grad = contract(pair, slope, 0, 0)
                query_grad = part_grad if query_grad is None else query_grad + part_grad
        outs.append((query_grad[:HEAD] * HEAD**-0.5).astype(BF16))
    out = jnp.concatenate(outs, 0)
    for h in range(halves):
        for b in range(blocks):
            at = (h * blocks + b) * part
            dq_ref[h, b] = out[:, at : at + part]


def self_backward_kernel(at_ref, *refs):
    x_refs, refs = refs[:-10], refs[-10:]
    q_ref, kv_ref, o_ref, do_ref, lse_ref, grad_ref, dw_ref, db_ref, dkv_ref, all_ref = refs
    halves, blocks, _, part = o_ref.shape
    block = halves * part
    dkv_ref[...] = jnp.zeros_like(dkv_ref)
    parts = []
    for i in range(blocks):
        lanes = slice(i * block, (i + 1) * block)
        reach = (i + 1) * block
        keys = kv_ref[0, :reach]
        query = with_zeros_below(q_ref[0, :, lanes])
        grad = jnp.concatenate([do_ref[h, i] for h in range(halves)], 1)
        mixed = jnp.concatenate([o_ref[h, i] for h in range(halves)], 1)
        inner = jnp.sum(grad.astype(F32) * mixed.astype(F32), 0, keepdims=True)
        grad = with_zeros_above(grad)
        weight = jnp.exp(contract(keys, query, 1, 0) - lse_ref[0, :, lanes])
        slope = (weight * (contract(keys, grad, 1, 0) - inner)).astype(BF16)
        parts.append(contract(keys, slope, 0, 0)[:HEAD] * HEAD**-0.5)
        dkv_ref[:, :reach] += contract(query, slope, 1, 1) + contract(
            grad, weight.astype(BF16), 1, 1
        )
    grads = jnp.concatenate(
        [jnp.concatenate(parts, 1).astype(BF16), dkv_ref[...].astype(BF16)], 0
    )
    all_ref[...] = grads
    for i in range(blocks):
        for h in range(halves):
            at = i * block + h * part
            grad_ref[h, i] = grads[:, at : at + part]

    @pl.when(pl.program_id(0) == 0)
    def _():
        dw_ref[...] = jnp.zeros_like(dw_ref)
        db_ref[...] = jnp.zeros_like(db_ref)

    dw_ref[...] += sum(
        contract(all_ref[:, slot_at(at_ref[0], k, block)], x_ref[0], 1, 0)
        for k, x_ref in enumerate(x_refs)
    )
    db_ref[...] += jnp.sum(grads.astype(F32), 1, keepdims=True)


def encoder_kernel(at_ref, e_ref, w_ref, b_ref, *refs):
    out_refs, all_ref = refs[:-1], refs[-1]
    all_ref[...] = (contract(e_ref[...], w_ref[...], 1, 0) + b_ref[...]).astype(BF16)
    for k, out_ref in enumerate(out_refs):
        out_ref[...] = all_ref[:, slot_at(at_ref[0], k, out_ref.shape[1])]


def encoder_back_kernel(at_ref, e_ref, w_ref, *refs):
    grad_refs, (part_ref, sum_ref, dw_ref, total_ref, all_ref) = refs[:-5], refs[-5:]
    for k, grad_ref in enumerate(grad_refs):
        all_ref[:, slot_at(at_ref[0], k, grad_ref.shape[1])] = grad_ref[...]
    grads = all_ref[...]
    part_ref[...] = contract(grads, w_ref[...], 1, 1).astype(BF16)

    @pl.when(pl.program_id(0) == 0)
    def _():
        total_ref[...] = jnp.zeros_like(total_ref)
        sum_ref[...] = jnp.zeros_like(sum_ref)

    total_ref[...] += contract(e_ref[...], grads, 0, 0)
    sum_ref[...] += jnp.sum(grads.astype(F32), 0, keepdims=True)

    @pl.when(pl.program_id(0) == pl.num_programs(0) - 1)
    def _():
        dw_ref[...] = total_ref[...].astype(BF16)


def plane_grad_kernel(sides, ready, at_ref, *refs):
    count = len(sides)
    lefts, rights, refs = refs[:count], refs[count : 2 * count], refs[2 * count :]
    ready_refs, out_refs = refs[:ready], refs[ready:]
    shard = out_refs[0].shape[1]
    for bit, out_ref in enumerate(out_refs):
        here = slot_at(at_ref[0], 2 * pl.program_id(0) + bit, shard)
        column = 0
        for left, right, side in zip(lefts, rights, sides):
            width = right.shape[1 - side]
            out_ref[0, :, column : column + width] = contract(
                left[:, here], right[...], 0, side
            ).astype(BF16)
            column += width
        for ready_ref in ready_refs:
            width = ready_ref.shape[1]
            out_ref[0, :, column : column + width] = ready_ref[here]
            column += width


def mlp_grad_kernel(two_ref, pre_ref, low_ref, active_ref, out_ref):
    width = pre_ref.shape[1]
    out_ref[:, :width] = contract(two_ref[...], pre_ref[...], 0, 0).astype(BF16)
    out_ref[:, width:] = contract(low_ref[...], active_ref[...], 0, 0).astype(BF16)


def halve_kernel(keep_ref, got_ref, *out_refs):
    size = out_refs[0].shape[0]
    for i, out_ref in enumerate(out_refs):
        for j in range(size):
            total = keep_ref[i * size + j].astype(F32) + got_ref[i * size + j].astype(F32)
            out_ref[j] = total.astype(BF16)


def rank_split_kernel(count, at_ref, *refs):
    part_refs, own_ref, send_refs = refs[:count], refs[count], refs[count + 1 :]
    kinds, _, columns = own_ref.shape
    for i in range(kinds):
        for k, out_ref in enumerate((own_ref, *send_refs)):
            first = (i * (len(send_refs) + 1) + (at_ref[0] ^ k)) * columns
            here = pl.ds(pl.multiple_of(first, columns), columns)
            total = sum(part_ref[0, :, here].astype(F32) for part_ref in part_refs)
            out_ref[i] = total.astype(out_ref.dtype)


def input_grad_kernel(stacked_ref, proj_ref, first_ref, out_ref, all_ref):
    @pl.when(pl.program_id(0) == 0)
    def _():
        heads = stacked_ref.shape[0]
        for j in range(3):
            rows = [stacked_ref[h, j * HEAD : (j + 1) * HEAD] for h in range(heads)]
            all_ref[:, j * heads * HEAD : (j + 1) * heads * HEAD] = jnp.concatenate(rows, 0).T

    out_ref[...] = (first_ref[...] + contract(all_ref[...], proj_ref[...], 1, 1)).astype(BF16)


def by_first(shape, lead=1):
    return pl.BlockSpec((lead,) + shape[1:], lambda s: (s,) + (0,) * (len(shape) - 1))


def whole(shape):
    return pl.BlockSpec(shape, lambda s: (0,) * len(shape))


def shaped(shape, dtype):
    return jax.ShapeDtypeStruct(shape, dtype)


def call(kernel, seqs, in_specs, out_specs, out_shape, operands, cost, scratch=()):
    flops, transcendentals = cost
    moved = sum(o.size * o.dtype.itemsize for o in operands)
    moved += sum(o.size * o.dtype.itemsize for o in out_shape)
    return pl.pallas_call(
        kernel,
        grid=(seqs,),
        in_specs=in_specs,
        out_specs=out_specs,
        out_shape=out_shape,
        scratch_shapes=scratch,
        compiler_params=pltpu.CompilerParams(
            dimension_semantics=("arbitrary",), vmem_limit_bytes=VMEM_BYTES
        ),
        cost_estimate=pl.CostEstimate(
            flops=flops // COST_SHARE,
            bytes_accessed=moved // COST_SHARE,
            transcendentals=transcendentals // COST_SHARE,
        ),
    )(*operands)


def one_step(kernel, out, *operands, flops=0):
    specs = [IN_SMEM if v.dtype == jnp.int32 else whole(v.shape) for v in operands]
    return call(kernel, 1, specs, [whole(out)], [shaped(out, BF16)], operands, (flops, 0))[0]


def self_forward(at, slots, weights, query_bias, pair_bias, chunk_shape):
    seqs, block, width = slots[0].shape
    length = block * len(slots)
    halves = chunk_shape[0] // seqs
    query, pair, lse = (seqs, HEAD, length), (seqs, length, 2 * HEAD), (seqs, 1, length)
    return call(
        self_forward_kernel,
        seqs,
        [IN_SMEM]
        + [by_first(x.shape) for x in slots]
        + [whole(weights.shape), whole(query_bias.shape), whole(pair_bias.shape)],
        [by_first(query), by_first(pair), by_first(chunk_shape, halves), by_first(lse)],
        [shaped(query, BF16), shaped(pair, BF16), shaped(chunk_shape, BF16), shaped(lse, F32)],
        [at, *slots, weights, query_bias, pair_bias],
        (seqs * length * (2 * width * 3 * HEAD + 8 * length * HEAD), seqs * length * length),
    )


def cross_forward(query, pairs):
    seqs = pairs[0].shape[0]
    halves, blocks, features, part = query.shape
    halves //= seqs
    length = halves * blocks * part
    keys = sum(p.shape[1] for p in pairs)
    out = (halves * seqs, blocks, features + STAT_ROWS, part)
    return call(
        cross_forward_kernel,
        seqs,
        [by_first(query.shape, halves)] + [by_first(p.shape) for p in pairs],
        [by_first(out, halves)],
        [shaped(out, BF16)],
        [query, *pairs],
        (seqs * length * keys * 8 * features, seqs * length * keys * features // HEAD),
    )[0]


def cross_backward(query, grad, pairs):
    seqs = pairs[0].shape[0]
    halves, blocks, features, part = query.shape
    halves //= seqs
    length = halves * blocks * part
    keys = sum(p.shape[1] for p in pairs)
    return call(
        cross_backward_kernel,
        seqs,
        [by_first(query.shape, halves), by_first(grad.shape, halves)] + [by_first(p.shape) for p in pairs],
        [by_first(p.shape) for p in pairs] + [by_first(query.shape, halves)],
        [shaped(p.shape, BF16) for p in pairs] + [shaped(query.shape, BF16)],
        [query, grad, *pairs],
        (seqs * length * keys * 20 * features, seqs * length * keys * features // HEAD),
    )


def self_backward(at, slots, query, pair, mixed, grad, lse):
    seqs, block, width = slots[0].shape
    length = block * len(slots)
    halves = mixed.shape[0] // seqs
    chunk = by_first(mixed.shape, halves)
    out = mixed.shape[:2] + (3 * HEAD, mixed.shape[3])
    return call(
        self_backward_kernel,
        seqs,
        [IN_SMEM]
        + [by_first(x.shape) for x in slots]
        + [by_first(query.shape), by_first(pair.shape), chunk, chunk, by_first(lse.shape)],
        [by_first(out, halves), whole((3 * HEAD, width)), whole((3 * HEAD, 1))],
        [shaped(out, BF16), shaped((3 * HEAD, width), F32), shaped((3 * HEAD, 1), F32)],
        [at, *slots, query, pair, mixed, grad, lse],
        (seqs * length * (2 * width * 3 * HEAD + 20 * length * HEAD), seqs * length * length),
        [pltpu.VMEM((2 * HEAD, length), F32), pltpu.VMEM((3 * HEAD, length), BF16)],
    )


def encoder_pairs(at, rows, weights, bias, count):
    length, width = rows.shape
    tile = min(ROW_TILE, length)
    pair = (length, weights.shape[1] // count)
    return call(
        encoder_kernel,
        length // tile,
        [IN_SMEM, by_first(rows.shape, tile), whole(weights.shape), whole(bias.shape)],
        [by_first(pair, tile)] * count,
        [shaped(pair, BF16)] * count,
        [at, rows, weights, bias],
        (2 * length * width * weights.shape[1], 0),
        [pltpu.VMEM((tile, weights.shape[1]), BF16)],
    )


def encoder_back(at, rows, weights, grads):
    length, width = rows.shape
    tile = min(ROW_TILE, length)
    columns = weights.shape[1]
    return call(
        encoder_back_kernel,
        length // tile,
        [IN_SMEM, by_first(rows.shape, tile), whole(weights.shape)]
        + [by_first(g.shape, tile) for g in grads],
        [by_first(rows.shape, tile), whole((1, columns)), whole(weights.shape)],
        [shaped(rows.shape, BF16), shaped((1, columns), F32), shaped(weights.shape, BF16)],
        [at, rows, weights, *grads],
        (4 * length * width * columns, 0),
        [pltpu.VMEM(weights.shape, F32), pltpu.VMEM((tile, columns), BF16)],
    )


def mlp_grads(two, pre_low, low, active):
    count, width = two.shape
    columns = pre_low.shape[1]
    tile = 256
    strip = pl.BlockSpec((count, tile), lambda i: (0, i))
    out = (width, 2 * columns)
    return call(
        mlp_grad_kernel,
        width // tile,
        [strip, whole(pre_low.shape), strip, whole(active.shape)],
        [by_first(out, tile)],
        [shaped(out, BF16)],
        [two, pre_low, low, active],
        (4 * count * width * columns, 0),
    )[0]


def halve(keep, got, groups):
    count, rows, columns = keep.shape
    tile = min(512, columns)
    stack = pl.BlockSpec((count, rows, tile), lambda i: (0, 0, i))
    strip = pl.BlockSpec((count // groups, rows, tile), lambda i: (0, 0, i))
    return call(
        halve_kernel,
        columns // tile,
        [stack, stack],
        [strip] * groups,
        [shaped((count // groups, rows, columns), BF16)] * groups,
        [keep, got],
        (keep.size, 0),
    )


def rank_split(at, parts, kinds, ranks):
    _, rows, columns = parts[0].shape
    out = (kinds, rows, columns // kinds // ranks)
    return call(
        functools.partial(rank_split_kernel, len(parts)),
        1,
        [IN_SMEM] + [whole(v.shape) for v in parts],
        [whole(out)] * ranks,
        [shaped(out, F32)] + [shaped(out, BF16)] * (ranks - 1),
        [at, *parts],
        (len(parts) * parts[0].size, 0),
    )


def input_grads(stacked, proj, first):
    part, width = first.shape
    tile = 256
    strip = pl.BlockSpec((part, tile), lambda i: (0, i))
    return call(
        input_grad_kernel,
        width // tile,
        [whole(stacked.shape), by_first(proj.shape, tile), strip],
        [strip],
        [shaped(first.shape, BF16)],
        [stacked, proj, first],
        (2 * part * proj.size, 0),
        [pltpu.VMEM((part, proj.shape[1]), BF16)],
    )[0]


def plane_grads(at, items, ready, shard):
    lefts, rights, sides = zip(*items) if items else ((), (), ())
    width = (lefts[0].T if items else ready[0]).shape[0]
    columns = sum(right.shape[1 - side] for right, side in zip(rights, sides))
    columns += sum(v.shape[1] for v in ready)
    out = (width // shard // 2, shard, columns)
    flops = sum(2 * width * right.size for right in rights)
    return call(
        functools.partial(plane_grad_kernel, sides, len(ready)),
        out[0],
        [IN_SMEM] + [whole(v.shape) for v in (*lefts, *rights, *ready)],
        [by_first(out)] * 2,
        [shaped(out, BF16)] * 2,
        [at, *lefts, *rights, *ready],
        (flops, 0),
    )


def body(
    hidden_in,
    encoder_states,
    out_cotangent,
    self_proj,
    self_qv_bias,
    self_out_proj,
    cross_q_proj,
    cross_kv_proj,
    cross_qv_bias,
    cross_out_proj,
    up_proj,
    up_bias,
    down_proj,
    norm_gain,
    norm_bias,
    out_bias,
):
    blocks, ranks = lax.axis_size("ctx"), lax.axis_size("tp")
    plane = lax.axis_size("dp") * blocks
    own_ctx, own_tp = lax.axis_index("ctx"), lax.axis_index("tp")
    seqs, block, width = hidden_in.shape
    rows = seqs * block
    part = rows // ranks
    shard = width // plane
    heads_here = self_qv_bias.shape[0]
    local_width = heads_here * HEAD
    all_heads = heads_here * ranks
    enc_len = encoder_states.shape[1]
    hidden = up_proj.shape[1]
    slots = range(blocks)

    def ctx_swap(values, k):
        return lax.ppermute(values, "ctx", [(i, i ^ k) for i in slots])

    def tp_swap(values, k):
        return lax.ppermute(values, "tp", [(i, i ^ k) for i in range(ranks)])

    def exchange(values):
        return lax.all_to_all(values, HEADS, split_axis=0, concat_axis=0, tiled=True)

    def own_rows(values):
        return lax.dynamic_slice_in_dim(values.reshape(rows, width), own_tp * part, part, 0)

    def in_swap_order(values, axis):
        return [lax.dynamic_index_in_dim(values, own_ctx ^ k, axis, keepdims=False) for k in slots]

    cores = 2
    pair_heads = heads_here // cores
    pair_rows = pair_heads * HEAD
    core_at = lax.rem(own_ctx, cores).reshape(1)
    ctx_at, plane_at = own_ctx.reshape(1), (lax.axis_index("dp") * blocks + own_ctx).reshape(1)

    def plane_swap(values, k):
        return lax.ppermute(values, PLANE, [(i, i ^ k) for i in range(plane)])

    def sum_begin(items, ready=()):
        if plane == 8:
            keep, send = plane_grads(plane_at, items, ready, shard)
            return (keep, plane_swap(send, 1))
        sums = [contract(left, right, 0, side).astype(BF16) for left, right, side in items]
        sums = jnp.concatenate([*sums, *ready], 1)
        return (lax.psum_scatter(sums, PLANE, scatter_dimension=0, tiled=True),)

    def sum_near(state, groups):
        return halve(*state, groups) if plane == 8 else state

    def sum_far(parts):
        return [plane_swap(part, 2 * j) if j else part for j, part in enumerate(parts)]

    def sum_dp(parts):
        return [parts[0], plane_swap(parts[1], 4)] if plane == 8 else parts

    def sum_x(parts):
        if plane != 8:
            return parts
        own, other = (parts[0][j].astype(F32) + parts[1][j].astype(F32) for j in range(2))
        return [own, plane_swap(other.astype(BF16), 2)]

    def sum_end(parts):
        return sum(part.astype(F32).reshape(shard, -1) for part in parts)

    def whole_on_ranks(values):
        values = jnp.broadcast_to(values[None], (ranks,) + values.shape)
        return lax.all_to_all(values, "tp", split_axis=0, concat_axis=0, tiled=True)

    bias_part = 2 * HEAD // plane
    count = heads_here * bias_part
    core_tokens, x_tokens = ctx_swap(hidden_in, 1), ctx_swap(hidden_in, 2)
    rank_at = own_tp.reshape(1)

    def rank_parts(values):
        return [values] + [tp_swap(values, k) for k in range(1, ranks)]

    def from_ranks(parts):
        out = (shard, parts[0].shape[0] * width)
        return one_step(rank_kernel, out, rank_at, *parts)

    square = one_step(
        square_pack_kernel, (3, shard, local_width), self_out_proj, cross_q_proj, cross_out_proj
    )
    square = rank_parts(square)
    square, first_proj, core_tokens, x_tokens = together(square, self_proj, core_tokens, x_tokens)
    vectors = jnp.concatenate([norm_gain, norm_bias, out_bias])
    small = jnp.concatenate([v.reshape(-1) for v in (self_qv_bias, cross_qv_bias, up_bias)])
    small = jnp.concatenate([vectors, small.reshape(-1, shard)])
    small = jnp.pad(small, ((0, 16 - small.shape[0]), (0, 0)))
    first = one_step(
        first_pack_kernel, (plane, 3 * HEAD + small.shape[0], shard), first_proj, small
    )
    first = lax.all_to_all(first, PLANE, split_axis=0, concat_axis=0, tiled=True)
    kv_weights = cross_kv_proj.reshape(2, shard, heads_here, HEAD).transpose(1, 2, 0, 3)
    kv_weights = lax.all_gather(
        kv_weights.reshape(shard, heads_here * 2 * HEAD), PLANE, axis=0, tiled=True
    )

    core_tokens, x_tokens, first, up_proj, down_proj = together(
        core_tokens, x_tokens, first, up_proj, down_proj
    )

    square = lax.all_gather(from_ranks(square), PLANE, axis=0, tiled=True)
    mlp = one_step(mlp_pack_kernel, (shard, 2 * hidden), up_proj, down_proj)
    mlp_other = tp_swap(mlp, 2)
    x_slots = [hidden_in, core_tokens, x_tokens, ctx_swap(x_tokens, 1)]
    own_head = first[:, : 3 * HEAD].swapaxes(0, 1).reshape(3 * HEAD, width)
    small = first[:, 3 * HEAD :]
    vectors = small[:, :9].swapaxes(0, 1).reshape(9, width).astype(F32)
    gains, shifts, branch_bias = vectors[:3], vectors[3:6], vectors[6:]
    small = small[:, 9:].reshape(plane, -1)

    def head_bias(values):
        values = values.reshape(plane, heads_here, bias_part).swapaxes(0, 1)
        return values.reshape(heads_here, 2 * HEAD).astype(F32)

    self_bias = head_bias(small[:, :count])
    cross_bias = head_bias(small[:, count : 2 * count])
    up_vector = small[:, 2 * count : 2 * count + up_bias.size]
    up_vector = up_vector.reshape((plane,) + up_bias.shape).swapaxes(0, 1).reshape(1, hidden)
    enc_rows = encoder_states.reshape(-1, width)
    value_bias = jnp.concatenate([jnp.zeros((heads_here, HEAD), F32), cross_bias[:, HEAD:]], 1)
    pairs = encoder_pairs(core_at, enc_rows, kv_weights, value_bias.reshape(1, -1), cores)
    x_slots, pairs = together(x_slots, pairs)
    pairs = [
        (ctx_swap(pair, k) if k else pair).reshape(seqs, enc_len, 2 * pair_rows)
        for k, pair in enumerate(pairs)
    ]

    def to_pairs(values):
        values = values.reshape(ranks, 1, cores, -1, part)
        values = jnp.broadcast_to(values, (ranks, blocks // cores) + values.shape[2:])
        return exchange(values.reshape(all_heads, -1, part)).reshape(ranks, blocks, -1, part)

    def from_pairs(values):
        values = exchange(values.reshape(all_heads, -1, part))
        return values.reshape(ranks, blocks // cores, cores, -1, part)
    head_row = lax.dynamic_index_in_dim(self_bias, own_ctx, 0, keepdims=False)
    query_column = head_row[:HEAD].reshape(HEAD, 1)
    pair_row = jnp.concatenate([jnp.zeros((HEAD,), F32), head_row[HEAD:]]).reshape(1, 2 * HEAD)
    chunk_shape = (ranks, blocks, HEAD, part)
    self_query, self_pair, self_mixed, self_lse = self_forward(
        ctx_at, x_slots, own_head, query_column, pair_row, chunk_shape
    )
    tokens_f = own_rows(hidden_in).astype(F32)
    mixed_t = exchange(self_mixed.reshape(all_heads, HEAD, part)).reshape(width, part)
    mixed_t, square, mlp_other, self_proj, pairs, up_vector = together(
        mixed_t, square, mlp_other, self_proj, pairs, up_vector
    )
    up_vector = jnp.concatenate([up_vector, tp_swap(up_vector, 2)], 1).astype(F32)
    self_out_all, cross_q_all, cross_out_all = (square[:, i * width : (i + 1) * width] for i in range(3))
    mlp = jnp.concatenate(
        [mlp[:, :hidden], mlp_other[:, :hidden], mlp[:, hidden:], mlp_other[:, hidden:]], 1
    )
    mlp = lax.all_gather(mlp, PLANE, axis=0, tiled=True)
    up_all, down_all = mlp[:, : 2 * hidden], mlp[:, 2 * hidden :]
    rank_proj = rank_parts(self_proj)
    attn_branch = contract(mixed_t, self_out_all, 0, 1) + branch_bias[0]
    first_out, first_normed, first_inv = norm_forward(tokens_f + attn_branch, gains[0], shifts[0])
    first_low = first_out.astype(BF16)
    cross_query = contract(cross_q_all, first_low, 0, 1).astype(BF16)
    cross_query = to_pairs(cross_query)
    cross_rows = lax.dynamic_slice_in_dim(cross_bias[:, :HEAD], core_at[0] * pair_heads, pair_heads, 0)
    cross_query = (
        (cross_query.astype(F32) + cross_rows.reshape(pair_rows, 1)).astype(BF16) * HEAD**-0.5
    )
    cross_mixed = cross_forward(cross_query, pairs)
    cross_mixed, rank_proj = together(cross_mixed, rank_proj)
    proj = lax.all_gather(from_ranks(rank_proj), PLANE, axis=0, tiled=True)
    halves = from_pairs(cross_mixed)
    stats = halves[:, :, :, pair_rows : pair_rows + 3 * pair_heads].astype(F32)
    stats = jnp.sum(stats.reshape(ranks, blocks // cores, cores, pair_heads, 3, part), 4, keepdims=True)
    top = jnp.max(stats, 1, keepdims=True)
    shares = jnp.exp(stats - top)
    total = jnp.sum(shares, 1, keepdims=True)
    halves = halves[:, :, :, :pair_rows].reshape(ranks, blocks // cores, cores, pair_heads, HEAD, part)
    cross_t = jnp.sum(halves.astype(F32) * (shares / total), 1).astype(BF16).reshape(width, part)
    cross_lse = (top + jnp.log(total)).reshape(all_heads, part)
    cross_branch = contract(cross_t, cross_out_all, 0, 1) + branch_bias[1]
    second_out, second_normed, second_inv = norm_forward(
        first_low.astype(F32) + cross_branch, gains[1], shifts[1]
    )
    second_low = second_out.astype(BF16)

    two = jnp.concatenate([second_low, tp_swap(second_low, 1)])
    pre_act = contract(two, up_all, 1, 0) + up_vector
    active = exact_gelu(pre_act).astype(BF16)
    mlp_part = contract(active, down_all, 1, 1)
    mlp_branch = (
        mlp_part[:part] + tp_swap(mlp_part[part:].astype(BF16), 1).astype(F32) + branch_bias[2]
    )
    third_out, third_normed, third_inv = norm_forward(
        second_low.astype(F32) + mlp_branch, gains[2], shifts[2]
    )
    hidden_out = third_out.astype(BF16)
    rms = jnp.stack([root_mean(attn_branch), root_mean(cross_branch), root_mean(mlp_branch)])

    out_grad = own_rows(out_cotangent).astype(F32)
    third_grad, gain_two, shift_two = norm_backward(out_grad, third_normed, third_inv, gains[2])
    mlp_bias_grad = jnp.sum(third_grad, 0)
    mlp_low = third_grad.astype(BF16)
    mlp_low = jnp.concatenate([mlp_low, tp_swap(mlp_low, 1)])
    active_grad = contract(mlp_low, down_all, 1, 0)
    pre_low = jax.vjp(exact_gelu, pre_act)[1](active_grad)[0].astype(BF16)
    mlp_grad = mlp_grads(two, pre_low, mlp_low, active)
    back_part = contract(pre_low, up_all, 1, 1)
    mlp_grad = lax.psum_scatter(mlp_grad, PLANE, scatter_dimension=0, tiled=True)
    back = back_part[:part] + tp_swap(back_part[part:].astype(BF16), 1).astype(F32)
    up_bias_grad = jnp.sum(pre_low.astype(F32), 0).reshape(2, hidden)
    second_grad, gain_one, shift_one = norm_backward(
        third_grad + back, second_normed, second_inv, gains[1]
    )
    cross_bias_sum = jnp.sum(second_grad, 0)
    second_grad_low = second_grad.astype(BF16)
    mix_grad = contract(cross_out_all, second_grad_low, 0, 1).astype(BF16)
    inner = jnp.sum(
        mix_grad.reshape(all_heads, HEAD, part).astype(F32)
        * cross_t.reshape(all_heads, HEAD, part).astype(F32),
        1,
    )
    def spread_rows(values):
        rows = []
        for _ in range(3):
            rows.append(lax.reduce_precision(values, 8, 7))
            values = values - rows[-1]
        return [row.astype(BF16) for row in rows]

    stats = jnp.stack([*spread_rows(cross_lse), *spread_rows(inner)], 1).reshape(ranks * cores, -1, part)
    stats = jnp.pad(stats, ((0, 0), (0, STAT_ROWS - stats.shape[1]), (0, 0)))
    mix_grad = to_pairs(jnp.concatenate([mix_grad.reshape(ranks * cores, pair_rows, part), stats], 1))
    mix_grad, hidden_out, proj = together(mix_grad, hidden_out, proj)
    hidden_out = whole_on_ranks(hidden_out)
    *pair_grads, query_grad = cross_backward(cross_query, mix_grad, pairs)
    query_grad, hidden_out = together(query_grad, hidden_out)
    pair_grads = [
        (ctx_swap(g, k) if k else g).reshape(-1, 2 * pair_rows) for k, g in enumerate(pair_grads)
    ]
    enc_part, value_sum, kv_grad = encoder_back(core_at, enc_rows, kv_weights, pair_grads)
    query_grad = from_pairs(query_grad)
    query_grad, enc_part, value_sum, kv_grad, mlp_grad = together(
        query_grad, enc_part, value_sum, kv_grad, mlp_grad
    )
    encoder_grad = lax.psum_scatter(
        enc_part.reshape(seqs, enc_len, width), "tp", scatter_dimension=2, tiled=True
    )
    value_sum = value_sum.reshape(heads_here, 2 * HEAD)[:, HEAD:]
    query_grad = jnp.sum(query_grad.astype(F32), 1).astype(BF16).reshape(width, part)
    query_sum = jnp.sum(query_grad.astype(F32), 1)

    first_grad, gain_zero, shift_zero = norm_backward(
        second_grad + contract(query_grad, cross_q_all, 0, 1), first_normed, first_inv, gains[0]
    )
    attn_bias_sum = jnp.sum(first_grad, 0)
    first_grad_low = first_grad.astype(BF16)
    squares = [(first_grad_low, mixed_t, 1), (first_low, query_grad, 1), (second_grad_low, cross_t, 1)]
    square_grad = sum_begin(squares)

    self_mix_grad = contract(self_out_all, first_grad_low, 0, 1).astype(BF16)
    self_mix_grad = exchange(self_mix_grad.reshape(all_heads, HEAD, part)).reshape(chunk_shape)
    kv_grad = sum_begin((), [kv_grad])
    square_grad, kv_grad = sum_near(square_grad, 4), sum_near(kv_grad, 2)
    self_mix_grad, square_grad, kv_grad = together(self_mix_grad, square_grad, kv_grad)
    square_grad, kv_grad = sum_far(square_grad), sum_dp(kv_grad)
    stacked, head_grad, head_sum = self_backward(
        ctx_at, x_slots, self_query, self_pair, self_mixed, self_mix_grad, self_lse
    )
    stacked, head_grad, square_grad, kv_grad, mlp_grad = together(
        stacked, head_grad, square_grad, kv_grad, mlp_grad
    )
    mlp_grad = mlp_grad.reshape(shard, 2, 2, hidden)
    mlp_grad = [mlp_grad[:, :, 0], mlp_grad[:, :, 1]]
    kv_grad = sum_x(kv_grad)
    stacked = exchange(stacked.reshape(all_heads, 3 * HEAD, part))
    stacked, head_grad, square_grad, kv_grad, mlp_grad, encoder_grad = together(
        stacked, head_grad, square_grad, kv_grad, mlp_grad, encoder_grad
    )
    mlp_grad = [mlp_grad[0], tp_swap(mlp_grad[1], 2)]
    if plane != 8:
        square_grad = [sum_end(square_grad).astype(BF16)[None]]
    square_grad = rank_split(rank_at, square_grad, 3, ranks)
    square_grad = [tp_swap(v, k) if k else v for k, v in enumerate(square_grad)]
    input_grad = input_grads(stacked, proj, first_grad)
    input_grad = lax.all_gather(input_grad, "tp", axis=0, tiled=True)

    head_grad = head_grad.reshape(3 * HEAD, plane, shard).swapaxes(0, 1)
    head_sum = head_sum.reshape(3, HEAD)
    head_sum = jnp.concatenate([head_sum[0], head_sum[2]]).reshape(plane, bias_part, 1)
    head_sum = jnp.pad(head_sum, ((0, 0), (0, 16 - bias_part), (0, 0)))
    def pieces(values):
        return values.reshape(-1, plane, values.shape[-1] // plane).swapaxes(0, 1).reshape(plane, -1)

    norm_sums = jnp.stack(
        [gain_zero, gain_one, gain_two, shift_zero, shift_one, shift_two]
        + [attn_bias_sum, cross_bias_sum, mlp_bias_grad]
    )
    up_cols = up_bias.shape[1]
    up_sums = pieces(up_bias_grad.reshape(-1, plane * up_cols))
    query_sums = pieces(jnp.pad(query_sum.reshape(all_heads, HEAD), ((0, 0), (0, HEAD))))
    value_sums = pieces(jnp.pad(value_sum, ((0, 0), (HEAD, 0))))
    sums = jnp.concatenate([pieces(norm_sums), up_sums, query_sums, value_sums], 1)
    sums = jnp.pad(sums, ((0, 0), (0, 16 * shard - sums.shape[1]))).reshape(plane, 16, shard)
    head_grad = jnp.concatenate(
        [head_grad, jnp.broadcast_to(head_sum, (plane, 16, shard)), sums], 1
    ).astype(BF16)
    head_grad = lax.all_to_all(head_grad, PLANE, split_axis=0, concat_axis=0, tiled=True)
    head_grad = head_grad.reshape(-1, blocks, 3 * HEAD + 32, shard).astype(F32)
    kv_grad = sum_end(kv_grad).reshape(shard, heads_here, 2, HEAD)
    kv_grad = kv_grad.transpose(2, 0, 1, 3).reshape(2, shard, local_width)
    sums = jnp.sum(head_grad[:, :, 3 * HEAD + 16 :], (0, 1))
    head_grad = jnp.sum(head_grad[:, :, : 3 * HEAD + 16], 0)
    self_proj_out = head_grad[:, : 3 * HEAD].reshape(blocks, 3, HEAD, shard)
    self_proj_out = self_proj_out.transpose(1, 3, 0, 2).reshape(3, shard, local_width)
    self_bias_out = head_grad[:, 3 * HEAD : 3 * HEAD + bias_part, 0]
    norm_out, sums = sums[:9].reshape(-1), sums[9:].reshape(-1)
    sums = jnp.concatenate([norm_out, sums[: 2 * up_bias.size + ranks * count + count], rms.reshape(-1)])
    ends = [0, norm_out.size]
    for size in (up_bias.size, up_bias.size, ranks * count, count, rms.size):
        ends.append(ends[-1] + size)
    sums = jnp.pad(sums, (0, 16 * 256 - sums.size)).reshape(16, 256).astype(BF16)

    sums, square_grad = together(sums, square_grad)
    mlp_grad = mlp_grad[0].astype(F32) + mlp_grad[1].astype(F32)
    up_out, down_out = mlp_grad[:, 0], mlp_grad[:, 1].T
    square_grad = sum(v.astype(F32) for v in square_grad)
    self_out_out, cross_q_out, cross_out_out = square_grad[0].T, square_grad[1], square_grad[2].T
    sums, input_grad = together(whole_on_ranks(sums), input_grad)
    input_grad, encoder_grad = input_grad.astype(F32), encoder_grad.astype(F32)
    sums = sums.astype(F32).reshape(ranks, -1)
    norm_out, up_own, up_other, query_sums, value_sums, rms = (
        sums[:, i:j] for i, j in zip(ends, ends[1:])
    )
    norm_out = jnp.sum(norm_out, 0).reshape(9, shard)

    def of_rank(values, at):
        return lax.dynamic_index_in_dim(values, at, 0, False)

    up_bias_out = (of_rank(up_own, own_tp) + of_rank(up_other, own_tp ^ 2)).reshape(up_bias.shape)
    cross_bias_out = of_rank(jnp.sum(query_sums, 0).reshape(ranks, count), own_tp)
    cross_bias_out = (cross_bias_out + of_rank(value_sums, own_tp)).reshape(heads_here, bias_part)
    rms = rms.reshape(ranks, 3, part).swapaxes(0, 1).reshape(3, rows)
    rms = jnp.concatenate([root_mean(hidden_in.reshape(rows, width).astype(F32))[None], rms])
    return (
        hidden_out.reshape(seqs, block, width),
        input_grad.reshape(seqs, block, width),
        encoder_grad,
        self_proj_out,
        self_bias_out,
        self_out_out,
        cross_q_out,
        kv_grad,
        cross_bias_out,
        cross_out_out,
        up_out,
        up_bias_out,
        down_out,
        norm_out[:3],
        norm_out[3:6],
        norm_out[6:],
        rms.reshape(4, seqs, block),
    )


def solution(mesh):
    rows, heads, columns = P("dp", "ctx", None), P("tp", PLANE), P(PLANE, "tp")
    stacked, vectors = P(None, PLANE, "tp"), P(None, PLANE)
    weights = (
        stacked, heads, heads, columns, stacked, heads, heads, columns, heads, heads,
        vectors, vectors, vectors,
    )
    return jax.shard_map(
        body,
        mesh=mesh,
        in_specs=(rows, rows, rows) + weights,
        out_specs=(rows, rows, P("dp", "ctx", "tp")) + weights + (P(None, "dp", "ctx"),),
        check_vma=False,
    )
```

```python
import functools

import jax
import jax.numpy as jnp
from jax import lax
from jax.experimental import pallas as pl
from jax.experimental.pallas import tpu as pltpu
from jax.sharding import PartitionSpec as P

EPSILON = 1e-05
HEAD = 64
KEY_TILE = 512
STAT_ROWS = 16
ROW_TILE = 512
COST_SHARE = 10
VMEM_BYTES = 50 * 1024 * 1024
PLANE = ("dp", "ctx")
HEADS = ("tp", "ctx")
F32 = jnp.float32
BF16 = jnp.bfloat16
IN_SMEM = pl.BlockSpec(memory_space=pltpu.SMEM)


def contract(left, right, left_dim, right_dim):
    return lax.dot_general(
        left, right, (((left_dim,), (right_dim,)), ((), ())), preferred_element_type=F32
    )


def together(*values):
    return lax.optimization_barrier(values)


def norm_forward(values, norm_gain, norm_shift):
    row_mean = jnp.mean(values, -1, keepdims=True)
    centered = values - row_mean
    inv_std = lax.rsqrt(jnp.mean(centered * centered, -1, keepdims=True) + EPSILON)
    normed = centered * inv_std
    return (normed * norm_gain + norm_shift, normed, inv_std)


def norm_backward(gradient, normed, inv_std, norm_gain):
    gain_grad = jnp.sum(gradient * normed, 0)
    shift_grad = jnp.sum(gradient, 0)
    scaled = gradient * norm_gain
    input_part = inv_std * (
        scaled
        - jnp.mean(scaled, -1, keepdims=True)
        - normed * jnp.mean(scaled * normed, -1, keepdims=True)
    )
    return (input_part, gain_grad, shift_grad)


def root_mean(values):
    return jnp.sqrt(jnp.mean(values * values, -1))


def exact_gelu(values):
    return jax.nn.gelu(values, approximate=False)


def with_zeros_below(values):
    return jnp.concatenate([values, jnp.zeros_like(values)], 0)


def with_zeros_above(values):
    return jnp.concatenate([jnp.zeros_like(values), values], 0)


def gather_chunks(ref):
    halves, blocks = ref.shape[:2]
    return jnp.concatenate([ref[h, b] for h in range(halves) for b in range(blocks)], 1)


def slot_at(own, k, size):
    return pl.ds(pl.multiple_of((own ^ k) * size, size), size)


def first_pack_kernel(proj_ref, small_ref, out_ref):
    blocks = proj_ref.shape[2] // HEAD
    for j in range(3):
        turned = proj_ref[j].T
        for e in range(out_ref.shape[0]):
            head = e % blocks * HEAD
            out_ref[e, j * HEAD : (j + 1) * HEAD] = turned[head : head + HEAD]
    for e in range(out_ref.shape[0]):
        out_ref[e, 3 * HEAD :] = small_ref[...]


def square_pack_kernel(self_out_ref, cross_q_ref, cross_out_ref, out_ref):
    out_ref[0] = self_out_ref[...].T
    out_ref[1] = cross_q_ref[...]
    out_ref[2] = cross_out_ref[...].T


def mlp_pack_kernel(up_ref, down_ref, out_ref):
    width = up_ref.shape[1]
    out_ref[:, :width] = up_ref[...]
    out_ref[:, width:] = down_ref[...].T


def rank_kernel(at_ref, *refs):
    part_refs, out_ref = refs[:-1], refs[-1]
    for k, part_ref in enumerate(part_refs):
        count, _, columns = part_ref.shape
        for i in range(count):
            first = (i * len(part_refs) + (at_ref[0] ^ k)) * columns
            out_ref[:, pl.ds(pl.multiple_of(first, columns), columns)] = part_ref[i]


def self_forward_kernel(at_ref, *refs):
    x_refs, (w_ref, bq_ref, bv_ref, q_ref, kv_ref, o_ref, lse_ref) = refs[:-7], refs[-7:]
    weights = w_ref[...]
    halves, blocks, _, part = o_ref.shape
    block = halves * part
    scale = HEAD**-0.5
    for k, x_ref in enumerate(x_refs):
        here = slot_at(at_ref[0], k, block)
        tokens = x_ref[0]
        q_ref[0, :, here] = (contract(weights[:HEAD], tokens, 1, 1) + bq_ref[...]).astype(BF16) * scale
        kv_ref[0, here] = (contract(tokens, weights[HEAD:], 1, 1) + bv_ref[...]).astype(BF16)
    for i in range(blocks):
        keys = kv_ref[0, : (i + 1) * block]
        query = q_ref[0, :, i * block : (i + 1) * block]
        scores = contract(keys, with_zeros_below(query), 1, 0)
        top = jnp.max(scores, 0, keepdims=True)
        weight = jnp.exp(scores - top)
        total = jnp.sum(weight, 0, keepdims=True)
        mixed = contract(keys, weight.astype(BF16), 0, 0)[HEAD:]
        out = (mixed / total).astype(BF16)
        for h in range(halves):
            o_ref[h, i] = out[:, h * part : (h + 1) * part]
        lse_ref[0, :, i * block : (i + 1) * block] = top + jnp.log(total)


def spread(values):
    rows = []
    for _ in range(3):
        rows.append(values.astype(BF16).astype(F32))
        values = values - rows[-1]
    return rows


def gathered(rows, at):
    return sum(rows[at + i : at + i + 1] for i in range(3))


def cross_forward_kernel(q_ref, *refs):
    kv_refs, o_ref = refs[:-1], refs[-1]
    halves, blocks, features, part = q_ref.shape
    queries = gather_chunks(q_ref)
    heads = features // HEAD
    outs, stats = [], []
    for n in range(heads):
        query = with_zeros_below(queries[n * HEAD : (n + 1) * HEAD])
        lanes = slice(n * 2 * HEAD, (n + 1) * 2 * HEAD)
        top = total = mixed = None
        for kv_ref in kv_refs:
            for start in range(0, kv_ref.shape[1], KEY_TILE):
                pair = kv_ref[0, start : start + KEY_TILE, lanes]
                scores = contract(pair, query, 1, 0)
                tile_top = jnp.max(scores, 0, keepdims=True)
                new_top = tile_top if top is None else jnp.maximum(top, tile_top)
                weight = jnp.exp(scores - new_top)
                tile_total = jnp.sum(weight, 0, keepdims=True)
                tile_mixed = contract(pair, weight.astype(BF16), 0, 0)
                if top is None:
                    total, mixed = tile_total, tile_mixed
                else:
                    fade = jnp.exp(top - new_top)
                    total = total * fade + tile_total
                    mixed = mixed * fade + tile_mixed
                top = new_top
        outs.append((mixed[HEAD:] / total).astype(BF16))
        stats += spread(top + jnp.log(total))
    spare = jnp.zeros((STAT_ROWS - len(stats), stats[0].shape[1]), F32)
    out = jnp.concatenate([*outs, jnp.concatenate([*stats, spare], 0).astype(BF16)], 0)
    for h in range(halves):
        for b in range(blocks):
            at = (h * blocks + b) * part
            o_ref[h, b] = out[:, at : at + part]


def cross_backward_kernel(q_ref, do_ref, *refs):
    count = (len(refs) - 1) // 2
    kv_refs, dkv_refs, dq_ref = refs[:count], refs[count:-1], refs[-1]
    halves, blocks, features, part = q_ref.shape
    width = halves * blocks * part
    queries, grads = gather_chunks(q_ref), gather_chunks(do_ref)
    heads = features // HEAD
    stats = grads[features:].astype(F32)
    outs = []
    for n in range(heads):
        query = with_zeros_below(queries[n * HEAD : (n + 1) * HEAD])
        grad = with_zeros_above(grads[n * HEAD : (n + 1) * HEAD])
        lse = gathered(stats, 6 * n)
        inner = gathered(stats, 6 * n + 3)
        lanes = slice(n * 2 * HEAD, (n + 1) * 2 * HEAD)
        both = jnp.concatenate([query, grad], 1)
        query_grad = None
        for kv_ref, dkv_ref in zip(kv_refs, dkv_refs):
            for start in range(0, kv_ref.shape[1], KEY_TILE):
                pair = kv_ref[0, start : start + KEY_TILE, lanes]
                products = contract(pair, both, 1, 0)
                weight = jnp.exp(products[:, :width] - lse)
                slope = (weight * (products[:, width:] - inner)).astype(BF16)
                dkv_ref[0, start : start + KEY_TILE, lanes] = (
                    contract(slope, query, 1, 1) + contract(weight.astype(BF16), grad, 1, 1)
                ).astype(BF16)
                part_grad = contract(pair, slope, 0, 0)
                query_grad = part_grad if query_grad is None else query_grad + part_grad
        outs.append((query_grad[:HEAD] * HEAD**-0.5).astype(BF16))
    out = jnp.concatenate(outs, 0)
    for h in range(halves):
        for b in range(blocks):
            at = (h * blocks + b) * part
            dq_ref[h, b] = out[:, at : at + part]


def self_backward_kernel(at_ref, *refs):
    x_refs, refs = refs[:-10], refs[-10:]
    q_ref, kv_ref, o_ref, do_ref, lse_ref, grad_ref, dw_ref, db_ref, dkv_ref, all_ref = refs
    halves, blocks, _, part = o_ref.shape
    block = halves * part
    dkv_ref[...] = jnp.zeros_like(dkv_ref)
    parts = []
    for i in range(blocks):
        lanes = slice(i * block, (i + 1) * block)
        reach = (i + 1) * block
        keys = kv_ref[0, :reach]
        query = with_zeros_below(q_ref[0, :, lanes])
        grad = jnp.concatenate([do_ref[h, i] for h in range(halves)], 1)
        mixed = jnp.concatenate([o_ref[h, i] for h in range(halves)], 1)
        inner = jnp.sum(grad.astype(F32) * mixed.astype(F32), 0, keepdims=True)
        grad = with_zeros_above(grad)
        weight = jnp.exp(contract(keys, query, 1, 0) - lse_ref[0, :, lanes])
        slope = (weight * (contract(keys, grad, 1, 0) - inner)).astype(BF16)
        parts.append(contract(keys, slope, 0, 0)[:HEAD] * HEAD**-0.5)
        dkv_ref[:, :reach] += contract(query, slope, 1, 1) + contract(
            grad, weight.astype(BF16), 1, 1
        )
    grads = jnp.concatenate(
        [jnp.concatenate(parts, 1).astype(BF16), dkv_ref[...].astype(BF16)], 0
    )
    all_ref[...] = grads
    for i in range(blocks):
        for h in range(halves):
            at = i * block + h * part
            grad_ref[h, i] = grads[:, at : at + part]

    @pl.when(pl.program_id(0) == 0)
    def _():
        dw_ref[...] = jnp.zeros_like(dw_ref)
        db_ref[...] = jnp.zeros_like(db_ref)

    dw_ref[...] += sum(
        contract(all_ref[:, slot_at(at_ref[0], k, block)], x_ref[0], 1, 0)
        for k, x_ref in enumerate(x_refs)
    )
    db_ref[...] += jnp.sum(grads.astype(F32), 1, keepdims=True)


def encoder_kernel(at_ref, e_ref, w_ref, b_ref, *refs):
    out_refs, all_ref = refs[:-1], refs[-1]
    all_ref[...] = (contract(e_ref[...], w_ref[...], 1, 0) + b_ref[...]).astype(BF16)
    for k, out_ref in enumerate(out_refs):
        out_ref[...] = all_ref[:, slot_at(at_ref[0], k, out_ref.shape[1])]


def encoder_back_kernel(at_ref, e_ref, w_ref, *refs):
    grad_refs, (part_ref, sum_ref, dw_ref, total_ref, all_ref) = refs[:-5], refs[-5:]
    for k, grad_ref in enumerate(grad_refs):
        all_ref[:, slot_at(at_ref[0], k, grad_ref.shape[1])] = grad_ref[...]
    grads = all_ref[...]
    part_ref[...] = contract(grads, w_ref[...], 1, 1).astype(BF16)

    @pl.when(pl.program_id(0) == 0)
    def _():
        total_ref[...] = jnp.zeros_like(total_ref)
        sum_ref[...] = jnp.zeros_like(sum_ref)

    total_ref[...] += contract(e_ref[...], grads, 0, 0)
    sum_ref[...] += jnp.sum(grads.astype(F32), 0, keepdims=True)

    @pl.when(pl.program_id(0) == pl.num_programs(0) - 1)
    def _():
        dw_ref[...] = total_ref[...].astype(BF16)


def plane_grad_kernel(sides, ready, at_ref, *refs):
    count = len(sides)
    lefts, rights, refs = refs[:count], refs[count : 2 * count], refs[2 * count :]
    ready_refs, out_refs = refs[:ready], refs[ready:]
    shard = out_refs[0].shape[1]
    for bit, out_ref in enumerate(out_refs):
        here = slot_at(at_ref[0], 2 * pl.program_id(0) + bit, shard)
        column = 0
        for left, right, side in zip(lefts, rights, sides):
            width = right.shape[1 - side]
            out_ref[0, :, column : column + width] = contract(
                left[:, here], right[...], 0, side
            ).astype(BF16)
            column += width
        for ready_ref in ready_refs:
            width = ready_ref.shape[1]
            out_ref[0, :, column : column + width] = ready_ref[here]
            column += width


def mlp_grad_kernel(two_ref, pre_ref, low_ref, active_ref, out_ref):
    width = pre_ref.shape[1]
    out_ref[:, :width] = contract(two_ref[...], pre_ref[...], 0, 0).astype(BF16)
    out_ref[:, width:] = contract(low_ref[...], active_ref[...], 0, 0).astype(BF16)


def halve_kernel(keep_ref, got_ref, *out_refs):
    size = out_refs[0].shape[0]
    for i, out_ref in enumerate(out_refs):
        for j in range(size):
            total = keep_ref[i * size + j].astype(F32) + got_ref[i * size + j].astype(F32)
            out_ref[j] = total.astype(BF16)


def rank_split_kernel(count, at_ref, *refs):
    part_refs, own_ref, send_refs = refs[:count], refs[count], refs[count + 1 :]
    kinds, _, columns = own_ref.shape
    for i in range(kinds):
        for k, out_ref in enumerate((own_ref, *send_refs)):
            first = (i * (len(send_refs) + 1) + (at_ref[0] ^ k)) * columns
            here = pl.ds(pl.multiple_of(first, columns), columns)
            total = sum(part_ref[0, :, here].astype(F32) for part_ref in part_refs)
            out_ref[i] = total.astype(out_ref.dtype)


def input_grad_kernel(stacked_ref, proj_ref, first_ref, out_ref, all_ref):
    @pl.when(pl.program_id(0) == 0)
    def _():
        heads = stacked_ref.shape[0]
        for j in range(3):
            rows = [stacked_ref[h, j * HEAD : (j + 1) * HEAD] for h in range(heads)]
            all_ref[:, j * heads * HEAD : (j + 1) * heads * HEAD] = jnp.concatenate(rows, 0).T

    out_ref[...] = (first_ref[...] + contract(all_ref[...], proj_ref[...], 1, 1)).astype(BF16)


def by_first(shape, lead=1):
    return pl.BlockSpec((lead,) + shape[1:], lambda s: (s,) + (0,) * (len(shape) - 1))


def whole(shape):
    return pl.BlockSpec(shape, lambda s: (0,) * len(shape))


def shaped(shape, dtype):
    return jax.ShapeDtypeStruct(shape, dtype)


def call(kernel, seqs, in_specs, out_specs, out_shape, operands, cost, scratch=()):
    flops, transcendentals = cost
    moved = sum(o.size * o.dtype.itemsize for o in operands)
    moved += sum(o.size * o.dtype.itemsize for o in out_shape)
    return pl.pallas_call(
        kernel,
        grid=(seqs,),
        in_specs=in_specs,
        out_specs=out_specs,
        out_shape=out_shape,
        scratch_shapes=scratch,
        compiler_params=pltpu.CompilerParams(
            dimension_semantics=("arbitrary",), vmem_limit_bytes=VMEM_BYTES
        ),
        cost_estimate=pl.CostEstimate(
            flops=flops // COST_SHARE,
            bytes_accessed=moved // COST_SHARE,
            transcendentals=transcendentals // COST_SHARE,
        ),
    )(*operands)


def one_step(kernel, out, *operands, flops=0):
    specs = [IN_SMEM if v.dtype == jnp.int32 else whole(v.shape) for v in operands]
    return call(kernel, 1, specs, [whole(out)], [shaped(out, BF16)], operands, (flops, 0))[0]


def self_forward(at, slots, weights, query_bias, pair_bias, chunk_shape):
    seqs, block, width = slots[0].shape
    length = block * len(slots)
    halves = chunk_shape[0] // seqs
    query, pair, lse = (seqs, HEAD, length), (seqs, length, 2 * HEAD), (seqs, 1, length)
    return call(
        self_forward_kernel,
        seqs,
        [IN_SMEM]
        + [by_first(x.shape) for x in slots]
        + [whole(weights.shape), whole(query_bias.shape), whole(pair_bias.shape)],
        [by_first(query), by_first(pair), by_first(chunk_shape, halves), by_first(lse)],
        [shaped(query, BF16), shaped(pair, BF16), shaped(chunk_shape, BF16), shaped(lse, F32)],
        [at, *slots, weights, query_bias, pair_bias],
        (seqs * length * (2 * width * 3 * HEAD + 8 * length * HEAD), seqs * length * length),
    )


def cross_forward(query, pairs):
    seqs = pairs[0].shape[0]
    halves, blocks, features, part = query.shape
    halves //= seqs
    length = halves * blocks * part
    keys = sum(p.shape[1] for p in pairs)
    out = (halves * seqs, blocks, features + STAT_ROWS, part)
    return call(
        cross_forward_kernel,
        seqs,
        [by_first(query.shape, halves)] + [by_first(p.shape) for p in pairs],
        [by_first(out, halves)],
        [shaped(out, BF16)],
        [query, *pairs],
        (seqs * length * keys * 8 * features, seqs * length * keys * features // HEAD),
    )[0]


def cross_backward(query, grad, pairs):
    seqs = pairs[0].shape[0]
    halves, blocks, features, part = query.shape
    halves //= seqs
    length = halves * blocks * part
    keys = sum(p.shape[1] for p in pairs)
    return call(
        cross_backward_kernel,
        seqs,
        [by_first(query.shape, halves), by_first(grad.shape, halves)] + [by_first(p.shape) for p in pairs],
        [by_first(p.shape) for p in pairs] + [by_first(query.shape, halves)],
        [shaped(p.shape, BF16) for p in pairs] + [shaped(query.shape, BF16)],
        [query, grad, *pairs],
        (seqs * length * keys * 20 * features, seqs * length * keys * features // HEAD),
    )


def self_backward(at, slots, query, pair, mixed, grad, lse):
    seqs, block, width = slots[0].shape
    length = block * len(slots)
    halves = mixed.shape[0] // seqs
    chunk = by_first(mixed.shape, halves)
    out = mixed.shape[:2] + (3 * HEAD, mixed.shape[3])
    return call(
        self_backward_kernel,
        seqs,
        [IN_SMEM]
        + [by_first(x.shape) for x in slots]
        + [by_first(query.shape), by_first(pair.shape), chunk, chunk, by_first(lse.shape)],
        [by_first(out, halves), whole((3 * HEAD, width)), whole((3 * HEAD, 1))],
        [shaped(out, BF16), shaped((3 * HEAD, width), F32), shaped((3 * HEAD, 1), F32)],
        [at, *slots, query, pair, mixed, grad, lse],
        (seqs * length * (2 * width * 3 * HEAD + 20 * length * HEAD), seqs * length * length),
        [pltpu.VMEM((2 * HEAD, length), F32), pltpu.VMEM((3 * HEAD, length), BF16)],
    )


def encoder_pairs(at, rows, weights, bias, count):
    length, width = rows.shape
    tile = min(ROW_TILE, length)
    pair = (length, weights.shape[1] // count)
    return call(
        encoder_kernel,
        length // tile,
        [IN_SMEM, by_first(rows.shape, tile), whole(weights.shape), whole(bias.shape)],
        [by_first(pair, tile)] * count,
        [shaped(pair, BF16)] * count,
        [at, rows, weights, bias],
        (2 * length * width * weights.shape[1], 0),
        [pltpu.VMEM((tile, weights.shape[1]), BF16)],
    )


def encoder_back(at, rows, weights, grads):
    length, width = rows.shape
    tile = min(ROW_TILE, length)
    columns = weights.shape[1]
    return call(
        encoder_back_kernel,
        length // tile,
        [IN_SMEM, by_first(rows.shape, tile), whole(weights.shape)]
        + [by_first(g.shape, tile) for g in grads],
        [by_first(rows.shape, tile), whole((1, columns)), whole(weights.shape)],
        [shaped(rows.shape, BF16), shaped((1, columns), F32), shaped(weights.shape, BF16)],
        [at, rows, weights, *grads],
        (4 * length * width * columns, 0),
        [pltpu.VMEM(weights.shape, F32), pltpu.VMEM((tile, columns), BF16)],
    )


def mlp_grads(two, pre_low, low, active):
    count, width = two.shape
    columns = pre_low.shape[1]
    tile = 256
    strip = pl.BlockSpec((count, tile), lambda i: (0, i))
    out = (width, 2 * columns)
    return call(
        mlp_grad_kernel,
        width // tile,
        [strip, whole(pre_low.shape), strip, whole(active.shape)],
        [by_first(out, tile)],
        [shaped(out, BF16)],
        [two, pre_low, low, active],
        (4 * count * width * columns, 0),
    )[0]


def halve(keep, got, groups):
    count, rows, columns = keep.shape
    tile = min(512, columns)
    stack = pl.BlockSpec((count, rows, tile), lambda i: (0, 0, i))
    strip = pl.BlockSpec((count // groups, rows, tile), lambda i: (0, 0, i))
    return call(
        halve_kernel,
        columns // tile,
        [stack, stack],
        [strip] * groups,
        [shaped((count // groups, rows, columns), BF16)] * groups,
        [keep, got],
        (keep.size, 0),
    )


def rank_split(at, parts, kinds, ranks):
    _, rows, columns = parts[0].shape
    out = (kinds, rows, columns // kinds // ranks)
    return call(
        functools.partial(rank_split_kernel, len(parts)),
        1,
        [IN_SMEM] + [whole(v.shape) for v in parts],
        [whole(out)] * ranks,
        [shaped(out, F32)] + [shaped(out, BF16)] * (ranks - 1),
        [at, *parts],
        (len(parts) * parts[0].size, 0),
    )


def input_grads(stacked, proj, first):
    part, width = first.shape
    tile = 256
    strip = pl.BlockSpec((part, tile), lambda i: (0, i))
    return call(
        input_grad_kernel,
        width // tile,
        [whole(stacked.shape), by_first(proj.shape, tile), strip],
        [strip],
        [shaped(first.shape, BF16)],
        [stacked, proj, first],
        (2 * part * proj.size, 0),
        [pltpu.VMEM((part, proj.shape[1]), BF16)],
    )[0]


def plane_grads(at, items, ready, shard):
    lefts, rights, sides = zip(*items) if items else ((), (), ())
    width = (lefts[0].T if items else ready[0]).shape[0]
    columns = sum(right.shape[1 - side] for right, side in zip(rights, sides))
    columns += sum(v.shape[1] for v in ready)
    out = (width // shard // 2, shard, columns)
    flops = sum(2 * width * right.size for right in rights)
    return call(
        functools.partial(plane_grad_kernel, sides, len(ready)),
        out[0],
        [IN_SMEM] + [whole(v.shape) for v in (*lefts, *rights, *ready)],
        [by_first(out)] * 2,
        [shaped(out, BF16)] * 2,
        [at, *lefts, *rights, *ready],
        (flops, 0),
    )


def body(
    hidden_in,
    encoder_states,
    out_cotangent,
    self_proj,
    self_qv_bias,
    self_out_proj,
    cross_q_proj,
    cross_kv_proj,
    cross_qv_bias,
    cross_out_proj,
    up_proj,
    up_bias,
    down_proj,
    norm_gain,
    norm_bias,
    out_bias,
):
    blocks, ranks = lax.axis_size("ctx"), lax.axis_size("tp")
    plane = lax.axis_size("dp") * blocks
    own_ctx, own_tp = lax.axis_index("ctx"), lax.axis_index("tp")
    seqs, block, width = hidden_in.shape
    rows = seqs * block
    part = rows // ranks
    shard = width // plane
    heads_here = self_qv_bias.shape[0]
    local_width = heads_here * HEAD
    all_heads = heads_here * ranks
    enc_len = encoder_states.shape[1]
    hidden = up_proj.shape[1]
    slots = range(blocks)

    def ctx_swap(values, k):
        return lax.ppermute(values, "ctx", [(i, i ^ k) for i in slots])

    def tp_swap(values, k):
        return lax.ppermute(values, "tp", [(i, i ^ k) for i in range(ranks)])

    def exchange(values):
        return lax.all_to_all(values, HEADS, split_axis=0, concat_axis=0, tiled=True)

    def own_rows(values):
        return lax.dynamic_slice_in_dim(values.reshape(rows, width), own_tp * part, part, 0)

    def in_swap_order(values, axis):
        return [lax.dynamic_index_in_dim(values, own_ctx ^ k, axis, keepdims=False) for k in slots]

    cores = 2
    pair_heads = heads_here // cores
    pair_rows = pair_heads * HEAD
    core_at = lax.rem(own_ctx, cores).reshape(1)
    ctx_at, plane_at = own_ctx.reshape(1), (lax.axis_index("dp") * blocks + own_ctx).reshape(1)

    def plane_swap(values, k):
        return lax.ppermute(values, PLANE, [(i, i ^ k) for i in range(plane)])

    def sum_begin(items, ready=()):
        if plane == 8:
            keep, send = plane_grads(plane_at, items, ready, shard)
            return (keep, plane_swap(send, 1))
        sums = [contract(left, right, 0, side).astype(BF16) for left, right, side in items]
        sums = jnp.concatenate([*sums, *ready], 1)
        return (lax.psum_scatter(sums, PLANE, scatter_dimension=0, tiled=True),)

    def sum_near(state, groups):
        return halve(*state, groups) if plane == 8 else state

    def sum_far(parts):
        return [plane_swap(part, 2 * j) if j else part for j, part in enumerate(parts)]

    def sum_dp(parts):
        return [parts[0], plane_swap(parts[1], 4)] if plane == 8 else parts

    def sum_x(parts):
        if plane != 8:
            return parts
        own, other = (parts[0][j].astype(F32) + parts[1][j].astype(F32) for j in range(2))
        return [own, plane_swap(other.astype(BF16), 2)]

    def sum_end(parts):
        return sum(part.astype(F32).reshape(shard, -1) for part in parts)

    def whole_on_ranks(values):
        values = jnp.broadcast_to(values[None], (ranks,) + values.shape)
        return lax.all_to_all(values, "tp", split_axis=0, concat_axis=0, tiled=True)

    bias_part = 2 * HEAD // plane
    count = heads_here * bias_part
    core_tokens, x_tokens = ctx_swap(hidden_in, 1), ctx_swap(hidden_in, 2)
    rank_at = own_tp.reshape(1)

    def rank_parts(values):
        return [values] + [tp_swap(values, k) for k in range(1, ranks)]

    def from_ranks(parts):
        out = (shard, parts[0].shape[0] * width)
        return one_step(rank_kernel, out, rank_at, *parts)

    square = one_step(
        square_pack_kernel, (3, shard, local_width), self_out_proj, cross_q_proj, cross_out_proj
    )
    square = rank_parts(square)
    square, first_proj, core_tokens, x_tokens = together(square, self_proj, core_tokens, x_tokens)
    vectors = jnp.concatenate([norm_gain, norm_bias, out_bias])
    small = jnp.concatenate([v.reshape(-1) for v in (self_qv_bias, cross_qv_bias, up_bias)])
    small = jnp.concatenate([vectors, small.reshape(-1, shard)])
    small = jnp.pad(small, ((0, 16 - small.shape[0]), (0, 0)))
    first = one_step(
        first_pack_kernel, (plane, 3 * HEAD + small.shape[0], shard), first_proj, small
    )
    first = lax.all_to_all(first, PLANE, split_axis=0, concat_axis=0, tiled=True)
    kv_weights = cross_kv_proj.reshape(2, shard, heads_here, HEAD).transpose(1, 2, 0, 3)
    kv_weights = lax.all_gather(
        kv_weights.reshape(shard, heads_here * 2 * HEAD), PLANE, axis=0, tiled=True
    )

    core_tokens, x_tokens, first, up_proj, down_proj = together(
        core_tokens, x_tokens, first, up_proj, down_proj
    )

    square = lax.all_gather(from_ranks(square), PLANE, axis=0, tiled=True)
    mlp = one_step(mlp_pack_kernel, (shard, 2 * hidden), up_proj, down_proj)
    mlp_other = tp_swap(mlp, 2)
    x_slots = [hidden_in, core_tokens, x_tokens, ctx_swap(x_tokens, 1)]
    own_head = first[:, : 3 * HEAD].swapaxes(0, 1).reshape(3 * HEAD, width)
    small = first[:, 3 * HEAD :]
    vectors = small[:, :9].swapaxes(0, 1).reshape(9, width).astype(F32)
    gains, shifts, branch_bias = vectors[:3], vectors[3:6], vectors[6:]
    small = small[:, 9:].reshape(plane, -1)

    def head_bias(values):
        values = values.reshape(plane, heads_here, bias_part).swapaxes(0, 1)
        return values.reshape(heads_here, 2 * HEAD).astype(F32)

    self_bias = head_bias(small[:, :count])
    cross_bias = head_bias(small[:, count : 2 * count])
    up_vector = small[:, 2 * count : 2 * count + up_bias.size]
    up_vector = up_vector.reshape((plane,) + up_bias.shape).swapaxes(0, 1).reshape(1, hidden)
    enc_rows = encoder_states.reshape(-1, width)
    value_bias = jnp.concatenate([jnp.zeros((heads_here, HEAD), F32), cross_bias[:, HEAD:]], 1)
    pairs = encoder_pairs(core_at, enc_rows, kv_weights, value_bias.reshape(1, -1), cores)
    x_slots, pairs = together(x_slots, pairs)
    pairs = [
        (ctx_swap(pair, k) if k else pair).reshape(seqs, enc_len, 2 * pair_rows)
        for k, pair in enumerate(pairs)
    ]

    def to_pairs(values):
        values = values.reshape(ranks, 1, cores, -1, part)
        values = jnp.broadcast_to(values, (ranks, blocks // cores) + values.shape[2:])
        return exchange(values.reshape(all_heads, -1, part)).reshape(ranks, blocks, -1, part)

    def from_pairs(values):
        values = exchange(values.reshape(all_heads, -1, part))
        return values.reshape(ranks, blocks // cores, cores, -1, part)
    head_row = lax.dynamic_index_in_dim(self_bias, own_ctx, 0, keepdims=False)
    query_column = head_row[:HEAD].reshape(HEAD, 1)
    pair_row = jnp.concatenate([jnp.zeros((HEAD,), F32), head_row[HEAD:]]).reshape(1, 2 * HEAD)
    chunk_shape = (ranks, blocks, HEAD, part)
    self_query, self_pair, self_mixed, self_lse = self_forward(
        ctx_at, x_slots, own_head, query_column, pair_row, chunk_shape
    )
    tokens_f = own_rows(hidden_in).astype(F32)
    mixed_t = exchange(self_mixed.reshape(all_heads, HEAD, part)).reshape(width, part)
    mixed_t, square, mlp_other, self_proj, pairs, up_vector = together(
        mixed_t, square, mlp_other, self_proj, pairs, up_vector
    )
    up_vector = jnp.concatenate([up_vector, tp_swap(up_vector, 2)], 1).astype(F32)
    self_out_all, cross_q_all, cross_out_all = (square[:, i * width : (i + 1) * width] for i in range(3))
    mlp = jnp.concatenate(
        [mlp[:, :hidden], mlp_other[:, :hidden], mlp[:, hidden:], mlp_other[:, hidden:]], 1
    )
    mlp = lax.all_gather(mlp, PLANE, axis=0, tiled=True)
    up_all, down_all = mlp[:, : 2 * hidden], mlp[:, 2 * hidden :]
    rank_proj = rank_parts(self_proj)
    attn_branch = contract(mixed_t, self_out_all, 0, 1) + branch_bias[0]
    first_out, first_normed, first_inv = norm_forward(tokens_f + attn_branch, gains[0], shifts[0])
    first_low = first_out.astype(BF16)
    cross_query = contract(cross_q_all, first_low, 0, 1).astype(BF16)
    cross_query = to_pairs(cross_query)
    cross_rows = lax.dynamic_slice_in_dim(cross_bias[:, :HEAD], core_at[0] * pair_heads, pair_heads, 0)
    cross_query = (
        (cross_query.astype(F32) + cross_rows.reshape(pair_rows, 1)).astype(BF16) * HEAD**-0.5
    )
    cross_mixed = cross_forward(cross_query, pairs)
    cross_mixed, rank_proj = together(cross_mixed, rank_proj)
    proj = lax.all_gather(from_ranks(rank_proj), PLANE, axis=0, tiled=True)
    halves = from_pairs(cross_mixed)
    stats = halves[:, :, :, pair_rows : pair_rows + 3 * pair_heads].astype(F32)
    stats = jnp.sum(stats.reshape(ranks, blocks // cores, cores, pair_heads, 3, part), 4, keepdims=True)
    top = jnp.max(stats, 1, keepdims=True)
    shares = jnp.exp(stats - top)
    total = jnp.sum(shares, 1, keepdims=True)
    halves = halves[:, :, :, :pair_rows].reshape(ranks, blocks // cores, cores, pair_heads, HEAD, part)
    cross_t = jnp.sum(halves.astype(F32) * (shares / total), 1).astype(BF16).reshape(width, part)
    cross_lse = (top + jnp.log(total)).reshape(all_heads, part)
    cross_branch = contract(cross_t, cross_out_all, 0, 1) + branch_bias[1]
    second_out, second_normed, second_inv = norm_forward(
        first_low.astype(F32) + cross_branch, gains[1], shifts[1]
    )
    second_low = second_out.astype(BF16)

    two = jnp.concatenate([second_low, tp_swap(second_low, 1)])
    pre_act = contract(two, up_all, 1, 0) + up_vector
    active = exact_gelu(pre_act).astype(BF16)
    mlp_part = contract(active, down_all, 1, 1)
    mlp_branch = (
        mlp_part[:part] + tp_swap(mlp_part[part:].astype(BF16), 1).astype(F32) + branch_bias[2]
    )
    third_out, third_normed, third_inv = norm_forward(
        second_low.astype(F32) + mlp_branch, gains[2], shifts[2]
    )
    hidden_out = third_out.astype(BF16)
    rms = jnp.stack([root_mean(attn_branch), root_mean(cross_branch), root_mean(mlp_branch)])

    out_grad = own_rows(out_cotangent).astype(F32)
    third_grad, gain_two, shift_two = norm_backward(out_grad, third_normed, third_inv, gains[2])
    mlp_bias_grad = jnp.sum(third_grad, 0)
    mlp_low = third_grad.astype(BF16)
    mlp_low = jnp.concatenate([mlp_low, tp_swap(mlp_low, 1)])
    active_grad = contract(mlp_low, down_all, 1, 0)
    pre_low = jax.vjp(exact_gelu, pre_act)[1](active_grad)[0].astype(BF16)
    mlp_grad = mlp_grads(two, pre_low, mlp_low, active)
    back_part = contract(pre_low, up_all, 1, 1)
    mlp_grad = lax.psum_scatter(mlp_grad, PLANE, scatter_dimension=0, tiled=True)
    back = back_part[:part] + tp_swap(back_part[part:].astype(BF16), 1).astype(F32)
    up_bias_grad = jnp.sum(pre_low.astype(F32), 0).reshape(2, hidden)
    second_grad, gain_one, shift_one = norm_backward(
        third_grad + back, second_normed, second_inv, gains[1]
    )
    cross_bias_sum = jnp.sum(second_grad, 0)
    second_grad_low = second_grad.astype(BF16)
    mix_grad = contract(cross_out_all, second_grad_low, 0, 1).astype(BF16)
    inner = jnp.sum(
        mix_grad.reshape(all_heads, HEAD, part).astype(F32)
        * cross_t.reshape(all_heads, HEAD, part).astype(F32),
        1,
    )
    def spread_rows(values):
        rows = []
        for _ in range(3):
            rows.append(lax.reduce_precision(values, 8, 7))
            values = values - rows[-1]
        return [row.astype(BF16) for row in rows]

    stats = jnp.stack([*spread_rows(cross_lse), *spread_rows(inner)], 1).reshape(ranks * cores, -1, part)
    stats = jnp.pad(stats, ((0, 0), (0, STAT_ROWS - stats.shape[1]), (0, 0)))
    mix_grad = to_pairs(jnp.concatenate([mix_grad.reshape(ranks * cores, pair_rows, part), stats], 1))
    mix_grad, hidden_out, proj = together(mix_grad, hidden_out, proj)
    hidden_out = whole_on_ranks(hidden_out)
    *pair_grads, query_grad = cross_backward(cross_query, mix_grad, pairs)
    query_grad, hidden_out = together(query_grad, hidden_out)
    pair_grads = [
        (ctx_swap(g, k) if k else g).reshape(-1, 2 * pair_rows) for k, g in enumerate(pair_grads)
    ]
    enc_part, value_sum, kv_grad = encoder_back(core_at, enc_rows, kv_weights, pair_grads)
    query_grad = from_pairs(query_grad)
    query_grad, enc_part, value_sum, kv_grad, mlp_grad = together(
        query_grad, enc_part, value_sum, kv_grad, mlp_grad
    )
    encoder_grad = lax.psum_scatter(
        enc_part.reshape(seqs, enc_len, width), "tp", scatter_dimension=2, tiled=True
    )
    value_sum = value_sum.reshape(heads_here, 2 * HEAD)[:, HEAD:]
    query_grad = jnp.sum(query_grad.astype(F32), 1).astype(BF16).reshape(width, part)
    query_sum = jnp.sum(query_grad.astype(F32), 1)

    first_grad, gain_zero, shift_zero = norm_backward(
        second_grad + contract(query_grad, cross_q_all, 0, 1), first_normed, first_inv, gains[0]
    )
    attn_bias_sum = jnp.sum(first_grad, 0)
    first_grad_low = first_grad.astype(BF16)
    squares = [(first_grad_low, mixed_t, 1), (first_low, query_grad, 1), (second_grad_low, cross_t, 1)]
    square_grad = sum_begin(squares)

    self_mix_grad = contract(self_out_all, first_grad_low, 0, 1).astype(BF16)
    self_mix_grad = exchange(self_mix_grad.reshape(all_heads, HEAD, part)).reshape(chunk_shape)
    kv_grad = sum_begin((), [kv_grad])
    square_grad, kv_grad = sum_near(square_grad, 4), sum_near(kv_grad, 2)
    self_mix_grad, square_grad, kv_grad = together(self_mix_grad, square_grad, kv_grad)
    kv_grad = sum_dp(kv_grad)
    stacked, head_grad, head_sum = self_backward(
        ctx_at, x_slots, self_query, self_pair, self_mixed, self_mix_grad, self_lse
    )
    mlp_grad = mlp_grad.reshape(shard, 2, 2, hidden)
    mlp_grad = [mlp_grad[:, :, 0], mlp_grad[:, :, 1]]
    stacked, head_grad, square_grad, kv_grad, mlp_grad = together(
        stacked, head_grad, square_grad, kv_grad, mlp_grad
    )
    square_grad, kv_grad = sum_far(square_grad), sum_x(kv_grad)
    stacked = exchange(stacked.reshape(all_heads, 3 * HEAD, part))
    mlp_grad = [mlp_grad[0], tp_swap(mlp_grad[1], 2)]
    stacked, head_grad, square_grad, kv_grad, mlp_grad, encoder_grad = together(
        stacked, head_grad, square_grad, kv_grad, mlp_grad, encoder_grad
    )
    if plane != 8:
        square_grad = [sum_end(square_grad).astype(BF16)[None]]
    square_grad = rank_split(rank_at, square_grad, 3, ranks)
    square_grad = [tp_swap(v, k) if k else v for k, v in enumerate(square_grad)]
    input_grad = input_grads(stacked, proj, first_grad)
    input_grad = lax.all_gather(input_grad, "tp", axis=0, tiled=True)

    head_grad = head_grad.reshape(3 * HEAD, plane, shard).swapaxes(0, 1)
    head_sum = head_sum.reshape(3, HEAD)
    head_sum = jnp.concatenate([head_sum[0], head_sum[2]]).reshape(plane, bias_part, 1)
    head_sum = jnp.pad(head_sum, ((0, 0), (0, 16 - bias_part), (0, 0)))
    def pieces(values):
        return values.reshape(-1, plane, values.shape[-1] // plane).swapaxes(0, 1).reshape(plane, -1)

    norm_sums = jnp.stack(
        [gain_zero, gain_one, gain_two, shift_zero, shift_one, shift_two]
        + [attn_bias_sum, cross_bias_sum, mlp_bias_grad]
    )
    up_cols = up_bias.shape[1]
    up_sums = pieces(up_bias_grad.reshape(-1, plane * up_cols))
    query_sums = pieces(jnp.pad(query_sum.reshape(all_heads, HEAD), ((0, 0), (0, HEAD))))
    value_sums = pieces(jnp.pad(value_sum, ((0, 0), (HEAD, 0))))
    sums = jnp.concatenate([pieces(norm_sums), up_sums, query_sums, value_sums], 1)
    sums = jnp.pad(sums, ((0, 0), (0, 16 * shard - sums.shape[1]))).reshape(plane, 16, shard)
    head_grad = jnp.concatenate(
        [head_grad, jnp.broadcast_to(head_sum, (plane, 16, shard)), sums], 1
    ).astype(BF16)
    head_grad = lax.all_to_all(head_grad, PLANE, split_axis=0, concat_axis=0, tiled=True)
    head_grad = head_grad.reshape(-1, blocks, 3 * HEAD + 32, shard).astype(F32)
    kv_grad = sum_end(kv_grad).reshape(shard, heads_here, 2, HEAD)
    kv_grad = kv_grad.transpose(2, 0, 1, 3).reshape(2, shard, local_width)
    sums = jnp.sum(head_grad[:, :, 3 * HEAD + 16 :], (0, 1))
    head_grad = jnp.sum(head_grad[:, :, : 3 * HEAD + 16], 0)
    self_proj_out = head_grad[:, : 3 * HEAD].reshape(blocks, 3, HEAD, shard)
    self_proj_out = self_proj_out.transpose(1, 3, 0, 2).reshape(3, shard, local_width)
    self_bias_out = head_grad[:, 3 * HEAD : 3 * HEAD + bias_part, 0]
    norm_out, sums = sums[:9].reshape(-1), sums[9:].reshape(-1)
    sums = jnp.concatenate([norm_out, sums[: 2 * up_bias.size + ranks * count + count], rms.reshape(-1)])
    ends = [0, norm_out.size]
    for size in (up_bias.size, up_bias.size, ranks * count, count, rms.size):
        ends.append(ends[-1] + size)
    sums = jnp.pad(sums, (0, 16 * 256 - sums.size)).reshape(16, 256).astype(BF16)

    sums, square_grad = together(sums, square_grad)
    mlp_grad = mlp_grad[0].astype(F32) + mlp_grad[1].astype(F32)
    up_out, down_out = mlp_grad[:, 0], mlp_grad[:, 1].T
    square_grad = sum(v.astype(F32) for v in square_grad)
    self_out_out, cross_q_out, cross_out_out = square_grad[0].T, square_grad[1], square_grad[2].T
    sums, input_grad = together(whole_on_ranks(sums), input_grad)
    input_grad, encoder_grad = input_grad.astype(F32), encoder_grad.astype(F32)
    sums = sums.astype(F32).reshape(ranks, -1)
    norm_out, up_own, up_other, query_sums, value_sums, rms = (
        sums[:, i:j] for i, j in zip(ends, ends[1:])
    )
    norm_out = jnp.sum(norm_out, 0).reshape(9, shard)

    def of_rank(values, at):
        return lax.dynamic_index_in_dim(values, at, 0, False)

    up_bias_out = (of_rank(up_own, own_tp) + of_rank(up_other, own_tp ^ 2)).reshape(up_bias.shape)
    cross_bias_out = of_rank(jnp.sum(query_sums, 0).reshape(ranks, count), own_tp)
    cross_bias_out = (cross_bias_out + of_rank(value_sums, own_tp)).reshape(heads_here, bias_part)
    rms = rms.reshape(ranks, 3, part).swapaxes(0, 1).reshape(3, rows)
    rms = jnp.concatenate([root_mean(hidden_in.reshape(rows, width).astype(F32))[None], rms])
    return (
        hidden_out.reshape(seqs, block, width),
        input_grad.reshape(seqs, block, width),
        encoder_grad,
        self_proj_out,
        self_bias_out,
        self_out_out,
        cross_q_out,
        kv_grad,
        cross_bias_out,
        cross_out_out,
        up_out,
        up_bias_out,
        down_out,
        norm_out[:3],
        norm_out[3:6],
        norm_out[6:],
        rms.reshape(4, seqs, block),
    )


def solution(mesh):
    rows, heads, columns = P("dp", "ctx", None), P("tp", PLANE), P(PLANE, "tp")
    stacked, vectors = P(None, PLANE, "tp"), P(None, PLANE)
    weights = (
        stacked, heads, heads, columns, stacked, heads, heads, columns, heads, heads,
        vectors, vectors, vectors,
    )
    return jax.shard_map(
        body,
        mesh=mesh,
        in_specs=(rows, rows, rows) + weights,
        out_specs=(rows, rows, P("dp", "ctx", "tp")) + weights + (P(None, "dp", "ctx"),),
        check_vma=False,
    )
```

```python
import functools

import jax
import jax.numpy as jnp
from jax import lax
from jax.experimental import pallas as pl
from jax.experimental.pallas import tpu as pltpu
from jax.sharding import PartitionSpec as P

EPSILON = 1e-05
HEAD = 64
KEY_TILE = 1024
STAT_ROWS = 16
ROW_TILE = 1024
COST_SHARE = 10
VMEM_BYTES = 50 * 1024 * 1024
PLANE = ("dp", "ctx")
HEADS = ("tp", "ctx")
F32 = jnp.float32
BF16 = jnp.bfloat16
IN_SMEM = pl.BlockSpec(memory_space=pltpu.SMEM)


def contract(left, right, left_dim, right_dim):
    return lax.dot_general(
        left, right, (((left_dim,), (right_dim,)), ((), ())), preferred_element_type=F32
    )


def together(*values):
    return lax.optimization_barrier(values)


def norm_forward(values, norm_gain, norm_shift):
    row_mean = jnp.mean(values, -1, keepdims=True)
    centered = values - row_mean
    inv_std = lax.rsqrt(jnp.mean(centered * centered, -1, keepdims=True) + EPSILON)
    normed = centered * inv_std
    return (normed * norm_gain + norm_shift, normed, inv_std)


def norm_backward(gradient, normed, inv_std, norm_gain):
    gain_grad = jnp.sum(gradient * normed, 0)
    shift_grad = jnp.sum(gradient, 0)
    scaled = gradient * norm_gain
    input_part = inv_std * (
        scaled
        - jnp.mean(scaled, -1, keepdims=True)
        - normed * jnp.mean(scaled * normed, -1, keepdims=True)
    )
    return (input_part, gain_grad, shift_grad)


def root_mean(values):
    return jnp.sqrt(jnp.mean(values * values, -1))


def exact_gelu(values):
    return jax.nn.gelu(values, approximate=False)


def with_zeros_below(values):
    return jnp.concatenate([values, jnp.zeros_like(values)], 0)


def with_zeros_above(values):
    return jnp.concatenate([jnp.zeros_like(values), values], 0)


def gather_chunks(ref):
    halves, blocks = ref.shape[:2]
    return jnp.concatenate([ref[h, b] for h in range(halves) for b in range(blocks)], 1)


def copy_kernel(in_ref, out_ref):
    out_ref[...] = in_ref[...]


def mlp_split_kernel(in_ref, *out_refs):
    width = out_refs[0].shape[2]
    for i, out_ref in enumerate(out_refs):
        for kind in range(2):
            at = (2 * kind + i) * width
            out_ref[kind] = in_ref[:, at : at + width]


def slot_at(own, k, size):
    return pl.ds(pl.multiple_of((own ^ k) * size, size), size)


def first_pack_kernel(proj_ref, small_ref, out_ref):
    blocks = proj_ref.shape[2] // HEAD
    for j in range(3):
        turned = proj_ref[j].T
        for e in range(out_ref.shape[0]):
            head = e % blocks * HEAD
            out_ref[e, j * HEAD : (j + 1) * HEAD] = turned[head : head + HEAD]
    for e in range(out_ref.shape[0]):
        out_ref[e, 3 * HEAD :] = small_ref[...]


def square_pack_kernel(self_out_ref, cross_q_ref, cross_out_ref, out_ref):
    out_ref[0] = self_out_ref[...].T
    out_ref[1] = cross_q_ref[...]
    out_ref[2] = cross_out_ref[...].T


def mlp_pack_kernel(up_ref, down_ref, out_ref):
    width = up_ref.shape[1]
    out_ref[:, :width] = up_ref[...]
    out_ref[:, width:] = down_ref[...].T


def rank_kernel(at_ref, *refs):
    part_refs, out_ref = refs[:-1], refs[-1]
    for k, part_ref in enumerate(part_refs):
        count, _, columns = part_ref.shape
        for i in range(count):
            first = (i * len(part_refs) + (at_ref[0] ^ k)) * columns
            out_ref[:, pl.ds(pl.multiple_of(first, columns), columns)] = part_ref[i]


def self_forward_kernel(at_ref, *refs):
    x_refs, (w_ref, bq_ref, bv_ref, q_ref, kv_ref, o_ref, lse_ref) = refs[:-7], refs[-7:]
    weights = w_ref[...]
    halves, blocks, _, part = o_ref.shape
    block = halves * part
    scale = HEAD**-0.5
    for k, x_ref in enumerate(x_refs):
        here = slot_at(at_ref[0], k, block)
        tokens = x_ref[0]
        q_ref[0, :, here] = (contract(weights[:HEAD], tokens, 1, 1) + bq_ref[...]).astype(BF16) * scale
        kv_ref[0, here] = (contract(tokens, weights[HEAD:], 1, 1) + bv_ref[...]).astype(BF16)
    for i in range(blocks):
        keys = kv_ref[0, : (i + 1) * block]
        query = q_ref[0, :, i * block : (i + 1) * block]
        scores = contract(keys, with_zeros_below(query), 1, 0)
        top = jnp.max(scores, 0, keepdims=True)
        weight = jnp.exp(scores - top)
        total = jnp.sum(weight, 0, keepdims=True)
        mixed = contract(keys, weight.astype(BF16), 0, 0)[HEAD:]
        out = (mixed / total).astype(BF16)
        for h in range(halves):
            o_ref[h, i] = out[:, h * part : (h + 1) * part]
        lse_ref[0, :, i * block : (i + 1) * block] = top + jnp.log(total)


def spread(values):
    rows = []
    for _ in range(3):
        rows.append(values.astype(BF16).astype(F32))
        values = values - rows[-1]
    return rows


def gathered(rows, at):
    return sum(rows[at + i : at + i + 1] for i in range(3))


def cross_forward_kernel(q_ref, *refs):
    kv_refs, o_ref = refs[:-1], refs[-1]
    halves, blocks, features, part = q_ref.shape
    queries = gather_chunks(q_ref)
    heads = features // HEAD
    outs, stats = [], []
    for n in range(heads):
        query = with_zeros_below(queries[n * HEAD : (n + 1) * HEAD])
        lanes = slice(n * 2 * HEAD, (n + 1) * 2 * HEAD)
        top = total = mixed = None
        for kv_ref in kv_refs:
            for start in range(0, kv_ref.shape[1], KEY_TILE):
                pair = kv_ref[0, start : start + KEY_TILE, lanes]
                scores = contract(pair, query, 1, 0)
                tile_top = jnp.max(scores, 0, keepdims=True)
                new_top = tile_top if top is None else jnp.maximum(top, tile_top)
                weight = jnp.exp(scores - new_top)
                tile_total = jnp.sum(weight, 0, keepdims=True)
                tile_mixed = contract(pair, weight.astype(BF16), 0, 0)
                if top is None:
                    total, mixed = tile_total, tile_mixed
                else:
                    fade = jnp.exp(top - new_top)
                    total = total * fade + tile_total
                    mixed = mixed * fade + tile_mixed
                top = new_top
        outs.append((mixed[HEAD:] / total).astype(BF16))
        stats += spread(top + jnp.log(total))
    spare = jnp.zeros((STAT_ROWS - len(stats), stats[0].shape[1]), F32)
    out = jnp.concatenate([*outs, jnp.concatenate([*stats, spare], 0).astype(BF16)], 0)
    for h in range(halves):
        for b in range(blocks):
            at = (h * blocks + b) * part
            o_ref[h, b] = out[:, at : at + part]


def cross_backward_kernel(q_ref, do_ref, *refs):
    count = (len(refs) - 1) // 2
    kv_refs, dkv_refs, dq_ref = refs[:count], refs[count:-1], refs[-1]
    halves, blocks, features, part = q_ref.shape
    width = halves * blocks * part
    queries, grads = gather_chunks(q_ref), gather_chunks(do_ref)
    heads = features // HEAD
    stats = grads[features:].astype(F32)
    outs = []
    for n in range(heads):
        query = with_zeros_below(queries[n * HEAD : (n + 1) * HEAD])
        grad = with_zeros_above(grads[n * HEAD : (n + 1) * HEAD])
        lse = gathered(stats, 6 * n)
        inner = gathered(stats, 6 * n + 3)
        lanes = slice(n * 2 * HEAD, (n + 1) * 2 * HEAD)
        both = jnp.concatenate([query, grad], 1)
        query_grad = None
        for kv_ref, dkv_ref in zip(kv_refs, dkv_refs):
            for start in range(0, kv_ref.shape[1], KEY_TILE):
                pair = kv_ref[0, start : start + KEY_TILE, lanes]
                products = contract(pair, both, 1, 0)
                weight = jnp.exp(products[:, :width] - lse)
                slope = (weight * (products[:, width:] - inner)).astype(BF16)
                dkv_ref[0, start : start + KEY_TILE, lanes] = (
                    contract(slope, query, 1, 1) + contract(weight.astype(BF16), grad, 1, 1)
                ).astype(BF16)
                part_grad = contract(pair, slope, 0, 0)
                query_grad = part_grad if query_grad is None else query_grad + part_grad
        outs.append((query_grad[:HEAD] * HEAD**-0.5).astype(BF16))
    out = jnp.concatenate(outs, 0)
    for h in range(halves):
        for b in range(blocks):
            at = (h * blocks + b) * part
            dq_ref[h, b] = out[:, at : at + part]


def self_backward_kernel(at_ref, *refs):
    x_refs, refs = refs[:-10], refs[-10:]
    q_ref, kv_ref, o_ref, do_ref, lse_ref, grad_ref, dw_ref, db_ref, dkv_ref, all_ref = refs
    halves, blocks, _, part = o_ref.shape
    block = halves * part
    dkv_ref[...] = jnp.zeros_like(dkv_ref)
    parts = []
    for i in range(blocks):
        lanes = slice(i * block, (i + 1) * block)
        reach = (i + 1) * block
        keys = kv_ref[0, :reach]
        query = with_zeros_below(q_ref[0, :, lanes])
        grad = jnp.concatenate([do_ref[h, i] for h in range(halves)], 1)
        mixed = jnp.concatenate([o_ref[h, i] for h in range(halves)], 1)
        inner = jnp.sum(grad.astype(F32) * mixed.astype(F32), 0, keepdims=True)
        grad = with_zeros_above(grad)
        weight = jnp.exp(contract(keys, query, 1, 0) - lse_ref[0, :, lanes])
        slope = (weight * (contract(keys, grad, 1, 0) - inner)).astype(BF16)
        parts.append(contract(keys, slope, 0, 0)[:HEAD] * HEAD**-0.5)
        dkv_ref[:, :reach] += contract(query, slope, 1, 1) + contract(
            grad, weight.astype(BF16), 1, 1
        )
    grads = jnp.concatenate(
        [jnp.concatenate(parts, 1).astype(BF16), dkv_ref[...].astype(BF16)], 0
    )
    all_ref[...] = grads
    for i in range(blocks):
        for h in range(halves):
            at = i * block + h * part
            grad_ref[h, i] = grads[:, at : at + part]

    @pl.when(pl.program_id(0) == 0)
    def _():
        dw_ref[...] = jnp.zeros_like(dw_ref)
        db_ref[...] = jnp.zeros_like(db_ref)

    dw_ref[...] += sum(
        contract(all_ref[:, slot_at(at_ref[0], k, block)], x_ref[0], 1, 0)
        for k, x_ref in enumerate(x_refs)
    )
    db_ref[...] += jnp.sum(grads.astype(F32), 1, keepdims=True)


def encoder_kernel(at_ref, e_ref, w_ref, b_ref, *refs):
    out_refs, all_ref = refs[:-1], refs[-1]
    all_ref[...] = (contract(e_ref[...], w_ref[...], 1, 0) + b_ref[...]).astype(BF16)
    for k, out_ref in enumerate(out_refs):
        out_ref[...] = all_ref[:, slot_at(at_ref[0], k, out_ref.shape[1])]


def encoder_back_kernel(at_ref, e_ref, w_ref, *refs):
    grad_refs, (part_ref, sum_ref, dw_ref, total_ref, all_ref) = refs[:-5], refs[-5:]
    for k, grad_ref in enumerate(grad_refs):
        all_ref[:, slot_at(at_ref[0], k, grad_ref.shape[1])] = grad_ref[...]
    grads = all_ref[...]
    part_ref[...] = contract(grads, w_ref[...], 1, 1).astype(BF16)

    @pl.when(pl.program_id(0) == 0)
    def _():
        total_ref[...] = jnp.zeros_like(total_ref)
        sum_ref[...] = jnp.zeros_like(sum_ref)

    total_ref[...] += contract(e_ref[...], grads, 0, 0)
    sum_ref[...] += jnp.sum(grads.astype(F32), 0, keepdims=True)

    @pl.when(pl.program_id(0) == pl.num_programs(0) - 1)
    def _():
        dw_ref[...] = total_ref[...].astype(BF16)


def plane_grad_kernel(sides, ready, at_ref, *refs):
    count = len(sides)
    lefts, rights, refs = refs[:count], refs[count : 2 * count], refs[2 * count :]
    ready_refs, out_refs = refs[:ready], refs[ready:]
    shard = out_refs[0].shape[1]
    for bit, out_ref in enumerate(out_refs):
        here = slot_at(at_ref[0], 2 * pl.program_id(0) + bit, shard)
        column = 0
        for left, right, side in zip(lefts, rights, sides):
            width = right.shape[1 - side]
            out_ref[0, :, column : column + width] = contract(
                left[:, here], right[...], 0, side
            ).astype(BF16)
            column += width
        for ready_ref in ready_refs:
            width = ready_ref.shape[1]
            out_ref[0, :, column : column + width] = ready_ref[here]
            column += width


def mlp_grad_kernel(two_ref, pre_ref, low_ref, active_ref, out_ref):
    width = pre_ref.shape[1]
    out_ref[:, :width] = contract(two_ref[...], pre_ref[...], 0, 0).astype(BF16)
    out_ref[:, width:] = contract(low_ref[...], active_ref[...], 0, 0).astype(BF16)


def halve_kernel(keep_ref, got_ref, *out_refs):
    size = out_refs[0].shape[0]
    for i, out_ref in enumerate(out_refs):
        for j in range(size):
            total = keep_ref[i * size + j].astype(F32) + got_ref[i * size + j].astype(F32)
            out_ref[j] = total.astype(BF16)


def rank_split_kernel(count, at_ref, *refs):
    part_refs, own_ref, send_refs = refs[:count], refs[count], refs[count + 1 :]
    kinds, _, columns = own_ref.shape
    for i in range(kinds):
        for k, out_ref in enumerate((own_ref, *send_refs)):
            first = (i * (len(send_refs) + 1) + (at_ref[0] ^ k)) * columns
            here = pl.ds(pl.multiple_of(first, columns), columns)
            total = sum(part_ref[0, :, here].astype(F32) for part_ref in part_refs)
            out_ref[i] = total.astype(out_ref.dtype)


def input_grad_kernel(stacked_ref, proj_ref, first_ref, out_ref, all_ref):
    @pl.when(pl.program_id(0) == 0)
    def _():
        heads = stacked_ref.shape[0]
        for j in range(3):
            rows = [stacked_ref[h, j * HEAD : (j + 1) * HEAD] for h in range(heads)]
            all_ref[:, j * heads * HEAD : (j + 1) * heads * HEAD] = jnp.concatenate(rows, 0).T

    out_ref[...] = (first_ref[...] + contract(all_ref[...], proj_ref[...], 1, 1)).astype(BF16)


def by_first(shape, lead=1):
    return pl.BlockSpec((lead,) + shape[1:], lambda s: (s,) + (0,) * (len(shape) - 1))


def whole(shape):
    return pl.BlockSpec(shape, lambda s: (0,) * len(shape))


def shaped(shape, dtype):
    return jax.ShapeDtypeStruct(shape, dtype)


def call(kernel, seqs, in_specs, out_specs, out_shape, operands, cost, scratch=()):
    flops, transcendentals = cost
    moved = sum(o.size * o.dtype.itemsize for o in operands)
    moved += sum(o.size * o.dtype.itemsize for o in out_shape)
    return pl.pallas_call(
        kernel,
        grid=(seqs,),
        in_specs=in_specs,
        out_specs=out_specs,
        out_shape=out_shape,
        scratch_shapes=scratch,
        compiler_params=pltpu.CompilerParams(
            dimension_semantics=("arbitrary",), vmem_limit_bytes=VMEM_BYTES
        ),
        cost_estimate=pl.CostEstimate(
            flops=flops // COST_SHARE,
            bytes_accessed=moved // COST_SHARE,
            transcendentals=transcendentals // COST_SHARE,
        ),
    )(*operands)


def one_step(kernel, out, *operands, flops=0):
    outs = out if isinstance(out, list) else [out]
    specs = [IN_SMEM if v.dtype == jnp.int32 else whole(v.shape) for v in operands]
    shapes = [shaped(v, BF16) for v in outs]
    results = call(kernel, 1, specs, [whole(v) for v in outs], shapes, operands, (flops, 0))
    return results if isinstance(out, list) else results[0]


def self_forward(at, slots, weights, query_bias, pair_bias, chunk_shape):
    seqs, block, width = slots[0].shape
    length = block * len(slots)
    halves = chunk_shape[0] // seqs
    query, pair, lse = (seqs, HEAD, length), (seqs, length, 2 * HEAD), (seqs, 1, length)
    return call(
        self_forward_kernel,
        seqs,
        [IN_SMEM]
        + [by_first(x.shape) for x in slots]
        + [whole(weights.shape), whole(query_bias.shape), whole(pair_bias.shape)],
        [by_first(query), by_first(pair), by_first(chunk_shape, halves), by_first(lse)],
        [shaped(query, BF16), shaped(pair, BF16), shaped(chunk_shape, BF16), shaped(lse, F32)],
        [at, *slots, weights, query_bias, pair_bias],
        (seqs * length * (2 * width * 3 * HEAD + 8 * length * HEAD), seqs * length * length),
    )


def cross_forward(query, pairs):
    seqs = pairs[0].shape[0]
    halves, blocks, features, part = query.shape
    halves //= seqs
    length = halves * blocks * part
    keys = sum(p.shape[1] for p in pairs)
    out = (halves * seqs, blocks, features + STAT_ROWS, part)
    return call(
        cross_forward_kernel,
        seqs,
        [by_first(query.shape, halves)] + [by_first(p.shape) for p in pairs],
        [by_first(out, halves)],
        [shaped(out, BF16)],
        [query, *pairs],
        (seqs * length * keys * 8 * features, seqs * length * keys * features // HEAD),
    )[0]


def cross_backward(query, grad, pairs):
    seqs = pairs[0].shape[0]
    halves, blocks, features, part = query.shape
    halves //= seqs
    length = halves * blocks * part
    keys = sum(p.shape[1] for p in pairs)
    return call(
        cross_backward_kernel,
        seqs,
        [by_first(query.shape, halves), by_first(grad.shape, halves)] + [by_first(p.shape) for p in pairs],
        [by_first(p.shape) for p in pairs] + [by_first(query.shape, halves)],
        [shaped(p.shape, BF16) for p in pairs] + [shaped(query.shape, BF16)],
        [query, grad, *pairs],
        (seqs * length * keys * 20 * features, seqs * length * keys * features // HEAD),
    )


def self_backward(at, slots, query, pair, mixed, grad, lse):
    seqs, block, width = slots[0].shape
    length = block * len(slots)
    halves = mixed.shape[0] // seqs
    chunk = by_first(mixed.shape, halves)
    out = mixed.shape[:2] + (3 * HEAD, mixed.shape[3])
    return call(
        self_backward_kernel,
        seqs,
        [IN_SMEM]
        + [by_first(x.shape) for x in slots]
        + [by_first(query.shape), by_first(pair.shape), chunk, chunk, by_first(lse.shape)],
        [by_first(out, halves), whole((3 * HEAD, width)), whole((3 * HEAD, 1))],
        [shaped(out, BF16), shaped((3 * HEAD, width), F32), shaped((3 * HEAD, 1), F32)],
        [at, *slots, query, pair, mixed, grad, lse],
        (seqs * length * (2 * width * 3 * HEAD + 20 * length * HEAD), seqs * length * length),
        [pltpu.VMEM((2 * HEAD, length), F32), pltpu.VMEM((3 * HEAD, length), BF16)],
    )


def encoder_pairs(at, rows, weights, bias, count):
    length, width = rows.shape
    tile = min(ROW_TILE, length)
    pair = (length, weights.shape[1] // count)
    return call(
        encoder_kernel,
        length // tile,
        [IN_SMEM, by_first(rows.shape, tile), whole(weights.shape), whole(bias.shape)],
        [by_first(pair, tile)] * count,
        [shaped(pair, BF16)] * count,
        [at, rows, weights, bias],
        (2 * length * width * weights.shape[1], 0),
        [pltpu.VMEM((tile, weights.shape[1]), BF16)],
    )


def encoder_back(at, rows, weights, grads):
    length, width = rows.shape
    tile = min(ROW_TILE, length)
    columns = weights.shape[1]
    return call(
        encoder_back_kernel,
        length // tile,
        [IN_SMEM, by_first(rows.shape, tile), whole(weights.shape)]
        + [by_first(g.shape, tile) for g in grads],
        [by_first(rows.shape, tile), whole((1, columns)), whole(weights.shape)],
        [shaped(rows.shape, BF16), shaped((1, columns), F32), shaped(weights.shape, BF16)],
        [at, rows, weights, *grads],
        (4 * length * width * columns, 0),
        [pltpu.VMEM(weights.shape, F32), pltpu.VMEM((tile, columns), BF16)],
    )


def mlp_grads(two, pre_low, low, active):
    count, width = two.shape
    columns = pre_low.shape[1]
    tile = 256
    strip = pl.BlockSpec((count, tile), lambda i: (0, i))
    out = (width, 2 * columns)
    return call(
        mlp_grad_kernel,
        width // tile,
        [strip, whole(pre_low.shape), strip, whole(active.shape)],
        [by_first(out, tile)],
        [shaped(out, BF16)],
        [two, pre_low, low, active],
        (4 * count * width * columns, 0),
    )[0]


def halve(keep, got, groups):
    count, rows, columns = keep.shape
    tile = min(512, columns)
    stack = pl.BlockSpec((count, rows, tile), lambda i: (0, 0, i))
    strip = pl.BlockSpec((count // groups, rows, tile), lambda i: (0, 0, i))
    return call(
        halve_kernel,
        columns // tile,
        [stack, stack],
        [strip] * groups,
        [shaped((count // groups, rows, columns), BF16)] * groups,
        [keep, got],
        (keep.size, 0),
    )


def rank_split(at, parts, kinds, ranks):
    _, rows, columns = parts[0].shape
    out = (kinds, rows, columns // kinds // ranks)
    return call(
        functools.partial(rank_split_kernel, len(parts)),
        1,
        [IN_SMEM] + [whole(v.shape) for v in parts],
        [whole(out)] * ranks,
        [shaped(out, F32)] + [shaped(out, BF16)] * (ranks - 1),
        [at, *parts],
        (len(parts) * parts[0].size, 0),
    )


def input_grads(stacked, proj, first):
    part, width = first.shape
    tile = 256
    strip = pl.BlockSpec((part, tile), lambda i: (0, i))
    return call(
        input_grad_kernel,
        width // tile,
        [whole(stacked.shape), by_first(proj.shape, tile), strip],
        [strip],
        [shaped(first.shape, BF16)],
        [stacked, proj, first],
        (2 * part * proj.size, 0),
        [pltpu.VMEM((part, proj.shape[1]), BF16)],
    )[0]


def plane_grads(at, items, ready, shard):
    lefts, rights, sides = zip(*items) if items else ((), (), ())
    width = (lefts[0].T if items else ready[0]).shape[0]
    columns = sum(right.shape[1 - side] for right, side in zip(rights, sides))
    columns += sum(v.shape[1] for v in ready)
    out = (width // shard // 2, shard, columns)
    flops = sum(2 * width * right.size for right in rights)
    return call(
        functools.partial(plane_grad_kernel, sides, len(ready)),
        out[0],
        [IN_SMEM] + [whole(v.shape) for v in (*lefts, *rights, *ready)],
        [by_first(out)] * 2,
        [shaped(out, BF16)] * 2,
        [at, *lefts, *rights, *ready],
        (flops, 0),
    )


def body(
    hidden_in,
    encoder_states,
    out_cotangent,
    self_proj,
    self_qv_bias,
    self_out_proj,
    cross_q_proj,
    cross_kv_proj,
    cross_qv_bias,
    cross_out_proj,
    up_proj,
    up_bias,
    down_proj,
    norm_gain,
    norm_bias,
    out_bias,
):
    blocks, ranks = lax.axis_size("ctx"), lax.axis_size("tp")
    plane = lax.axis_size("dp") * blocks
    own_ctx, own_tp = lax.axis_index("ctx"), lax.axis_index("tp")
    seqs, block, width = hidden_in.shape
    rows = seqs * block
    part = rows // ranks
    shard = width // plane
    heads_here = self_qv_bias.shape[0]
    local_width = heads_here * HEAD
    all_heads = heads_here * ranks
    enc_len = encoder_states.shape[1]
    hidden = up_proj.shape[1]
    slots = range(blocks)

    def ctx_swap(values, k):
        return lax.ppermute(values, "ctx", [(i, i ^ k) for i in slots])

    def tp_swap(values, k):
        return lax.ppermute(values, "tp", [(i, i ^ k) for i in range(ranks)])

    def exchange(values):
        return lax.all_to_all(values, HEADS, split_axis=0, concat_axis=0, tiled=True)

    def own_rows(values):
        return lax.dynamic_slice_in_dim(values.reshape(rows, width), own_tp * part, part, 0)

    def in_swap_order(values, axis):
        return [lax.dynamic_index_in_dim(values, own_ctx ^ k, axis, keepdims=False) for k in slots]

    cores = 2
    pair_heads = heads_here // cores
    pair_rows = pair_heads * HEAD
    core_at = lax.rem(own_ctx, cores).reshape(1)
    ctx_at, plane_at = own_ctx.reshape(1), (lax.axis_index("dp") * blocks + own_ctx).reshape(1)

    def plane_swap(values, k):
        return lax.ppermute(values, PLANE, [(i, i ^ k) for i in range(plane)])

    def sum_begin(items, ready=()):
        if plane == 8:
            keep, send = plane_grads(plane_at, items, ready, shard)
            return (keep, plane_swap(send, 1))
        sums = [contract(left, right, 0, side).astype(BF16) for left, right, side in items]
        sums = jnp.concatenate([*sums, *ready], 1)
        return (lax.psum_scatter(sums, PLANE, scatter_dimension=0, tiled=True),)

    def sum_near(state, groups):
        return halve(*state, groups) if plane == 8 else state

    def sum_far(parts):
        return [plane_swap(part, 2 * j) if j else part for j, part in enumerate(parts)]

    def sum_dp(parts):
        return [parts[0], plane_swap(parts[1], 4)] if plane == 8 else parts

    def sum_x(parts):
        if plane != 8:
            return parts
        own, other = (parts[0][j].astype(F32) + parts[1][j].astype(F32) for j in range(2))
        return [own, plane_swap(other.astype(BF16), 2)]

    def sum_end(parts):
        return sum(part.astype(F32).reshape(shard, -1) for part in parts)

    def whole_on_ranks(values):
        values = jnp.broadcast_to(values[None], (ranks,) + values.shape)
        return lax.all_to_all(values, "tp", split_axis=0, concat_axis=0, tiled=True)

    bias_part = 2 * HEAD // plane
    count = heads_here * bias_part
    core_tokens, x_tokens = ctx_swap(hidden_in, 1), ctx_swap(hidden_in, 2)
    rank_at = own_tp.reshape(1)

    def rank_parts(values):
        return [values] + [tp_swap(values, k) for k in range(1, ranks)]

    def from_ranks(parts):
        out = (shard, parts[0].shape[0] * width)
        return one_step(rank_kernel, out, rank_at, *parts)

    square = one_step(
        square_pack_kernel, (3, shard, local_width), self_out_proj, cross_q_proj, cross_out_proj
    )
    square = rank_parts(square)
    square, first_proj, core_tokens, x_tokens = together(square, self_proj, core_tokens, x_tokens)
    vectors = jnp.concatenate([norm_gain, norm_bias, out_bias])
    small = jnp.concatenate([v.reshape(-1) for v in (self_qv_bias, cross_qv_bias, up_bias)])
    small = jnp.concatenate([vectors, small.reshape(-1, shard)])
    small = jnp.pad(small, ((0, 16 - small.shape[0]), (0, 0)))
    first = one_step(
        first_pack_kernel, (plane, 3 * HEAD + small.shape[0], shard), first_proj, small
    )
    first = lax.all_to_all(first, PLANE, split_axis=0, concat_axis=0, tiled=True)
    kv_weights = cross_kv_proj.reshape(2, shard, heads_here, HEAD).transpose(1, 2, 0, 3)
    kv_weights = lax.all_gather(
        kv_weights.reshape(shard, heads_here * 2 * HEAD), PLANE, axis=0, tiled=True
    )

    core_tokens, x_tokens, first, up_proj, down_proj = together(
        core_tokens, x_tokens, first, up_proj, down_proj
    )

    square = lax.all_gather(from_ranks(square), PLANE, axis=0, tiled=True)
    mlp = one_step(mlp_pack_kernel, (shard, 2 * hidden), up_proj, down_proj)
    mlp_other = tp_swap(mlp, 2)
    x_slots = [hidden_in, core_tokens, x_tokens, ctx_swap(x_tokens, 1)]
    own_head = first[:, : 3 * HEAD].swapaxes(0, 1).reshape(3 * HEAD, width)
    small = first[:, 3 * HEAD :]
    vectors = small[:, :9].swapaxes(0, 1).reshape(9, width).astype(F32)
    gains, shifts, branch_bias = vectors[:3], vectors[3:6], vectors[6:]
    small = small[:, 9:].reshape(plane, -1)

    def head_bias(values):
        values = values.reshape(plane, heads_here, bias_part).swapaxes(0, 1)
        return values.reshape(heads_here, 2 * HEAD).astype(F32)

    self_bias = head_bias(small[:, :count])
    cross_bias = head_bias(small[:, count : 2 * count])
    up_vector = small[:, 2 * count : 2 * count + up_bias.size]
    up_vector = up_vector.reshape((plane,) + up_bias.shape).swapaxes(0, 1).reshape(1, hidden)
    enc_rows = encoder_states.reshape(-1, width)
    value_bias = jnp.concatenate([jnp.zeros((heads_here, HEAD), F32), cross_bias[:, HEAD:]], 1)
    pairs = encoder_pairs(core_at, enc_rows, kv_weights, value_bias.reshape(1, -1), cores)
    x_slots, pairs = together(x_slots, pairs)
    pairs = [
        (ctx_swap(pair, k) if k else pair).reshape(seqs, enc_len, 2 * pair_rows)
        for k, pair in enumerate(pairs)
    ]

    def to_pairs(values):
        values = values.reshape(ranks, 1, cores, -1, part)
        values = jnp.broadcast_to(values, (ranks, blocks // cores) + values.shape[2:])
        return exchange(values.reshape(all_heads, -1, part)).reshape(ranks, blocks, -1, part)

    def from_pairs(values):
        values = exchange(values.reshape(all_heads, -1, part))
        return values.reshape(ranks, blocks // cores, cores, -1, part)
    head_row = lax.dynamic_index_in_dim(self_bias, own_ctx, 0, keepdims=False)
    query_column = head_row[:HEAD].reshape(HEAD, 1)
    pair_row = jnp.concatenate([jnp.zeros((HEAD,), F32), head_row[HEAD:]]).reshape(1, 2 * HEAD)
    chunk_shape = (ranks, blocks, HEAD, part)
    self_query, self_pair, self_mixed, self_lse = self_forward(
        ctx_at, x_slots, own_head, query_column, pair_row, chunk_shape
    )
    tokens_f = own_rows(hidden_in).astype(F32)
    mixed_t = exchange(self_mixed.reshape(all_heads, HEAD, part)).reshape(width, part)
    mixed_t, square, mlp_other, self_proj, pairs, up_vector = together(
        mixed_t, square, mlp_other, self_proj, pairs, up_vector
    )
    up_vector = jnp.concatenate([up_vector, tp_swap(up_vector, 2)], 1).astype(F32)
    self_out_all, cross_q_all, cross_out_all = (square[:, i * width : (i + 1) * width] for i in range(3))
    mlp = jnp.concatenate(
        [mlp[:, :hidden], mlp_other[:, :hidden], mlp[:, hidden:], mlp_other[:, hidden:]], 1
    )
    mlp = lax.all_gather(mlp, PLANE, axis=0, tiled=True)
    up_all, down_all = mlp[:, : 2 * hidden], mlp[:, 2 * hidden :]
    rank_proj = rank_parts(self_proj)
    attn_branch = contract(mixed_t, self_out_all, 0, 1) + branch_bias[0]
    first_out, first_normed, first_inv = norm_forward(tokens_f + attn_branch, gains[0], shifts[0])
    first_low = first_out.astype(BF16)
    cross_query = contract(cross_q_all, first_low, 0, 1).astype(BF16)
    cross_query = to_pairs(cross_query)
    cross_rows = lax.dynamic_slice_in_dim(cross_bias[:, :HEAD], core_at[0] * pair_heads, pair_heads, 0)
    cross_query = (
        (cross_query.astype(F32) + cross_rows.reshape(pair_rows, 1)).astype(BF16) * HEAD**-0.5
    )
    cross_mixed = cross_forward(cross_query, pairs)
    cross_mixed, rank_proj = together(cross_mixed, rank_proj)
    proj = lax.all_gather(from_ranks(rank_proj), PLANE, axis=0, tiled=True)
    halves = from_pairs(cross_mixed)
    stats = halves[:, :, :, pair_rows : pair_rows + 3 * pair_heads].astype(F32)
    stats = jnp.sum(stats.reshape(ranks, blocks // cores, cores, pair_heads, 3, part), 4, keepdims=True)
    top = jnp.max(stats, 1, keepdims=True)
    shares = jnp.exp(stats - top)
    total = jnp.sum(shares, 1, keepdims=True)
    halves = halves[:, :, :, :pair_rows].reshape(ranks, blocks // cores, cores, pair_heads, HEAD, part)
    cross_t = jnp.sum(halves.astype(F32) * (shares / total), 1).astype(BF16).reshape(width, part)
    cross_lse = (top + jnp.log(total)).reshape(all_heads, part)
    cross_branch = contract(cross_t, cross_out_all, 0, 1) + branch_bias[1]
    second_out, second_normed, second_inv = norm_forward(
        first_low.astype(F32) + cross_branch, gains[1], shifts[1]
    )
    second_low = second_out.astype(BF16)

    two = jnp.concatenate([second_low, tp_swap(second_low, 1)])
    pre_act = contract(two, up_all, 1, 0) + up_vector
    active = exact_gelu(pre_act).astype(BF16)
    mlp_part = contract(active, down_all, 1, 1)
    mlp_branch = (
        mlp_part[:part] + tp_swap(mlp_part[part:].astype(BF16), 1).astype(F32) + branch_bias[2]
    )
    third_out, third_normed, third_inv = norm_forward(
        second_low.astype(F32) + mlp_branch, gains[2], shifts[2]
    )
    hidden_out = third_out.astype(BF16)
    rms = jnp.stack([root_mean(attn_branch), root_mean(cross_branch), root_mean(mlp_branch)])

    out_grad = own_rows(out_cotangent).astype(F32)
    third_grad, gain_two, shift_two = norm_backward(out_grad, third_normed, third_inv, gains[2])
    mlp_bias_grad = jnp.sum(third_grad, 0)
    mlp_low = third_grad.astype(BF16)
    mlp_low = jnp.concatenate([mlp_low, tp_swap(mlp_low, 1)])
    active_grad = contract(mlp_low, down_all, 1, 0)
    pre_low = jax.vjp(exact_gelu, pre_act)[1](active_grad)[0].astype(BF16)
    mlp_grad = mlp_grads(two, pre_low, mlp_low, active)
    back_part = contract(pre_low, up_all, 1, 1)
    mlp_grad = lax.psum_scatter(mlp_grad, PLANE, scatter_dimension=0, tiled=True)
    back = back_part[:part] + tp_swap(back_part[part:].astype(BF16), 1).astype(F32)
    up_bias_grad = jnp.sum(pre_low.astype(F32), 0).reshape(2, hidden)
    second_grad, gain_one, shift_one = norm_backward(
        third_grad + back, second_normed, second_inv, gains[1]
    )
    cross_bias_sum = jnp.sum(second_grad, 0)
    second_grad_low = second_grad.astype(BF16)
    mix_grad = contract(cross_out_all, second_grad_low, 0, 1).astype(BF16)
    inner = jnp.sum(
        mix_grad.reshape(all_heads, HEAD, part).astype(F32)
        * cross_t.reshape(all_heads, HEAD, part).astype(F32),
        1,
    )
    def spread_rows(values):
        rows = []
        for _ in range(3):
            rows.append(lax.reduce_precision(values, 8, 7))
            values = values - rows[-1]
        return [row.astype(BF16) for row in rows]

    stats = jnp.stack([*spread_rows(cross_lse), *spread_rows(inner)], 1).reshape(ranks * cores, -1, part)
    stats = jnp.pad(stats, ((0, 0), (0, STAT_ROWS - stats.shape[1]), (0, 0)))
    mix_grad = to_pairs(jnp.concatenate([mix_grad.reshape(ranks * cores, pair_rows, part), stats], 1))
    mix_grad, hidden_out, proj = together(mix_grad, hidden_out, proj)
    hidden_out = whole_on_ranks(hidden_out)
    *pair_grads, query_grad = cross_backward(cross_query, mix_grad, pairs)
    query_grad, hidden_out = together(query_grad, hidden_out)
    pair_grads = [
        (ctx_swap(g, k) if k else g).reshape(-1, 2 * pair_rows) for k, g in enumerate(pair_grads)
    ]
    enc_part, value_sum, kv_grad = encoder_back(core_at, enc_rows, kv_weights, pair_grads)
    query_grad = from_pairs(query_grad)
    query_grad, enc_part, value_sum, kv_grad, mlp_grad = together(
        query_grad, enc_part, value_sum, kv_grad, mlp_grad
    )
    encoder_grad = lax.psum_scatter(
        enc_part.reshape(seqs, enc_len, width), "tp", scatter_dimension=2, tiled=True
    )
    value_sum = value_sum.reshape(heads_here, 2 * HEAD)[:, HEAD:]
    query_grad = jnp.sum(query_grad.astype(F32), 1).astype(BF16).reshape(width, part)
    query_sum = jnp.sum(query_grad.astype(F32), 1)

    first_grad, gain_zero, shift_zero = norm_backward(
        second_grad + contract(query_grad, cross_q_all, 0, 1), first_normed, first_inv, gains[0]
    )
    attn_bias_sum = jnp.sum(first_grad, 0)
    first_grad_low = first_grad.astype(BF16)
    squares = [(first_grad_low, mixed_t, 1), (first_low, query_grad, 1), (second_grad_low, cross_t, 1)]
    square_grad = sum_begin(squares)

    self_mix_grad = contract(self_out_all, first_grad_low, 0, 1).astype(BF16)
    self_mix_grad = exchange(self_mix_grad.reshape(all_heads, HEAD, part)).reshape(chunk_shape)
    kv_grad = sum_begin((), [kv_grad])
    square_grad, kv_grad = sum_near(square_grad, 4), sum_near(kv_grad, 2)
    self_mix_grad, square_grad, kv_grad = together(self_mix_grad, square_grad, kv_grad)
    kv_grad = sum_dp(kv_grad)
    stacked, head_grad, head_sum = self_backward(
        ctx_at, x_slots, self_query, self_pair, self_mixed, self_mix_grad, self_lse
    )
    mlp_grad = one_step(mlp_split_kernel, [(2, shard, hidden)] * 2, mlp_grad)
    stacked, head_grad, square_grad, kv_grad, mlp_grad, hidden_out = together(
        stacked, head_grad, square_grad, kv_grad, mlp_grad, hidden_out
    )
    hidden_out = one_step(copy_kernel, (rows, width), hidden_out.reshape(rows, width))
    square_grad, kv_grad = sum_far(square_grad), sum_x(kv_grad)
    stacked = exchange(stacked.reshape(all_heads, 3 * HEAD, part))
    mlp_grad = [mlp_grad[0], tp_swap(mlp_grad[1], 2)]
    head_grad, square_grad, kv_grad, mlp_grad, encoder_grad, hidden_out = together(
        head_grad, square_grad, kv_grad, mlp_grad, encoder_grad, hidden_out
    )
    if plane != 8:
        square_grad = [sum_end(square_grad).astype(BF16)[None]]
    square_grad = rank_split(rank_at, square_grad, 3, ranks)
    square_grad = [tp_swap(v, k) if k else v for k, v in enumerate(square_grad)]
    input_grad = input_grads(stacked, proj, first_grad)
    input_grad = lax.all_gather(input_grad, "tp", axis=0, tiled=True)

    head_grad = head_grad.reshape(3 * HEAD, plane, shard).swapaxes(0, 1)
    head_sum = head_sum.reshape(3, HEAD)
    head_sum = jnp.concatenate([head_sum[0], head_sum[2]]).reshape(plane, bias_part, 1)
    head_sum = jnp.pad(head_sum, ((0, 0), (0, 16 - bias_part), (0, 0)))
    def pieces(values):
        return values.reshape(-1, plane, values.shape[-1] // plane).swapaxes(0, 1).reshape(plane, -1)

    norm_sums = jnp.stack(
        [gain_zero, gain_one, gain_two, shift_zero, shift_one, shift_two]
        + [attn_bias_sum, cross_bias_sum, mlp_bias_grad]
    )
    up_cols = up_bias.shape[1]
    up_sums = pieces(up_bias_grad.reshape(-1, plane * up_cols))
    query_sums = pieces(jnp.pad(query_sum.reshape(all_heads, HEAD), ((0, 0), (0, HEAD))))
    value_sums = pieces(jnp.pad(value_sum, ((0, 0), (HEAD, 0))))
    sums = jnp.concatenate([pieces(norm_sums), up_sums, query_sums, value_sums], 1)
    sums = jnp.pad(sums, ((0, 0), (0, 16 * shard - sums.shape[1]))).reshape(plane, 16, shard)
    head_grad = jnp.concatenate(
        [head_grad, jnp.broadcast_to(head_sum, (plane, 16, shard)), sums], 1
    ).astype(BF16)
    head_grad = lax.all_to_all(head_grad, PLANE, split_axis=0, concat_axis=0, tiled=True)
    head_grad = head_grad.reshape(-1, blocks, 3 * HEAD + 32, shard).astype(F32)
    kv_grad = sum_end(kv_grad).reshape(shard, heads_here, 2, HEAD)
    kv_grad = kv_grad.transpose(2, 0, 1, 3).reshape(2, shard, local_width)
    sums = jnp.sum(head_grad[:, :, 3 * HEAD + 16 :], (0, 1))
    head_grad = jnp.sum(head_grad[:, :, : 3 * HEAD + 16], 0)
    self_proj_out = head_grad[:, : 3 * HEAD].reshape(blocks, 3, HEAD, shard)
    self_proj_out = self_proj_out.transpose(1, 3, 0, 2).reshape(3, shard, local_width)
    self_bias_out = head_grad[:, 3 * HEAD : 3 * HEAD + bias_part, 0]
    norm_out, sums = sums[:9].reshape(-1), sums[9:].reshape(-1)
    sums = jnp.concatenate([norm_out, sums[: 2 * up_bias.size + ranks * count + count], rms.reshape(-1)])
    ends = [0, norm_out.size]
    for size in (up_bias.size, up_bias.size, ranks * count, count, rms.size):
        ends.append(ends[-1] + size)
    sums = jnp.pad(sums, (0, 16 * 256 - sums.size)).reshape(16, 256).astype(BF16)

    mlp_grad = mlp_grad[0].astype(F32) + mlp_grad[1].astype(F32)
    up_out, down_out = mlp_grad[0], mlp_grad[1].T
    sums, input_grad, square_grad = together(whole_on_ranks(sums), input_grad, square_grad)
    square_grad = sum(v.astype(F32) for v in square_grad)
    self_out_out, cross_q_out, cross_out_out = square_grad[0].T, square_grad[1], square_grad[2].T
    input_grad, encoder_grad = input_grad.astype(F32), encoder_grad.astype(F32)
    sums = sums.astype(F32).reshape(ranks, -1)
    norm_out, up_own, up_other, query_sums, value_sums, rms = (
        sums[:, i:j] for i, j in zip(ends, ends[1:])
    )
    norm_out = jnp.sum(norm_out, 0).reshape(9, shard)

    def of_rank(values, at):
        return lax.dynamic_index_in_dim(values, at, 0, False)

    up_bias_out = (of_rank(up_own, own_tp) + of_rank(up_other, own_tp ^ 2)).reshape(up_bias.shape)
    cross_bias_out = of_rank(jnp.sum(query_sums, 0).reshape(ranks, count), own_tp)
    cross_bias_out = (cross_bias_out + of_rank(value_sums, own_tp)).reshape(heads_here, bias_part)
    rms = rms.reshape(ranks, 3, part).swapaxes(0, 1).reshape(3, rows)
    rms = jnp.concatenate([root_mean(hidden_in.reshape(rows, width).astype(F32))[None], rms])
    return (
        hidden_out.reshape(seqs, block, width),
        input_grad.reshape(seqs, block, width),
        encoder_grad,
        self_proj_out,
        self_bias_out,
        self_out_out,
        cross_q_out,
        kv_grad,
        cross_bias_out,
        cross_out_out,
        up_out,
        up_bias_out,
        down_out,
        norm_out[:3],
        norm_out[3:6],
        norm_out[6:],
        rms.reshape(4, seqs, block),
    )


def solution(mesh):
    rows, heads, columns = P("dp", "ctx", None), P("tp", PLANE), P(PLANE, "tp")
    stacked, vectors = P(None, PLANE, "tp"), P(None, PLANE)
    weights = (
        stacked, heads, heads, columns, stacked, heads, heads, columns, heads, heads,
        vectors, vectors, vectors,
    )
    return jax.shard_map(
        body,
        mesh=mesh,
        in_specs=(rows, rows, rows) + weights,
        out_specs=(rows, rows, P("dp", "ctx", "tp")) + weights + (P(None, "dp", "ctx"),),
        check_vma=False,
    )
```

```python
import functools

import jax
import jax.numpy as jnp
from jax import lax
from jax.experimental import pallas as pl
from jax.experimental.pallas import tpu as pltpu
from jax.sharding import PartitionSpec as P

EPSILON = 1e-05
HEAD = 64
KEY_TILE = 1024
STAT_ROWS = 16
ROW_TILE = 1024
COST_SHARE = 10
VMEM_BYTES = 50 * 1024 * 1024
PLANE = ("dp", "ctx")
HEADS = ("tp", "ctx")
F32 = jnp.float32
BF16 = jnp.bfloat16
IN_SMEM = pl.BlockSpec(memory_space=pltpu.SMEM)


def contract(left, right, left_dim, right_dim):
    return lax.dot_general(
        left, right, (((left_dim,), (right_dim,)), ((), ())), preferred_element_type=F32
    )


def together(*values):
    return lax.optimization_barrier(values)


def norm_forward(values, norm_gain, norm_shift):
    row_mean = jnp.mean(values, -1, keepdims=True)
    centered = values - row_mean
    inv_std = lax.rsqrt(jnp.mean(centered * centered, -1, keepdims=True) + EPSILON)
    normed = centered * inv_std
    return (normed * norm_gain + norm_shift, normed, inv_std)


def norm_backward(gradient, normed, inv_std, norm_gain):
    gain_grad = jnp.sum(gradient * normed, 0)
    shift_grad = jnp.sum(gradient, 0)
    scaled = gradient * norm_gain
    input_part = inv_std * (
        scaled
        - jnp.mean(scaled, -1, keepdims=True)
        - normed * jnp.mean(scaled * normed, -1, keepdims=True)
    )
    return (input_part, gain_grad, shift_grad)


def root_mean(values):
    return jnp.sqrt(jnp.mean(values * values, -1))


def exact_gelu(values):
    return jax.nn.gelu(values, approximate=False)


def with_zeros_below(values):
    return jnp.concatenate([values, jnp.zeros_like(values)], 0)


def with_zeros_above(values):
    return jnp.concatenate([jnp.zeros_like(values), values], 0)


def gather_chunks(ref):
    halves, blocks = ref.shape[:2]
    return jnp.concatenate([ref[h, b] for h in range(halves) for b in range(blocks)], 1)


def copy_kernel(in_ref, out_ref):
    out_ref[...] = in_ref[...]


def mlp_split_kernel(in_ref, *out_refs):
    width = out_refs[0].shape[2]
    for i, out_ref in enumerate(out_refs):
        for kind in range(2):
            at = (2 * kind + i) * width
            out_ref[kind] = in_ref[:, at : at + width]


def slot_at(own, k, size):
    return pl.ds(pl.multiple_of((own ^ k) * size, size), size)


def first_pack_kernel(proj_ref, small_ref, out_ref):
    blocks = proj_ref.shape[2] // HEAD
    for j in range(3):
        turned = proj_ref[j].T
        for e in range(out_ref.shape[0]):
            head = e % blocks * HEAD
            out_ref[e, j * HEAD : (j + 1) * HEAD] = turned[head : head + HEAD]
    for e in range(out_ref.shape[0]):
        out_ref[e, 3 * HEAD :] = small_ref[...]


def square_pack_kernel(self_out_ref, cross_q_ref, cross_out_ref, out_ref):
    out_ref[0] = self_out_ref[...].T
    out_ref[1] = cross_q_ref[...]
    out_ref[2] = cross_out_ref[...].T


def mlp_pack_kernel(up_ref, down_ref, out_ref):
    width = up_ref.shape[1]
    out_ref[:, :width] = up_ref[...]
    out_ref[:, width:] = down_ref[...].T


def rank_kernel(at_ref, *refs):
    part_refs, out_ref = refs[:-1], refs[-1]
    for k, part_ref in enumerate(part_refs):
        count, _, columns = part_ref.shape
        for i in range(count):
            first = (i * len(part_refs) + (at_ref[0] ^ k)) * columns
            out_ref[:, pl.ds(pl.multiple_of(first, columns), columns)] = part_ref[i]


def self_forward_kernel(at_ref, *refs):
    x_refs, (w_ref, bq_ref, bv_ref, q_ref, kv_ref, o_ref, lse_ref) = refs[:-7], refs[-7:]
    weights = w_ref[...]
    halves, blocks, _, part = o_ref.shape
    block = halves * part
    scale = HEAD**-0.5
    for k, x_ref in enumerate(x_refs):
        here = slot_at(at_ref[0], k, block)
        tokens = x_ref[0]
        q_ref[0, :, here] = (contract(weights[:HEAD], tokens, 1, 1) + bq_ref[...]).astype(BF16) * scale
        kv_ref[0, here] = (contract(tokens, weights[HEAD:], 1, 1) + bv_ref[...]).astype(BF16)
    for i in range(blocks):
        keys = kv_ref[0, : (i + 1) * block]
        query = q_ref[0, :, i * block : (i + 1) * block]
        scores = contract(keys, with_zeros_below(query), 1, 0)
        top = jnp.max(scores, 0, keepdims=True)
        weight = jnp.exp(scores - top)
        total = jnp.sum(weight, 0, keepdims=True)
        mixed = contract(keys, weight.astype(BF16), 0, 0)[HEAD:]
        out = (mixed / total).astype(BF16)
        for h in range(halves):
            o_ref[h, i] = out[:, h * part : (h + 1) * part]
        lse_ref[0, :, i * block : (i + 1) * block] = top + jnp.log(total)


def spread(values):
    rows = []
    for _ in range(3):
        rows.append(values.astype(BF16).astype(F32))
        values = values - rows[-1]
    return rows


def gathered(rows, at):
    return sum(rows[at + i : at + i + 1] for i in range(3))


def cross_forward_kernel(q_ref, *refs):
    kv_refs, o_ref = refs[:-1], refs[-1]
    halves, blocks, features, part = q_ref.shape
    queries = gather_chunks(q_ref)
    heads = features // HEAD
    outs, stats = [], []
    for n in range(heads):
        query = with_zeros_below(queries[n * HEAD : (n + 1) * HEAD])
        lanes = slice(n * 2 * HEAD, (n + 1) * 2 * HEAD)
        top = total = mixed = None
        for kv_ref in kv_refs:
            for start in range(0, kv_ref.shape[1], KEY_TILE):
                pair = kv_ref[0, start : start + KEY_TILE, lanes]
                scores = contract(pair, query, 1, 0)
                tile_top = jnp.max(scores, 0, keepdims=True)
                new_top = tile_top if top is None else jnp.maximum(top, tile_top)
                weight = jnp.exp(scores - new_top)
                tile_total = jnp.sum(weight, 0, keepdims=True)
                tile_mixed = contract(pair, weight.astype(BF16), 0, 0)
                if top is None:
                    total, mixed = tile_total, tile_mixed
                else:
                    fade = jnp.exp(top - new_top)
                    total = total * fade + tile_total
                    mixed = mixed * fade + tile_mixed
                top = new_top
        outs.append((mixed[HEAD:] / total).astype(BF16))
        stats += spread(top + jnp.log(total))
    spare = jnp.zeros((STAT_ROWS - len(stats), stats[0].shape[1]), F32)
    out = jnp.concatenate([*outs, jnp.concatenate([*stats, spare], 0).astype(BF16)], 0)
    for h in range(halves):
        for b in range(blocks):
            at = (h * blocks + b) * part
            o_ref[h, b] = out[:, at : at + part]


def cross_backward_kernel(q_ref, do_ref, *refs):
    count = (len(refs) - 1) // 2
    kv_refs, dkv_refs, dq_ref = refs[:count], refs[count:-1], refs[-1]
    halves, blocks, features, part = q_ref.shape
    width = halves * blocks * part
    queries, grads = gather_chunks(q_ref), gather_chunks(do_ref)
    heads = features // HEAD
    stats = grads[features:].astype(F32)
    outs = []
    for n in range(heads):
        query = with_zeros_below(queries[n * HEAD : (n + 1) * HEAD])
        grad = with_zeros_above(grads[n * HEAD : (n + 1) * HEAD])
        lse = gathered(stats, 6 * n)
        inner = gathered(stats, 6 * n + 3)
        lanes = slice(n * 2 * HEAD, (n + 1) * 2 * HEAD)
        both = jnp.concatenate([query, grad], 1)
        query_grad = None
        for kv_ref, dkv_ref in zip(kv_refs, dkv_refs):
            for start in range(0, kv_ref.shape[1], KEY_TILE):
                pair = kv_ref[0, start : start + KEY_TILE, lanes]
                products = contract(pair, both, 1, 0)
                weight = jnp.exp(products[:, :width] - lse)
                slope = (weight * (products[:, width:] - inner)).astype(BF16)
                dkv_ref[0, start : start + KEY_TILE, lanes] = (
                    contract(slope, query, 1, 1) + contract(weight.astype(BF16), grad, 1, 1)
                ).astype(BF16)
                part_grad = contract(pair, slope, 0, 0)
                query_grad = part_grad if query_grad is None else query_grad + part_grad
        outs.append((query_grad[:HEAD] * HEAD**-0.5).astype(BF16))
    out = jnp.concatenate(outs, 0)
    for h in range(halves):
        for b in range(blocks):
            at = (h * blocks + b) * part
            dq_ref[h, b] = out[:, at : at + part]


def self_backward_kernel(at_ref, *refs):
    x_refs, refs = refs[:-10], refs[-10:]
    q_ref, kv_ref, o_ref, do_ref, lse_ref, grad_ref, dw_ref, db_ref, dkv_ref, all_ref = refs
    halves, blocks, _, part = o_ref.shape
    block = halves * part
    dkv_ref[...] = jnp.zeros_like(dkv_ref)
    parts = []
    for i in range(blocks):
        lanes = slice(i * block, (i + 1) * block)
        reach = (i + 1) * block
        keys = kv_ref[0, :reach]
        query = with_zeros_below(q_ref[0, :, lanes])
        grad = jnp.concatenate([do_ref[h, i] for h in range(halves)], 1)
        mixed = jnp.concatenate([o_ref[h, i] for h in range(halves)], 1)
        inner = jnp.sum(grad.astype(F32) * mixed.astype(F32), 0, keepdims=True)
        grad = with_zeros_above(grad)
        weight = jnp.exp(contract(keys, query, 1, 0) - lse_ref[0, :, lanes])
        slope = (weight * (contract(keys, grad, 1, 0) - inner)).astype(BF16)
        parts.append(contract(keys, slope, 0, 0)[:HEAD] * HEAD**-0.5)
        dkv_ref[:, :reach] += contract(query, slope, 1, 1) + contract(
            grad, weight.astype(BF16), 1, 1
        )
    grads = jnp.concatenate(
        [jnp.concatenate(parts, 1).astype(BF16), dkv_ref[...].astype(BF16)], 0
    )
    all_ref[...] = grads
    for i in range(blocks):
        for h in range(halves):
            at = i * block + h * part
            grad_ref[h, i] = grads[:, at : at + part]

    @pl.when(pl.program_id(0) == 0)
    def _():
        dw_ref[...] = jnp.zeros_like(dw_ref)
        db_ref[...] = jnp.zeros_like(db_ref)

    dw_ref[...] += sum(
        contract(all_ref[:, slot_at(at_ref[0], k, block)], x_ref[0], 1, 0)
        for k, x_ref in enumerate(x_refs)
    )
    db_ref[...] += jnp.sum(grads.astype(F32), 1, keepdims=True)


def encoder_kernel(at_ref, e_ref, w_ref, b_ref, *refs):
    out_refs, all_ref = refs[:-1], refs[-1]
    all_ref[...] = (contract(e_ref[...], w_ref[...], 1, 0) + b_ref[...]).astype(BF16)
    for k, out_ref in enumerate(out_refs):
        out_ref[...] = all_ref[:, slot_at(at_ref[0], k, out_ref.shape[1])]


def encoder_back_kernel(at_ref, e_ref, w_ref, *refs):
    grad_refs, (part_ref, sum_ref, dw_ref, total_ref, all_ref) = refs[:-5], refs[-5:]
    for k, grad_ref in enumerate(grad_refs):
        all_ref[:, slot_at(at_ref[0], k, grad_ref.shape[1])] = grad_ref[...]
    grads = all_ref[...]
    part_ref[...] = contract(grads, w_ref[...], 1, 1).astype(BF16)

    @pl.when(pl.program_id(0) == 0)
    def _():
        total_ref[...] = jnp.zeros_like(total_ref)
        sum_ref[...] = jnp.zeros_like(sum_ref)

    total_ref[...] += contract(e_ref[...], grads, 0, 0)
    sum_ref[...] += jnp.sum(grads.astype(F32), 0, keepdims=True)

    @pl.when(pl.program_id(0) == pl.num_programs(0) - 1)
    def _():
        dw_ref[...] = total_ref[...].astype(BF16)


def plane_grad_kernel(sides, ready, at_ref, *refs):
    count = len(sides)
    lefts, rights, refs = refs[:count], refs[count : 2 * count], refs[2 * count :]
    ready_refs, out_refs = refs[:ready], refs[ready:]
    shard = out_refs[0].shape[1]
    for bit, out_ref in enumerate(out_refs):
        here = slot_at(at_ref[0], 2 * pl.program_id(0) + bit, shard)
        column = 0
        for left, right, side in zip(lefts, rights, sides):
            width = right.shape[1 - side]
            out_ref[0, :, column : column + width] = contract(
                left[:, here], right[...], 0, side
            ).astype(BF16)
            column += width
        for ready_ref in ready_refs:
            width = ready_ref.shape[1]
            out_ref[0, :, column : column + width] = ready_ref[here]
            column += width


def mlp_grad_kernel(two_ref, pre_ref, low_ref, active_ref, out_ref):
    width = pre_ref.shape[1]
    out_ref[:, :width] = contract(two_ref[...], pre_ref[...], 0, 0).astype(BF16)
    out_ref[:, width:] = contract(low_ref[...], active_ref[...], 0, 0).astype(BF16)


def halve_kernel(keep_ref, got_ref, *out_refs):
    size = out_refs[0].shape[0]
    for i, out_ref in enumerate(out_refs):
        for j in range(size):
            total = keep_ref[i * size + j].astype(F32) + got_ref[i * size + j].astype(F32)
            out_ref[j] = total.astype(BF16)


def rank_split_kernel(count, at_ref, *refs):
    part_refs, own_ref, send_refs = refs[:count], refs[count], refs[count + 1 :]
    kinds, _, columns = own_ref.shape
    for i in range(kinds):
        for k, out_ref in enumerate((own_ref, *send_refs)):
            first = (i * (len(send_refs) + 1) + (at_ref[0] ^ k)) * columns
            here = pl.ds(pl.multiple_of(first, columns), columns)
            total = sum(part_ref[0, :, here].astype(F32) for part_ref in part_refs)
            out_ref[i] = total.astype(out_ref.dtype)


def input_grad_kernel(stacked_ref, proj_ref, first_ref, out_ref, all_ref):
    @pl.when(pl.program_id(0) == 0)
    def _():
        heads = stacked_ref.shape[0]
        for j in range(3):
            rows = [stacked_ref[h, j * HEAD : (j + 1) * HEAD] for h in range(heads)]
            all_ref[:, j * heads * HEAD : (j + 1) * heads * HEAD] = jnp.concatenate(rows, 0).T

    out_ref[...] = (first_ref[...] + contract(all_ref[...], proj_ref[...], 1, 1)).astype(BF16)


def by_first(shape, lead=1):
    return pl.BlockSpec((lead,) + shape[1:], lambda s: (s,) + (0,) * (len(shape) - 1))


def whole(shape):
    return pl.BlockSpec(shape, lambda s: (0,) * len(shape))


def shaped(shape, dtype):
    return jax.ShapeDtypeStruct(shape, dtype)


def call(kernel, seqs, in_specs, out_specs, out_shape, operands, cost, scratch=()):
    flops, transcendentals = cost
    moved = sum(o.size * o.dtype.itemsize for o in operands)
    moved += sum(o.size * o.dtype.itemsize for o in out_shape)
    return pl.pallas_call(
        kernel,
        grid=(seqs,),
        in_specs=in_specs,
        out_specs=out_specs,
        out_shape=out_shape,
        scratch_shapes=scratch,
        compiler_params=pltpu.CompilerParams(
            dimension_semantics=("arbitrary",), vmem_limit_bytes=VMEM_BYTES
        ),
        cost_estimate=pl.CostEstimate(
            flops=flops // COST_SHARE,
            bytes_accessed=moved // COST_SHARE,
            transcendentals=transcendentals // COST_SHARE,
        ),
    )(*operands)


def one_step(kernel, out, *operands, flops=0):
    outs = out if isinstance(out, list) else [out]
    specs = [IN_SMEM if v.dtype == jnp.int32 else whole(v.shape) for v in operands]
    shapes = [shaped(v, BF16) for v in outs]
    results = call(kernel, 1, specs, [whole(v) for v in outs], shapes, operands, (flops, 0))
    return results if isinstance(out, list) else results[0]


def self_forward(at, slots, weights, query_bias, pair_bias, chunk_shape):
    seqs, block, width = slots[0].shape
    length = block * len(slots)
    halves = chunk_shape[0] // seqs
    query, pair, lse = (seqs, HEAD, length), (seqs, length, 2 * HEAD), (seqs, 1, length)
    return call(
        self_forward_kernel,
        seqs,
        [IN_SMEM]
        + [by_first(x.shape) for x in slots]
        + [whole(weights.shape), whole(query_bias.shape), whole(pair_bias.shape)],
        [by_first(query), by_first(pair), by_first(chunk_shape, halves), by_first(lse)],
        [shaped(query, BF16), shaped(pair, BF16), shaped(chunk_shape, BF16), shaped(lse, F32)],
        [at, *slots, weights, query_bias, pair_bias],
        (seqs * length * (2 * width * 3 * HEAD + 8 * length * HEAD), seqs * length * length),
    )


def cross_forward(query, pairs):
    seqs = pairs[0].shape[0]
    halves, blocks, features, part = query.shape
    halves //= seqs
    length = halves * blocks * part
    keys = sum(p.shape[1] for p in pairs)
    out = (halves * seqs, blocks, features + STAT_ROWS, part)
    return call(
        cross_forward_kernel,
        seqs,
        [by_first(query.shape, halves)] + [by_first(p.shape) for p in pairs],
        [by_first(out, halves)],
        [shaped(out, BF16)],
        [query, *pairs],
        (seqs * length * keys * 8 * features, seqs * length * keys * features // HEAD),
    )[0]


def cross_backward(query, grad, pairs):
    seqs = pairs[0].shape[0]
    halves, blocks, features, part = query.shape
    halves //= seqs
    length = halves * blocks * part
    keys = sum(p.shape[1] for p in pairs)
    return call(
        cross_backward_kernel,
        seqs,
        [by_first(query.shape, halves), by_first(grad.shape, halves)] + [by_first(p.shape) for p in pairs],
        [by_first(p.shape) for p in pairs] + [by_first(query.shape, halves)],
        [shaped(p.shape, BF16) for p in pairs] + [shaped(query.shape, BF16)],
        [query, grad, *pairs],
        (seqs * length * keys * 20 * features, seqs * length * keys * features // HEAD),
    )


def self_backward(at, slots, query, pair, mixed, grad, lse):
    seqs, block, width = slots[0].shape
    length = block * len(slots)
    halves = mixed.shape[0] // seqs
    chunk = by_first(mixed.shape, halves)
    out = mixed.shape[:2] + (3 * HEAD, mixed.shape[3])
    return call(
        self_backward_kernel,
        seqs,
        [IN_SMEM]
        + [by_first(x.shape) for x in slots]
        + [by_first(query.shape), by_first(pair.shape), chunk, chunk, by_first(lse.shape)],
        [by_first(out, halves), whole((3 * HEAD, width)), whole((3 * HEAD, 1))],
        [shaped(out, BF16), shaped((3 * HEAD, width), F32), shaped((3 * HEAD, 1), F32)],
        [at, *slots, query, pair, mixed, grad, lse],
        (seqs * length * (2 * width * 3 * HEAD + 20 * length * HEAD), seqs * length * length),
        [pltpu.VMEM((2 * HEAD, length), F32), pltpu.VMEM((3 * HEAD, length), BF16)],
    )


def encoder_pairs(at, rows, weights, bias, count):
    length, width = rows.shape
    tile = min(ROW_TILE, length)
    pair = (length, weights.shape[1] // count)
    return call(
        encoder_kernel,
        length // tile,
        [IN_SMEM, by_first(rows.shape, tile), whole(weights.shape), whole(bias.shape)],
        [by_first(pair, tile)] * count,
        [shaped(pair, BF16)] * count,
        [at, rows, weights, bias],
        (2 * length * width * weights.shape[1], 0),
        [pltpu.VMEM((tile, weights.shape[1]), BF16)],
    )


def encoder_back(at, rows, weights, grads):
    length, width = rows.shape
    tile = min(ROW_TILE, length)
    columns = weights.shape[1]
    return call(
        encoder_back_kernel,
        length // tile,
        [IN_SMEM, by_first(rows.shape, tile), whole(weights.shape)]
        + [by_first(g.shape, tile) for g in grads],
        [by_first(rows.shape, tile), whole((1, columns)), whole(weights.shape)],
        [shaped(rows.shape, BF16), shaped((1, columns), F32), shaped(weights.shape, BF16)],
        [at, rows, weights, *grads],
        (4 * length * width * columns, 0),
        [pltpu.VMEM(weights.shape, F32), pltpu.VMEM((tile, columns), BF16)],
    )


def mlp_grads(two, pre_low, low, active):
    count, width = two.shape
    columns = pre_low.shape[1]
    tile = 256
    strip = pl.BlockSpec((count, tile), lambda i: (0, i))
    out = (width, 2 * columns)
    return call(
        mlp_grad_kernel,
        width // tile,
        [strip, whole(pre_low.shape), strip, whole(active.shape)],
        [by_first(out, tile)],
        [shaped(out, BF16)],
        [two, pre_low, low, active],
        (4 * count * width * columns, 0),
    )[0]


def halve(keep, got, groups):
    count, rows, columns = keep.shape
    tile = min(512, columns)
    stack = pl.BlockSpec((count, rows, tile), lambda i: (0, 0, i))
    strip = pl.BlockSpec((count // groups, rows, tile), lambda i: (0, 0, i))
    return call(
        halve_kernel,
        columns // tile,
        [stack, stack],
        [strip] * groups,
        [shaped((count // groups, rows, columns), BF16)] * groups,
        [keep, got],
        (keep.size, 0),
    )


def rank_split(at, parts, kinds, ranks):
    _, rows, columns = parts[0].shape
    out = (kinds, rows, columns // kinds // ranks)
    return call(
        functools.partial(rank_split_kernel, len(parts)),
        1,
        [IN_SMEM] + [whole(v.shape) for v in parts],
        [whole(out)] * ranks,
        [shaped(out, F32)] + [shaped(out, BF16)] * (ranks - 1),
        [at, *parts],
        (len(parts) * parts[0].size, 0),
    )


def input_grads(stacked, proj, first):
    part, width = first.shape
    tile = 256
    strip = pl.BlockSpec((part, tile), lambda i: (0, i))
    return call(
        input_grad_kernel,
        width // tile,
        [whole(stacked.shape), by_first(proj.shape, tile), strip],
        [strip],
        [shaped(first.shape, BF16)],
        [stacked, proj, first],
        (2 * part * proj.size, 0),
        [pltpu.VMEM((part, proj.shape[1]), BF16)],
    )[0]


def plane_grads(at, items, ready, shard):
    lefts, rights, sides = zip(*items) if items else ((), (), ())
    width = (lefts[0].T if items else ready[0]).shape[0]
    columns = sum(right.shape[1 - side] for right, side in zip(rights, sides))
    columns += sum(v.shape[1] for v in ready)
    out = (width // shard // 2, shard, columns)
    flops = sum(2 * width * right.size for right in rights)
    return call(
        functools.partial(plane_grad_kernel, sides, len(ready)),
        out[0],
        [IN_SMEM] + [whole(v.shape) for v in (*lefts, *rights, *ready)],
        [by_first(out)] * 2,
        [shaped(out, BF16)] * 2,
        [at, *lefts, *rights, *ready],
        (flops, 0),
    )


def body(
    hidden_in,
    encoder_states,
    out_cotangent,
    self_proj,
    self_qv_bias,
    self_out_proj,
    cross_q_proj,
    cross_kv_proj,
    cross_qv_bias,
    cross_out_proj,
    up_proj,
    up_bias,
    down_proj,
    norm_gain,
    norm_bias,
    out_bias,
):
    blocks, ranks = lax.axis_size("ctx"), lax.axis_size("tp")
    plane = lax.axis_size("dp") * blocks
    own_ctx, own_tp = lax.axis_index("ctx"), lax.axis_index("tp")
    seqs, block, width = hidden_in.shape
    rows = seqs * block
    part = rows // ranks
    shard = width // plane
    heads_here = self_qv_bias.shape[0]
    local_width = heads_here * HEAD
    all_heads = heads_here * ranks
    enc_len = encoder_states.shape[1]
    hidden = up_proj.shape[1]
    slots = range(blocks)

    def ctx_swap(values, k):
        return lax.ppermute(values, "ctx", [(i, i ^ k) for i in slots])

    def tp_swap(values, k):
        return lax.ppermute(values, "tp", [(i, i ^ k) for i in range(ranks)])

    def exchange(values):
        return lax.all_to_all(values, HEADS, split_axis=0, concat_axis=0, tiled=True)

    def own_rows(values):
        return lax.dynamic_slice_in_dim(values.reshape(rows, width), own_tp * part, part, 0)

    def in_swap_order(values, axis):
        return [lax.dynamic_index_in_dim(values, own_ctx ^ k, axis, keepdims=False) for k in slots]

    cores = 2
    pair_heads = heads_here // cores
    pair_rows = pair_heads * HEAD
    core_at = lax.rem(own_ctx, cores).reshape(1)
    ctx_at, plane_at = own_ctx.reshape(1), (lax.axis_index("dp") * blocks + own_ctx).reshape(1)

    def plane_swap(values, k):
        return lax.ppermute(values, PLANE, [(i, i ^ k) for i in range(plane)])

    def sum_begin(items, ready=()):
        if plane == 8:
            keep, send = plane_grads(plane_at, items, ready, shard)
            return (keep, plane_swap(send, 1))
        sums = [contract(left, right, 0, side).astype(BF16) for left, right, side in items]
        sums = jnp.concatenate([*sums, *ready], 1)
        return (lax.psum_scatter(sums, PLANE, scatter_dimension=0, tiled=True),)

    def sum_near(state, groups):
        return halve(*state, groups) if plane == 8 else state

    def sum_far(parts):
        return [plane_swap(part, 2 * j) if j else part for j, part in enumerate(parts)]

    def sum_dp(parts):
        return [parts[0], plane_swap(parts[1], 4)] if plane == 8 else parts

    def sum_x(parts):
        if plane != 8:
            return parts
        own, other = (parts[0][j].astype(F32) + parts[1][j].astype(F32) for j in range(2))
        return [own, plane_swap(other.astype(BF16), 2)]

    def sum_end(parts):
        return sum(part.astype(F32).reshape(shard, -1) for part in parts)

    def whole_on_ranks(values):
        values = jnp.broadcast_to(values[None], (ranks,) + values.shape)
        return lax.all_to_all(values, "tp", split_axis=0, concat_axis=0, tiled=True)

    bias_part = 2 * HEAD // plane
    count = heads_here * bias_part
    core_tokens, x_tokens = ctx_swap(hidden_in, 1), ctx_swap(hidden_in, 2)
    rank_at = own_tp.reshape(1)

    def rank_parts(values):
        return [values] + [tp_swap(values, k) for k in range(1, ranks)]

    def from_ranks(parts):
        out = (shard, parts[0].shape[0] * width)
        return one_step(rank_kernel, out, rank_at, *parts)

    square = one_step(
        square_pack_kernel, (3, shard, local_width), self_out_proj, cross_q_proj, cross_out_proj
    )
    square = rank_parts(square)
    square, first_proj, core_tokens, x_tokens = together(square, self_proj, core_tokens, x_tokens)
    vectors = jnp.concatenate([norm_gain, norm_bias, out_bias])
    small = jnp.concatenate([v.reshape(-1) for v in (self_qv_bias, cross_qv_bias, up_bias)])
    small = jnp.concatenate([vectors, small.reshape(-1, shard)])
    small = jnp.pad(small, ((0, 16 - small.shape[0]), (0, 0)))
    first = one_step(
        first_pack_kernel, (plane, 3 * HEAD + small.shape[0], shard), first_proj, small
    )
    first = lax.all_to_all(first, PLANE, split_axis=0, concat_axis=0, tiled=True)
    kv_weights = cross_kv_proj.reshape(2, shard, heads_here, HEAD).transpose(1, 2, 0, 3)
    kv_weights = lax.all_gather(
        kv_weights.reshape(shard, heads_here * 2 * HEAD), PLANE, axis=0, tiled=True
    )

    core_tokens, x_tokens, first, up_proj, down_proj = together(
        core_tokens, x_tokens, first, up_proj, down_proj
    )

    square = lax.all_gather(from_ranks(square), PLANE, axis=0, tiled=True)
    mlp = one_step(mlp_pack_kernel, (shard, 2 * hidden), up_proj, down_proj)
    mlp_other = tp_swap(mlp, 2)
    x_slots = [hidden_in, core_tokens, x_tokens, ctx_swap(x_tokens, 1)]
    own_head = first[:, : 3 * HEAD].swapaxes(0, 1).reshape(3 * HEAD, width)
    small = first[:, 3 * HEAD :]
    vectors = small[:, :9].swapaxes(0, 1).reshape(9, width).astype(F32)
    gains, shifts, branch_bias = vectors[:3], vectors[3:6], vectors[6:]
    small = small[:, 9:].reshape(plane, -1)

    def head_bias(values):
        values = values.reshape(plane, heads_here, bias_part).swapaxes(0, 1)
        return values.reshape(heads_here, 2 * HEAD).astype(F32)

    self_bias = head_bias(small[:, :count])
    cross_bias = head_bias(small[:, count : 2 * count])
    up_vector = small[:, 2 * count : 2 * count + up_bias.size]
    up_vector = up_vector.reshape((plane,) + up_bias.shape).swapaxes(0, 1).reshape(1, hidden)
    enc_rows = encoder_states.reshape(-1, width)
    value_bias = jnp.concatenate([jnp.zeros((heads_here, HEAD), F32), cross_bias[:, HEAD:]], 1)
    pairs = encoder_pairs(core_at, enc_rows, kv_weights, value_bias.reshape(1, -1), cores)
    x_slots, pairs = together(x_slots, pairs)
    pairs = [
        (ctx_swap(pair, k) if k else pair).reshape(seqs, enc_len, 2 * pair_rows)
        for k, pair in enumerate(pairs)
    ]

    def to_pairs(values):
        values = values.reshape(ranks, 1, cores, -1, part)
        values = jnp.broadcast_to(values, (ranks, blocks // cores) + values.shape[2:])
        return exchange(values.reshape(all_heads, -1, part)).reshape(ranks, blocks, -1, part)

    def from_pairs(values):
        values = exchange(values.reshape(all_heads, -1, part))
        return values.reshape(ranks, blocks // cores, cores, -1, part)
    head_row = lax.dynamic_index_in_dim(self_bias, own_ctx, 0, keepdims=False)
    query_column = head_row[:HEAD].reshape(HEAD, 1)
    pair_row = jnp.concatenate([jnp.zeros((HEAD,), F32), head_row[HEAD:]]).reshape(1, 2 * HEAD)
    chunk_shape = (ranks, blocks, HEAD, part)
    self_query, self_pair, self_mixed, self_lse = self_forward(
        ctx_at, x_slots, own_head, query_column, pair_row, chunk_shape
    )
    tokens_f = own_rows(hidden_in).astype(F32)
    mixed_t = exchange(self_mixed.reshape(all_heads, HEAD, part)).reshape(width, part)
    mixed_t, square, mlp_other, self_proj, pairs, up_vector = together(
        mixed_t, square, mlp_other, self_proj, pairs, up_vector
    )
    up_vector = jnp.concatenate([up_vector, tp_swap(up_vector, 2)], 1).astype(F32)
    self_out_all, cross_q_all, cross_out_all = (square[:, i * width : (i + 1) * width] for i in range(3))
    mlp = jnp.concatenate(
        [mlp[:, :hidden], mlp_other[:, :hidden], mlp[:, hidden:], mlp_other[:, hidden:]], 1
    )
    mlp = lax.all_gather(mlp, PLANE, axis=0, tiled=True)
    up_all, down_all = mlp[:, : 2 * hidden], mlp[:, 2 * hidden :]
    rank_proj = rank_parts(self_proj)
    attn_branch = contract(mixed_t, self_out_all, 0, 1) + branch_bias[0]
    first_out, first_normed, first_inv = norm_forward(tokens_f + attn_branch, gains[0], shifts[0])
    first_low = first_out.astype(BF16)
    cross_query = contract(cross_q_all, first_low, 0, 1).astype(BF16)
    cross_query = to_pairs(cross_query)
    cross_rows = lax.dynamic_slice_in_dim(cross_bias[:, :HEAD], core_at[0] * pair_heads, pair_heads, 0)
    cross_query = (
        (cross_query.astype(F32) + cross_rows.reshape(pair_rows, 1)).astype(BF16) * HEAD**-0.5
    )
    cross_mixed = cross_forward(cross_query, pairs)
    cross_mixed, rank_proj = together(cross_mixed, rank_proj)
    proj = lax.all_gather(from_ranks(rank_proj), PLANE, axis=0, tiled=True)
    halves = from_pairs(cross_mixed)
    stats = halves[:, :, :, pair_rows : pair_rows + 3 * pair_heads].astype(F32)
    stats = jnp.sum(stats.reshape(ranks, blocks // cores, cores, pair_heads, 3, part), 4, keepdims=True)
    top = jnp.max(stats, 1, keepdims=True)
    shares = jnp.exp(stats - top)
    total = jnp.sum(shares, 1, keepdims=True)
    halves = halves[:, :, :, :pair_rows].reshape(ranks, blocks // cores, cores, pair_heads, HEAD, part)
    cross_t = jnp.sum(halves.astype(F32) * (shares / total), 1).astype(BF16).reshape(width, part)
    cross_lse = (top + jnp.log(total)).reshape(all_heads, part)
    cross_branch = contract(cross_t, cross_out_all, 0, 1) + branch_bias[1]
    second_out, second_normed, second_inv = norm_forward(
        first_low.astype(F32) + cross_branch, gains[1], shifts[1]
    )
    second_low = second_out.astype(BF16)

    two = jnp.concatenate([second_low, tp_swap(second_low, 1)])
    pre_act = contract(two, up_all, 1, 0) + up_vector
    active = exact_gelu(pre_act).astype(BF16)
    mlp_part = contract(active, down_all, 1, 1)
    mlp_branch = (
        mlp_part[:part] + tp_swap(mlp_part[part:].astype(BF16), 1).astype(F32) + branch_bias[2]
    )
    third_out, third_normed, third_inv = norm_forward(
        second_low.astype(F32) + mlp_branch, gains[2], shifts[2]
    )
    hidden_out = third_out.astype(BF16)
    rms = jnp.stack([root_mean(attn_branch), root_mean(cross_branch), root_mean(mlp_branch)])

    out_grad = own_rows(out_cotangent).astype(F32)
    third_grad, gain_two, shift_two = norm_backward(out_grad, third_normed, third_inv, gains[2])
    mlp_bias_grad = jnp.sum(third_grad, 0)
    mlp_low = third_grad.astype(BF16)
    mlp_low = jnp.concatenate([mlp_low, tp_swap(mlp_low, 1)])
    active_grad = contract(mlp_low, down_all, 1, 0)
    pre_low = jax.vjp(exact_gelu, pre_act)[1](active_grad)[0].astype(BF16)
    mlp_grad = mlp_grads(two, pre_low, mlp_low, active)
    back_part = contract(pre_low, up_all, 1, 1)
    mlp_grad = lax.psum_scatter(mlp_grad, PLANE, scatter_dimension=0, tiled=True)
    back = back_part[:part] + tp_swap(back_part[part:].astype(BF16), 1).astype(F32)
    up_bias_grad = jnp.sum(pre_low.astype(F32), 0).reshape(2, hidden)
    second_grad, gain_one, shift_one = norm_backward(
        third_grad + back, second_normed, second_inv, gains[1]
    )
    cross_bias_sum = jnp.sum(second_grad, 0)
    second_grad_low = second_grad.astype(BF16)
    mix_grad = contract(cross_out_all, second_grad_low, 0, 1).astype(BF16)
    inner = jnp.sum(
        mix_grad.reshape(all_heads, HEAD, part).astype(F32)
        * cross_t.reshape(all_heads, HEAD, part).astype(F32),
        1,
    )
    def spread_rows(values):
        rows = []
        for _ in range(3):
            rows.append(lax.reduce_precision(values, 8, 7))
            values = values - rows[-1]
        return [row.astype(BF16) for row in rows]

    stats = jnp.stack([*spread_rows(cross_lse), *spread_rows(inner)], 1).reshape(ranks * cores, -1, part)
    stats = jnp.pad(stats, ((0, 0), (0, STAT_ROWS - stats.shape[1]), (0, 0)))
    mix_grad = to_pairs(jnp.concatenate([mix_grad.reshape(ranks * cores, pair_rows, part), stats], 1))
    mix_grad, hidden_out, proj = together(mix_grad, hidden_out, proj)
    hidden_out = whole_on_ranks(hidden_out)
    *pair_grads, query_grad = cross_backward(cross_query, mix_grad, pairs)
    query_grad, hidden_out = together(query_grad, hidden_out)
    pair_grads = [
        (ctx_swap(g, k) if k else g).reshape(-1, 2 * pair_rows) for k, g in enumerate(pair_grads)
    ]
    enc_part, value_sum, kv_grad = encoder_back(core_at, enc_rows, kv_weights, pair_grads)
    query_grad = from_pairs(query_grad)
    query_grad, enc_part, value_sum, kv_grad, mlp_grad = together(
        query_grad, enc_part, value_sum, kv_grad, mlp_grad
    )
    encoder_grad = lax.psum_scatter(
        enc_part.reshape(seqs, enc_len, width), "tp", scatter_dimension=2, tiled=True
    )
    value_sum = value_sum.reshape(heads_here, 2 * HEAD)[:, HEAD:]
    query_grad = jnp.sum(query_grad.astype(F32), 1).astype(BF16).reshape(width, part)
    query_sum = jnp.sum(query_grad.astype(F32), 1)

    first_grad, gain_zero, shift_zero = norm_backward(
        second_grad + contract(query_grad, cross_q_all, 0, 1), first_normed, first_inv, gains[0]
    )
    attn_bias_sum = jnp.sum(first_grad, 0)
    first_grad_low = first_grad.astype(BF16)
    self_mix_grad = contract(self_out_all, first_grad_low, 0, 1).astype(BF16)
    self_mix_grad, first_grad_low = together(self_mix_grad, first_grad_low)
    squares = [(first_grad_low, mixed_t, 1), (first_low, query_grad, 1), (second_grad_low, cross_t, 1)]
    square_grad = sum_begin(squares)

    self_mix_grad = exchange(self_mix_grad.reshape(all_heads, HEAD, part)).reshape(chunk_shape)
    kv_grad = sum_begin((), [kv_grad])
    square_grad, kv_grad = sum_near(square_grad, 4), sum_near(kv_grad, 2)
    kv_grad = sum_dp(kv_grad)
    stacked, head_grad, head_sum = self_backward(
        ctx_at, x_slots, self_query, self_pair, self_mixed, self_mix_grad, self_lse
    )
    mlp_grad = one_step(mlp_split_kernel, [(2, shard, hidden)] * 2, mlp_grad)
    stacked, head_grad, square_grad, kv_grad, mlp_grad, hidden_out = together(
        stacked, head_grad, square_grad, kv_grad, mlp_grad, hidden_out
    )
    hidden_out = one_step(copy_kernel, (rows, width), hidden_out.reshape(rows, width))
    square_grad, kv_grad = sum_far(square_grad), sum_x(kv_grad)
    stacked = exchange(stacked.reshape(all_heads, 3 * HEAD, part))
    mlp_grad = [mlp_grad[0], tp_swap(mlp_grad[1], 2)]
    head_grad, square_grad, kv_grad, mlp_grad, encoder_grad, hidden_out = together(
        head_grad, square_grad, kv_grad, mlp_grad, encoder_grad, hidden_out
    )
    if plane != 8:
        square_grad = [sum_end(square_grad).astype(BF16)[None]]
    square_grad = rank_split(rank_at, square_grad, 3, ranks)
    square_grad = [tp_swap(v, k) if k else v for k, v in enumerate(square_grad)]
    input_grad = input_grads(stacked, proj, first_grad)
    input_grad = lax.all_gather(input_grad, "tp", axis=0, tiled=True)

    head_grad = head_grad.reshape(3 * HEAD, plane, shard).swapaxes(0, 1)
    head_sum = head_sum.reshape(3, HEAD)
    head_sum = jnp.concatenate([head_sum[0], head_sum[2]]).reshape(plane, bias_part, 1)
    head_sum = jnp.pad(head_sum, ((0, 0), (0, 16 - bias_part), (0, 0)))
    def pieces(values):
        return values.reshape(-1, plane, values.shape[-1] // plane).swapaxes(0, 1).reshape(plane, -1)

    norm_sums = jnp.stack(
        [gain_zero, gain_one, gain_two, shift_zero, shift_one, shift_two]
        + [attn_bias_sum, cross_bias_sum, mlp_bias_grad]
    )
    up_cols = up_bias.shape[1]
    up_sums = pieces(up_bias_grad.reshape(-1, plane * up_cols))
    query_sums = pieces(jnp.pad(query_sum.reshape(all_heads, HEAD), ((0, 0), (0, HEAD))))
    value_sums = pieces(jnp.pad(value_sum, ((0, 0), (HEAD, 0))))
    sums = jnp.concatenate([pieces(norm_sums), up_sums, query_sums, value_sums], 1)
    sums = jnp.pad(sums, ((0, 0), (0, 16 * shard - sums.shape[1]))).reshape(plane, 16, shard)
    head_grad = jnp.concatenate(
        [head_grad, jnp.broadcast_to(head_sum, (plane, 16, shard)), sums], 1
    ).astype(BF16)
    head_grad = lax.all_to_all(head_grad, PLANE, split_axis=0, concat_axis=0, tiled=True)
    head_grad = head_grad.reshape(-1, blocks, 3 * HEAD + 32, shard).astype(F32)
    kv_grad = sum_end(kv_grad).reshape(shard, heads_here, 2, HEAD)
    kv_grad = kv_grad.transpose(2, 0, 1, 3).reshape(2, shard, local_width)
    sums = jnp.sum(head_grad[:, :, 3 * HEAD + 16 :], (0, 1))
    head_grad = jnp.sum(head_grad[:, :, : 3 * HEAD + 16], 0)
    self_proj_out = head_grad[:, : 3 * HEAD].reshape(blocks, 3, HEAD, shard)
    self_proj_out = self_proj_out.transpose(1, 3, 0, 2).reshape(3, shard, local_width)
    self_bias_out = head_grad[:, 3 * HEAD : 3 * HEAD + bias_part, 0]
    norm_out, sums = sums[:9].reshape(-1), sums[9:].reshape(-1)
    sums = jnp.concatenate([norm_out, sums[: 2 * up_bias.size + ranks * count + count], rms.reshape(-1)])
    ends = [0, norm_out.size]
    for size in (up_bias.size, up_bias.size, ranks * count, count, rms.size):
        ends.append(ends[-1] + size)
    sums = jnp.pad(sums, (0, 16 * 256 - sums.size)).reshape(16, 256).astype(BF16)

    mlp_grad = mlp_grad[0].astype(F32) + mlp_grad[1].astype(F32)
    up_out, down_out = mlp_grad[0], mlp_grad[1].T
    sums, input_grad, square_grad = together(whole_on_ranks(sums), input_grad, square_grad)
    square_grad = sum(v.astype(F32) for v in square_grad)
    self_out_out, cross_q_out, cross_out_out = square_grad[0].T, square_grad[1], square_grad[2].T
    input_grad, encoder_grad = input_grad.astype(F32), encoder_grad.astype(F32)
    sums = sums.astype(F32).reshape(ranks, -1)
    norm_out, up_own, up_other, query_sums, value_sums, rms = (
        sums[:, i:j] for i, j in zip(ends, ends[1:])
    )
    norm_out = jnp.sum(norm_out, 0).reshape(9, shard)

    def of_rank(values, at):
        return lax.dynamic_index_in_dim(values, at, 0, False)

    up_bias_out = (of_rank(up_own, own_tp) + of_rank(up_other, own_tp ^ 2)).reshape(up_bias.shape)
    cross_bias_out = of_rank(jnp.sum(query_sums, 0).reshape(ranks, count), own_tp)
    cross_bias_out = (cross_bias_out + of_rank(value_sums, own_tp)).reshape(heads_here, bias_part)
    rms = rms.reshape(ranks, 3, part).swapaxes(0, 1).reshape(3, rows)
    rms = jnp.concatenate([root_mean(hidden_in.reshape(rows, width).astype(F32))[None], rms])
    return (
        hidden_out.reshape(seqs, block, width),
        input_grad.reshape(seqs, block, width),
        encoder_grad,
        self_proj_out,
        self_bias_out,
        self_out_out,
        cross_q_out,
        kv_grad,
        cross_bias_out,
        cross_out_out,
        up_out,
        up_bias_out,
        down_out,
        norm_out[:3],
        norm_out[3:6],
        norm_out[6:],
        rms.reshape(4, seqs, block),
    )


def solution(mesh):
    rows, heads, columns = P("dp", "ctx", None), P("tp", PLANE), P(PLANE, "tp")
    stacked, vectors = P(None, PLANE, "tp"), P(None, PLANE)
    weights = (
        stacked, heads, heads, columns, stacked, heads, heads, columns, heads, heads,
        vectors, vectors, vectors,
    )
    return jax.shard_map(
        body,
        mesh=mesh,
        in_specs=(rows, rows, rows) + weights,
        out_specs=(rows, rows, P("dp", "ctx", "tp")) + weights + (P(None, "dp", "ctx"),),
        check_vma=False,
    )
```
